32 devices in a mesh: batch: 4 (over z), blk: 8 (over y, x, core).
Axes of the slice: x: 2, y: 2, z: 4, core: 2. Of those that a mesh axis runs over, the one named last changes fastest.
Arguments:
- tokens: bfloat16 [4, 8192, 1024], P('batch', 'blk'), may hold values from -6 to 6
- out_cot: bfloat16 [4, 8192, 1024], P('batch', 'blk'), may hold values from -6 to 6
- norm_gain: float32 [1024], replicated, may hold values from 0.5 to 1.5
- in_weight: bfloat16 [1024, 4096], replicated, may hold values from -0.1875 to 0.1875
- conv_weight: float32 [4, 2048], replicated, may hold values from -3 to 3
- conv_bias: float32 [2048], replicated, may hold values from -0.5 to 0.5
- xproj_weight: bfloat16 [2048, 96], replicated, may hold values from -0.5 to 0.5
- dt_weight: bfloat16 [64, 2048], replicated, may hold values from -0.75 to 0.75
- dt_bias: float32 [2048], replicated, may hold values from -10 to -3
- a_log: float32 [16, 2048], replicated, may hold values from 0 to 1.4
- d_skip: float32 [2048], replicated, may hold values from 0.5 to 1.5
- out_weight: bfloat16 [2048, 1024], replicated, may hold values from -0.375 to 0.375
- moment_one: float32 [6667264], P(('batch', 'blk')), may hold values from -0.0006 to 0.0006
- moment_two: float32 [6667264], P(('batch', 'blk')), may hold values from 1e-09 to 1e-07
Outputs:
- result: bfloat16 [4, 8192, 1024], P('batch', 'blk')
- grad_tokens: bfloat16 [4, 8192, 1024], P('batch', 'blk')
- grads: float32 [6667264], P(('batch', 'blk'))
- grad_norm: float32 [], replicated
- param_step: float32 [6667264], P(('batch', 'blk'))
- new_one: float32 [6667264], P(('batch', 'blk'))
- new_two: float32 [6667264], P(('batch', 'blk'))
The draws below stay inside these ranges and needn't reach their ends.
All inputs are finite; a program needn't handle non-finite values.
Results may differ from the reference program's by a relative error of at most 0.012.
The reference program's roundings to bfloat16 on the way count: a program that leaves them out, or rounds other values in their place, can miss the bound.
Values sent between devices are 32-bit elements; how exact they have to be, the bound alone decides.
A program may use at most 704 MiB of HBM per device.

```python
import math
import jax
import jax.numpy as jnp
from jax import lax

D = 1024
DI = 2048
STATE = 16
CONV = 4
RANK = 64
ADAM_STEP = 100
CTX = 8192
CONTEXTS = 4
PARAMS = 6667264


def draw_dt_bias(key, part):
    key = jax.random.fold_in(key, 11)
    pick_key, slow_key, fast_key = jax.random.split(key, 3)
    share = 0.5
    chosen = jax.random.uniform(pick_key, (DI,), jnp.float32) < share
    slow = jnp.exp(jax.random.uniform(slow_key, (DI,), jnp.float32, math.log(0.0001), math.log(0.001)))
    fast = jnp.exp(jax.random.uniform(fast_key, (DI,), jnp.float32, math.log(0.003), math.log(0.03)))
    picked = jnp.where(chosen, slow, fast)
    return jnp.log(jnp.expm1(picked)).astype(jnp.float32)


def levels(rng, shape, shards, low, top_value):
    level, own = 1.0, jax.random.fold_in(rng, 6)
    for axis_at, parts in shards:
        draws = jnp.exp(jax.random.uniform(jax.random.fold_in(own, axis_at), (parts,), jnp.float32, low / len(shards), top_value / len(shards)))
        level = level * jnp.repeat(draws, shape[axis_at] // parts).reshape([-1 if axis == axis_at else 1 for axis in range(len(shape))])
    return level


def gaussian(key, dims, scale, bound, shards=(), kind=jnp.bfloat16):
    values = jax.random.normal(key, dims, jnp.float32) * scale
    if len(shards) > 0:
        values = levels(key, dims, shards, -0.22, 0.18) * values
    return jnp.clip(values, min=-bound, max=bound).astype(kind)


def setup_inputs(seed: int = 0) -> dict:
    key_list = jax.random.split(jax.random.key(seed), 15)
    return {
        "tokens": gaussian(key_list[0], (CONTEXTS, CTX, D), 1.0, 6.0, ((0, 4), (1, 8))),
        "out_cot": gaussian(key_list[1], (CONTEXTS, CTX, D), 1.0, 6.0, ((0, 4), (1, 8))),
        "norm_gain": jnp.clip(1.0 + 0.1 * jax.random.normal(key_list[2], (D,), jnp.float32), 0.5, 1.5),
        "in_weight": gaussian(key_list[3], (D, 2 * DI), D ** -0.5, 0.1875),
        "conv_weight": gaussian(key_list[4], (CONV, DI), CONV ** -0.5, 3.0, (), jnp.float32),
        "conv_bias": jnp.clip(jax.random.uniform(key_list[5], (DI,), jnp.float32, -0.5, 0.5), -0.5, 0.5),
        "xproj_weight": gaussian(key_list[6], (DI, RANK + 2 * STATE), (DI // 16) ** -0.5, 0.5),
        "dt_weight": gaussian(key_list[7], (RANK, DI), RANK ** -0.5, 0.75),
        "dt_bias": draw_dt_bias(jax.random.fold_in(key_list[14], 71), 0),
        "a_log": jnp.clip(jax.random.uniform(key_list[9], (STATE, DI), jnp.float32, 0.0, 1.4), 0.0, 1.4),
        "d_skip": jnp.clip(jax.random.uniform(key_list[10], (DI,), jnp.float32, 0.5, 1.5), 0.5, 1.5),
        "out_weight": gaussian(key_list[11], (DI, D), (DI // 8) ** -0.5, 0.375),
        "moment_one": gaussian(key_list[12], (PARAMS,), 0.0001, 0.0006, ((0, 32),), jnp.float32),
        "moment_two": jnp.clip(jnp.exp(math.log(1.0000000116860974e-07) - 4.6051702 * jax.random.uniform(key_list[13], (PARAMS,), jnp.float32) ** levels(key_list[13], (PARAMS,), ((0, 32),), -0.2, 0.2)), 9.999999717180685e-10, 1.0000000116860974e-07),
    }


EPS = 1e-05
RATE = 0.002
BETA_ONE = 0.9
BETA_TWO = 0.95
ADAM_EPS = 1e-08
DECAY = 0.1
CLIP = 1.0

@jax.custom_vjp
def low(v):
    return lax.optimization_barrier(v.astype(jnp.bfloat16)).astype(jnp.float32)

@jax.custom_vjp
def low_back(v):
    return v

def low_keep(v):
    return (low(v), None)

def low_pass(kept, grad):
    return (grad,)

def back_keep(v):
    return (v, None)

def back_low(kept, grad):
    return (low(grad),)
low.defvjp(low_keep, low_pass)
low_back.defvjp(back_keep, back_low)

def hi_dot(left, right):
    return jnp.dot(left, right, precision=lax.Precision.HIGHEST, preferred_element_type=jnp.float32)

def silu(value):
    return value * jax.nn.sigmoid(value)

def selective(step_size, conv_out, inject, readout, rates):
    rblock = 128
    count = step_size.shape[0] // rblock

    def advance(state, row):
        step_row, conv_row, inject_row, readout_row = row
        state = jnp.exp(step_row[None, :] * rates) * state + (step_row * conv_row)[None, :] * inject_row[:, None]
        return (state, lax.optimization_barrier(jnp.sum(readout_row[:, None] * state, axis=0)))

    def block_run(state, rows):
        return lax.scan(advance, state, rows)
    rows = tuple((value.reshape(count, rblock, value.shape[1]) for value in (step_size, conv_out, inject, readout)))
    start = jnp.zeros(rates.shape, jnp.float32)
    final, outputs = lax.scan(jax.checkpoint(block_run), start, rows)
    return outputs.reshape(step_size.shape)

def context(source, norm_gain, in_weight, conv_weight, conv_bias, xproj_weight, dt_weight, dt_bias, a_log, d_skip, out_weight):
    inner = conv_bias.shape[0]
    rank = dt_weight.shape[0]
    state = a_log.shape[0]
    width = conv_weight.shape[0]
    length = source.shape[0]
    meansq = lax.optimization_barrier(jnp.mean(source * source, axis=-1, keepdims=True))
    normed = low(source * lax.rsqrt(meansq + EPS) * norm_gain)
    projected = low_back(hi_dot(normed, in_weight))
    stream = projected[:, :inner]
    gating = projected[:, inner:]
    padded = jnp.concatenate([jnp.zeros((width - 1, inner), jnp.float32), stream], 0)
    conv_sum = conv_bias + jnp.zeros((length, inner), jnp.float32)
    for offset in range(width):
        conv_sum = conv_sum + conv_weight[offset] * padded[offset:offset + length]
    conv_out = low(silu(conv_sum))
    selectors = low_back(hi_dot(conv_out, xproj_weight))
    step_low = low(selectors[:, :rank])
    inject = selectors[:, rank:rank + state]
    readout = selectors[:, rank + state:]
    step_size = jax.nn.softplus(low_back(hi_dot(step_low, dt_weight)) + dt_bias)
    rates = -jnp.exp(a_log)
    scanned = selective(step_size, conv_out, inject, readout, rates) + d_skip * conv_out
    gated = low(scanned * silu(gating))
    return source + hi_dot(gated, out_weight)

def reference(tokens, out_cot, norm_gain, in_weight, conv_weight, conv_bias, xproj_weight, dt_weight, dt_bias, a_log, d_skip, out_weight, moment_one, moment_two):
    params = (norm_gain, in_weight.astype(jnp.float32), conv_weight, conv_bias, xproj_weight.astype(jnp.float32), dt_weight.astype(jnp.float32), dt_bias, a_log, d_skip, out_weight.astype(jnp.float32))
    source = tokens.astype(jnp.float32)

    def whole(inputs, *weights):

        def single(one):
            return context(one, *weights)
        return lax.map(jax.checkpoint(single), inputs)
    output, pullback = jax.vjp(whole, source, *params)
    cotangents = pullback(out_cot.astype(jnp.float32))
    grad_source = cotangents[0]
    grads = jnp.concatenate([value.reshape(-1) for value in cotangents[1:]])
    flat_params = jnp.concatenate([value.reshape(-1) for value in params])
    grad_norm = jnp.sqrt(jnp.sum(grads * grads))
    clipped = grads * jnp.minimum(1.0, CLIP / (grad_norm + 1e-06))
    new_one = BETA_ONE * moment_one + (1.0 - BETA_ONE) * clipped
    new_two = BETA_TWO * moment_two + (1.0 - BETA_TWO) * clipped * clipped
    first = new_one / (1.0 - BETA_ONE ** ADAM_STEP)
    second = new_two / (1.0 - BETA_TWO ** ADAM_STEP)
    pieces = []
    for number, value in enumerate(params):
        flag = 0.0 if number in (6, 7, 8) else 1.0
        pieces.append(jnp.full((value.size,), flag, jnp.float32))
    keep = jnp.concatenate(pieces)
    param_step = -RATE * (first / (jnp.sqrt(second) + ADAM_EPS) + DECAY * keep * flat_params)
    return (output.astype(jnp.bfloat16), grad_source.astype(jnp.bfloat16), grads, grad_norm, param_step, new_one, new_two)
```

```python
import functools
import math

import jax
import jax.numpy as jnp
from jax import lax
from jax.experimental import pallas as pl
from jax.experimental.pallas import tpu as pltpu
from jax.sharding import PartitionSpec as P

ADAM_STEP = 100
EPS = 1e-05
RATE = 0.002
BETA_ONE = 0.9
BETA_TWO = 0.95
ADAM_EPS = 1e-08
DECAY = 0.1
CLIP = 1.0

LOG2E = 1.0 / math.log(2.0)
LN2 = math.log(2.0)
SUB = 8
LANE = 128
ROW = 1024
VMEM_BYTES = 56 * 2**20

MESH = pl.DeviceIdType.MESH

f32 = jnp.float32
bf16 = jnp.bfloat16


def shifted(x, axis, by):
    count = lax.axis_size(axis)
    pairs = [(i, i + by) for i in range(count) if 0 <= i + by < count]
    return lax.ppermute(x, axis, pairs)


def silu_slope(value):
    sig = jax.nn.sigmoid(value)
    return sig * (1.0 + value * (1.0 - sig))


def interleave(x):
    rows, width = x.shape
    return x.reshape(SUB, rows // SUB, width).transpose(1, 0, 2).reshape(rows, width)


def restore(x):
    rows, width = x.shape
    return x.reshape(rows // SUB, SUB, width).transpose(1, 0, 2).reshape(rows, width)


def at(start, size):
    return pl.ds(pl.multiple_of(start, size), size)


def spread(sel_ref, base, state, tiles, out_ref):
    def one(i, carry):
        tile = sel_ref[at(i * SUB, SUB), :]
        for n in range(state):
            out_ref[at((i * state + n) * SUB, SUB), :] = jnp.broadcast_to(
                tile[:, base + n : base + n + 1], (SUB, LANE)
            )
        return carry

    lax.fori_loop(0, tiles, one, 0)


def gather_lanes(src_ref, state, tiles, out_ref):
    lane = lax.broadcasted_iota(jnp.int32, (SUB, LANE), 1)

    def one(i, carry):
        total = jnp.zeros((SUB, LANE), f32)
        for n in range(state):
            part = jnp.sum(src_ref[at((i * state + n) * SUB, SUB), :], axis=1, keepdims=True)
            total = jnp.where(lane == n, part, total)
        out_ref[at(i * SUB, SUB), :] = total
        return carry

    lax.fori_loop(0, tiles, one, 0)


def summary_kernel(
    shape,
    step_ref,
    drive_ref,
    grad_ref,
    sel_ref,
    rates_ref,
    pre_decay_ref,
    pre_state_ref,
    post_decay_ref,
    post_state_ref,
    totals_ref,
    end_ref,
    exit_ref,
    prod_ref,
    inject_ref,
    readout_ref,
):
    tiles, state, inner, rank, cols, group = shape
    turn = pl.program_id(0)

    @pl.when(turn == 0)
    def _():
        end_ref[...] = jnp.zeros_like(end_ref)
        exit_ref[...] = jnp.zeros_like(exit_ref)
        prod_ref[...] = jnp.ones_like(prod_ref)

    spread(sel_ref, rank, state, tiles, inject_ref)
    spread(sel_ref, rank + state, state, tiles, readout_ref)

    def columns(c, carry):
        lanes = [at((c * cols + k) * LANE, LANE) for k in range(cols)]
        for first in range(0, state, group):
            spots = [(n, k) for n in range(group) for k in range(cols)]
            where = [(slice((first + n) * SUB, (first + n + 1) * SUB), lanes[k]) for n, k in spots]
            rates = [rates_ref[w] for w in where]

            def advance(i, carry):
                ends, exits, prods = carry
                here = at(i * SUB, SUB)
                step = [step_ref[here, l] for l in lanes]
                drive = [drive_ref[here, l] for l in lanes]
                grad = [grad_ref[here, l] for l in lanes]
                inject = [inject_ref[at((i * state + first + n) * SUB, SUB), :] for n in range(group)]
                readout = [readout_ref[at((i * state + first + n) * SUB, SUB), :] for n in range(group)]
                new = ([], [], [])
                for s, (n, k) in enumerate(spots):
                    decay = jnp.exp2(step[k] * rates[s])
                    prod = prods[s] * decay
                    new[0].append(ends[s] * decay + drive[k] * inject[n])
                    new[1].append(exits[s] + prod * (grad[k] * readout[n]))
                    new[2].append(prod)
                return tuple(tuple(x) for x in new)

            start = tuple(tuple(ref[w] for w in where) for ref in (end_ref, exit_ref, prod_ref))
            ends, exits, prods = lax.fori_loop(0, tiles, advance, start, unroll=8)
            for s, w in enumerate(where):
                end_ref[w] = ends[s]
                exit_ref[w] = exits[s]
                prod_ref[w] = prods[s]
        return carry

    lax.fori_loop(0, inner // (LANE * cols), columns, 0)

    @pl.when(turn == pl.num_programs(0) - 1)
    def _():
        row = lax.broadcasted_iota(jnp.int32, (SUB, LANE), 0)

        def columns(c, carry):
            lanes = at(c * LANE, LANE)
            for n in range(state):
                here = (slice(n * SUB, (n + 1) * SUB), lanes)
                for way, src, decay_out, state_out, total_row in (
                    (1, end_ref, pre_decay_ref, pre_state_ref, 1),
                    (-1, exit_ref, post_decay_ref, post_state_ref, 2),
                ):
                    decay, value = prod_ref[here], src[here]

                    def seen(by):
                        return row >= by if way > 0 else row < SUB - by

                    for by in (1, 2, 4):
                        far_decay = pltpu.roll(decay, by if way > 0 else SUB - by, 0)
                        far_value = pltpu.roll(value, by if way > 0 else SUB - by, 0)
                        value = jnp.where(seen(by), value + decay * far_value, value)
                        decay = jnp.where(seen(by), decay * far_decay, decay)
                    last = SUB - 1 if way > 0 else 0
                    totals_ref[pl.ds(n, 1), lanes] = decay[last : last + 1]
                    totals_ref[pl.ds(total_row * state + n, 1), lanes] = value[last : last + 1]
                    turn_by = 1 if way > 0 else SUB - 1
                    decay_out[here] = jnp.where(seen(1), pltpu.roll(decay, turn_by, 0), 1.0)
                    state_out[here] = jnp.where(seen(1), pltpu.roll(value, turn_by, 0), 0.0)
            return carry

        lax.fori_loop(0, inner // LANE, columns, 0)


def forward_kernel(
    shape,
    step_ref,
    drive_ref,
    grad_ref,
    sel_ref,
    rates_ref,
    pre_decay_ref,
    pre_state_ref,
    entry_ref,
    scanned_ref,
    prior_ref,
    readout_grad_ref,
    state_ref,
    inject_ref,
    readout_ref,
    sums_ref,
):
    tiles, state, inner, rank, cols, group = shape

    @pl.when(pl.program_id(0) == 0)
    def _():
        for n in range(state):
            here = slice(n * SUB, (n + 1) * SUB)
            state_ref[here, :] = pre_state_ref[here, :] + pre_decay_ref[here, :] * entry_ref[n : n + 1, :]

    spread(sel_ref, rank, state, tiles, inject_ref)
    spread(sel_ref, rank + state, state, tiles, readout_ref)
    sums_ref[...] = jnp.zeros_like(sums_ref)

    def columns(c, carry):
        lanes = [at((c * cols + k) * LANE, LANE) for k in range(cols)]
        for first in range(0, state, group):
            spots = [(n, k) for n in range(group) for k in range(cols)]
            where = [(slice((first + n) * SUB, (first + n + 1) * SUB), lanes[k]) for n, k in spots]
            rates = [rates_ref[w] for w in where]

            def advance(i, states):
                here = at(i * SUB, SUB)
                step = [step_ref[here, l] for l in lanes]
                drive = [drive_ref[here, l] for l in lanes]
                grad = [grad_ref[here, l] for l in lanes]
                outs = [None] * cols
                new = []
                for n in range(group):
                    spot = at((i * state + first + n) * SUB, SUB)
                    inject = inject_ref[spot, :]
                    readout = readout_ref[spot, :]
                    total = None
                    for k in range(cols):
                        s = n * cols + k
                        decay = jnp.exp2(step[k] * rates[s])
                        fresh = decay * states[s] + drive[k] * inject
                        new.append(fresh)
                        part = readout * fresh
                        outs[k] = part if outs[k] is None else outs[k] + part
                        part = grad[k] * fresh
                        total = part if total is None else total + part
                    sums_ref[spot, :] += total
                    if n % 2 == 1:
                        pair = pl.ds(pl.multiple_of((i * state + first + n - 1) * SUB, 2 * SUB), 2 * SUB)
                        for k in range(cols):
                            prior_ref[pair, lanes[k]] = jnp.concatenate(
                                [states[(n - 1) * cols + k], states[n * cols + k]], 0
                            ).astype(bf16)
                for k in range(cols):
                    if first == 0:
                        scanned_ref[here, lanes[k]] = outs[k]
                    else:
                        scanned_ref[here, lanes[k]] += outs[k]
                return tuple(new)

            states = lax.fori_loop(0, tiles, advance, tuple(state_ref[w] for w in where), unroll=4)
            for s, w in enumerate(where):
                state_ref[w] = states[s]
        return carry

    lax.fori_loop(0, inner // (LANE * cols), columns, 0)
    gather_lanes(sums_ref, state, tiles, readout_grad_ref)


def backward_kernel(
    shape,
    step_ref,
    drive_ref,
    grad_ref,
    sel_ref,
    rates_ref,
    post_decay_ref,
    post_state_ref,
    arriving_ref,
    prior_ref,
    through_ref,
    feed_ref,
    inject_grad_ref,
    rate_grad_ref,
    carry_ref,
    inject_ref,
    readout_ref,
    sums_ref,
):
    tiles, state, inner, rank, cols, group = shape

    @pl.when(pl.program_id(0) == 0)
    def _():
        rate_grad_ref[...] = jnp.zeros_like(rate_grad_ref)
        for n in range(state):
            here = slice(n * SUB, (n + 1) * SUB)
            carry_ref[here, :] = post_state_ref[here, :] + post_decay_ref[here, :] * arriving_ref[n : n + 1, :]

    spread(sel_ref, rank, state, tiles, inject_ref)
    spread(sel_ref, rank + state, state, tiles, readout_ref)
    sums_ref[...] = jnp.zeros_like(sums_ref)

    def columns(c, carry):
        lanes = [at((c * cols + k) * LANE, LANE) for k in range(cols)]
        for first in range(0, state, group):
            spots = [(n, k) for n in range(group) for k in range(cols)]
            where = [(slice((first + n) * SUB, (first + n + 1) * SUB), lanes[k]) for n, k in spots]
            rates = [rates_ref[w] for w in where]

            def retreat(turn, carry):
                carries, rate_grads = carry
                i = tiles - 1 - turn
                here = at(i * SUB, SUB)
                step = [step_ref[here, l] for l in lanes]
                drive = [drive_ref[here, l] for l in lanes]
                grad = [grad_ref[here, l] for l in lanes]
                throughs = [None] * cols
                feeds = [None] * cols
                new = ([], [])
                for n in range(group):
                    spot = at((i * state + first + n) * SUB, SUB)
                    inject = inject_ref[spot, :]
                    readout = readout_ref[spot, :]
                    if n % 2 == 0:
                        pair = pl.ds(pl.multiple_of((i * state + first + n) * SUB, 2 * SUB), 2 * SUB)
                        pairs = [prior_ref[pair, lanes[k]].astype(f32) for k in range(cols)]
                    total = None
                    for k in range(cols):
                        s = n * cols + k
                        prior = pairs[k][(n % 2) * SUB : (n % 2 + 1) * SUB]
                        power = step[k] * rates[s]
                        adjoint = grad[k] * readout + carries[s]
                        back = jnp.exp2(power) * adjoint
                        through = back * prior * power
                        new[0].append(back)
                        new[1].append(rate_grads[s] + through)
                        throughs[k] = through if throughs[k] is None else throughs[k] + through
                        part = adjoint * inject
                        feeds[k] = part if feeds[k] is None else feeds[k] + part
                        part = adjoint * drive[k]
                        total = part if total is None else total + part
                    sums_ref[spot, :] += total
                for k in range(cols):
                    if first == 0:
                        through_ref[here, lanes[k]] = throughs[k]
                        feed_ref[here, lanes[k]] = feeds[k]
                    else:
                        through_ref[here, lanes[k]] += throughs[k]
                        feed_ref[here, lanes[k]] += feeds[k]
                return tuple(tuple(x) for x in new)

            start = tuple(tuple(ref[w] for w in where) for ref in (carry_ref, rate_grad_ref))
            carries, rate_grads = lax.fori_loop(0, tiles, retreat, start, unroll=4)
            for s, w in enumerate(where):
                carry_ref[w] = carries[s]
                rate_grad_ref[w] = rate_grads[s]
        return carry

    lax.fori_loop(0, inner // (LANE * cols), columns, 0)
    gather_lanes(sums_ref, state, tiles, inject_grad_ref)


def scan_shapes(rows, state, inner):
    tiles = min(16, rows // SUB)
    count = rows // (SUB * tiles)
    return tiles, count


def summary_call(step, drive, grad, sel, rates, rank):
    rows, inner = step.shape
    state = rates.shape[0] // SUB
    tiles, count = scan_shapes(rows, state, inner)
    wide = pl.BlockSpec((tiles * SUB, inner), lambda t: (t, 0))
    thin = pl.BlockSpec((tiles * SUB, sel.shape[1]), lambda t: (t, 0))
    whole = pl.BlockSpec((state * SUB, inner), lambda t: (0, 0))
    total = pl.BlockSpec((3 * state, inner), lambda t: (0, 0))
    shape = (tiles, state, inner, rank, 2, 4)
    big = jax.ShapeDtypeStruct((state * SUB, inner), f32)
    return pl.pallas_call(
        functools.partial(summary_kernel, shape),
        name="scan_summary",
        grid=(count,),
        in_specs=[wide, wide, wide, thin, whole],
        out_specs=[whole] * 4 + [total],
        out_shape=[big] * 4 + [jax.ShapeDtypeStruct((3 * state, inner), f32)],
        scratch_shapes=[pltpu.VMEM((state * SUB, inner), f32)] * 3
        + [pltpu.VMEM((tiles * state * SUB, LANE), f32)] * 2,
        compiler_params=pltpu.CompilerParams(vmem_limit_bytes=VMEM_BYTES),
    )(step, drive, grad, sel, rates)


def forward_call(step, drive, grad, sel, rates, pre_decay, pre_state, entry, rank):
    rows, inner = step.shape
    state = rates.shape[0] // SUB
    tiles, count = scan_shapes(rows, state, inner)
    wide = pl.BlockSpec((tiles * SUB, inner), lambda t: (t, 0))
    thin = pl.BlockSpec((tiles * SUB, sel.shape[1]), lambda t: (t, 0))
    whole = pl.BlockSpec((state * SUB, inner), lambda t: (0, 0), pipeline_mode=pl.Buffered(1))
    short = pl.BlockSpec((state, inner), lambda t: (0, 0))
    shape = (tiles, state, inner, rank, 2, 8)
    return pl.pallas_call(
        functools.partial(forward_kernel, shape),
        name="scan_forward",
        grid=(count,),
        in_specs=[wide, wide, wide, thin, whole, whole, whole, short],
        out_specs=[
            wide,
            pl.BlockSpec((tiles * state * SUB, inner), lambda t: (t, 0)),
            pl.BlockSpec((tiles * SUB, LANE), lambda t: (t, 0)),
        ],
        out_shape=[
            jax.ShapeDtypeStruct((rows, inner), f32),
            jax.ShapeDtypeStruct((rows * state, inner), bf16),
            jax.ShapeDtypeStruct((rows, LANE), f32),
        ],
        scratch_shapes=[pltpu.VMEM((state * SUB, inner), f32)]
        + [pltpu.VMEM((tiles * state * SUB, LANE), f32)] * 3,
        compiler_params=pltpu.CompilerParams(vmem_limit_bytes=VMEM_BYTES),
    )(step, drive, grad, sel, rates, pre_decay, pre_state, entry)


def backward_call(step, drive, grad, sel, rates, post_decay, post_state, arriving, prior, rank):
    rows, inner = step.shape
    state = rates.shape[0] // SUB
    tiles, count = scan_shapes(rows, state, inner)

    def back(t):
        return (count - 1 - t, 0)

    wide = pl.BlockSpec((tiles * SUB, inner), back)
    thin = pl.BlockSpec((tiles * SUB, sel.shape[1]), back)
    whole = pl.BlockSpec((state * SUB, inner), lambda t: (0, 0), pipeline_mode=pl.Buffered(1))
    short = pl.BlockSpec((state, inner), lambda t: (0, 0))
    shape = (tiles, state, inner, rank, 2, 4)
    return pl.pallas_call(
        functools.partial(backward_kernel, shape),
        name="scan_backward",
        grid=(count,),
        in_specs=[wide, wide, wide, thin, whole, whole, whole, short]
        + [pl.BlockSpec((tiles * state * SUB, inner), back)],
        out_specs=[
            wide,
            wide,
            pl.BlockSpec((tiles * SUB, LANE), back),
            pl.BlockSpec((state * SUB, inner), lambda t: (0, 0)),
        ],
        out_shape=[
            jax.ShapeDtypeStruct((rows, inner), f32),
            jax.ShapeDtypeStruct((rows, inner), f32),
            jax.ShapeDtypeStruct((rows, LANE), f32),
            jax.ShapeDtypeStruct((state * SUB, inner), f32),
        ],
        scratch_shapes=[pltpu.VMEM((state * SUB, inner), f32)]
        + [pltpu.VMEM((tiles * state * SUB, LANE), f32)] * 3,
        compiler_params=pltpu.CompilerParams(vmem_limit_bytes=VMEM_BYTES),
    )(step, drive, grad, sel, rates, post_decay, post_state, arriving, prior)


def flatten_kernel(rows_in, rows_out, in_base, small_base, out_base, stream_ref, gate_ref, out_w_ref, gain_ref, small_ref, flat_ref, in_buf, out_buf, sems):
    turn = pl.program_id(0)
    count = pl.num_programs(0)
    slot = turn % 2
    half = stream_ref.shape[1] // LANE
    wide = 2 * half

    def copies(step, slot):
        size_in, size_out = rows_in * wide // SUB, rows_out
        return (
            pltpu.make_async_copy(
                in_buf.at[slot], flat_ref.at[pl.ds(in_base + step * size_in, size_in)], sems.at[slot]
            ),
            pltpu.make_async_copy(
                out_buf.at[slot], flat_ref.at[pl.ds(out_base + step * size_out, size_out)], sems.at[2 + slot]
            ),
        )

    def extras():
        return (
            pltpu.make_async_copy(gain_ref, flat_ref.at[pl.ds(0, gain_ref.shape[0])], sems.at[4]),
            pltpu.make_async_copy(
                small_ref, flat_ref.at[pl.ds(small_base, small_ref.shape[0])], sems.at[5]
            ),
        )

    @pl.when(turn == 0)
    def _():
        for copy in extras():
            copy.start()

    @pl.when(turn >= 2)
    def _():
        for copy in copies(turn - 2, slot):
            copy.wait()

    for r in range(rows_in // SUB):
        rows = slice(r * SUB, (r + 1) * SUB)
        for a in range(wide):
            src = stream_ref if a < half else gate_ref
            tile = src[rows, (a % half) * LANE : (a % half + 1) * LANE]
            for_tile = in_buf.at[slot, r * wide : (r + 1) * wide]
            for_tile[pl.ds(a // SUB, SUB, stride=wide // SUB), a % SUB, :] = tile
    deep = out_w_ref.shape[1] // LANE
    for r in range(rows_out // SUB):
        rows = slice(r * SUB, (r + 1) * SUB)
        for a in range(deep):
            out_buf[slot, rows, a, :] = out_w_ref[rows, a * LANE : (a + 1) * LANE]
    for copy in copies(turn, slot):
        copy.start()

    @pl.when(turn == count - 1)
    def _():
        for copy in copies(turn - 1, 1 - slot):
            copy.wait()
        for copy in copies(turn, slot):
            copy.wait()
        for copy in extras():
            copy.wait()


def flatten_call(stream, gate, out_w, gain, small, total):
    depth, half = stream.shape
    steps = 16
    rows_in, rows_out = depth // steps, out_w.shape[0] // steps
    wide = 2 * half // LANE
    in_base = gain.shape[0]
    small_base = in_base + depth * wide // SUB
    out_base = small_base + small.shape[0]
    return pl.pallas_call(
        functools.partial(flatten_kernel, rows_in, rows_out, in_base, small_base, out_base),
        name="flatten",
        grid=(steps,),
        in_specs=[
            pl.BlockSpec((rows_in, half), lambda t: (t, 0)),
            pl.BlockSpec((rows_in, half), lambda t: (t, 0)),
            pl.BlockSpec((rows_out, out_w.shape[1]), lambda t: (t, 0)),
            pl.BlockSpec(memory_space=pl.ANY),
            pl.BlockSpec(memory_space=pl.ANY),
        ],
        out_specs=pl.BlockSpec(memory_space=pl.ANY),
        out_shape=jax.ShapeDtypeStruct((total, SUB, LANE), f32),
        scratch_shapes=[
            pltpu.VMEM((2, rows_in * wide // SUB, SUB, LANE), f32),
            pltpu.VMEM((2, rows_out, SUB, LANE), f32),
            pltpu.SemaphoreType.DMA((6,)),
        ],
        compiler_params=pltpu.CompilerParams(vmem_limit_bytes=VMEM_BYTES),
    )(stream, gate, out_w, gain, small)


def reduce_kernel(
    depth,
    bits,
    phases,
    half,
    span,
    flat_ref,
    out_ref,
    norm_ref,
    acc,
    first_recv,
    *rest,
):
    n = bits - 1
    bit_recvs = rest[:n]
    down_recv, up_recv, ring, sums, square_ref = rest[n : n + 5]
    local_sem, core_send, core_recv, bit_send, bit_recv, z_send, z_recv, ring_send, ring_recv = rest[n + 5 :]
    blk = lax.axis_index("blk")
    z = lax.axis_index("batch")
    mine = [(blk // 2**b) % 2 for b in range(bits)]
    partner = [blk + (1 - 2 * mine[b]) * 2**b for b in range(bits)]
    below, above = (z + depth - 1) % depth, (z + 1) % depth
    barrier = pltpu.get_barrier_semaphore()
    for b in range(bits):
        pl.semaphore_signal(barrier, inc=1, device_id={"blk": partner[b]}, device_id_type=MESH)
    for other in (below, above):
        pl.semaphore_signal(barrier, inc=1, device_id={"batch": other}, device_id_type=MESH)
    pl.semaphore_wait(barrier, bits + 2)

    def digits(r):
        return tuple((r // 2**i) % 2 for i in reversed(range(n)))

    def window(r, core, zz, p):
        owner = zz * 2**bits + 2 * r + core
        return pl.ds((owner * span) // ROW + p * 2 * half, 2 * half)

    def core_copies(p, own_too=True):
        remote, own = [], []
        for r in range(2**n):
            for zz in range(depth):
                at_slot = (p,) + digits(r) + (zz,)
                spot = (p * 2**n + r) * depth + zz
                remote.append(
                    pltpu.make_async_remote_copy(
                        src_ref=flat_ref.at[window(r, 1 - mine[0], zz, p)],
                        dst_ref=first_recv.at[at_slot],
                        send_sem=core_send.at[spot],
                        recv_sem=core_recv.at[spot],
                        device_id={"blk": partner[0]},
                        device_id_type=MESH,
                    )
                )
                if own_too:
                    own.append(
                        pltpu.make_async_copy(
                            flat_ref.at[window(r, mine[0], zz, p)], acc.at[at_slot], local_sem.at[spot]
                        )
                    )
        return remote, own

    def order(part):
        return list(range(n)) if part == 0 else list(reversed(range(n)))

    def place(p, part, done, pick):
        spots = [slice(None)] * n
        for i in order(part)[:done]:
            spots[i] = mine[i + 1]
        if pick is not None:
            spots[order(part)[done]] = pick
        return (p,) + tuple(reversed(spots)) + (slice(None), slice(part * half, (part + 1) * half))

    def bit_copies(p, s):
        copies = []
        for part in range(2):
            i = order(part)[s]
            spot = (p * n + s) * 2 + part
            copies.append(
                pltpu.make_async_remote_copy(
                    src_ref=acc.at[place(p, part, s, 1 - mine[i + 1])],
                    dst_ref=bit_recvs[s].at[p, part],
                    send_sem=bit_send.at[spot],
                    recv_sem=bit_recv.at[spot],
                    device_id={"blk": partner[i + 1]},
                    device_id_type=MESH,
                )
            )
        return copies

    settled = tuple(reversed([mine[i + 1] for i in range(n)]))

    def z_moves(p, u):
        down = u - (depth - 1 - z)
        up = depth - 1 - (u - z)
        spot = (p * (depth - 1) + u) * 2
        return (
            (
                (down >= 0) & (down < z),
                lax.max(down, 0),
                z < depth - 1,
                down_recv,
                below,
                spot,
            ),
            (
                (u >= z) & (up > z),
                lax.min(up, depth - 1),
                z > 0,
                up_recv,
                above,
                spot + 1,
            ),
        )

    def z_copy(p, goal, recv, to, spot):
        return pltpu.make_async_remote_copy(
            src_ref=acc.at[(p,) + settled + (goal,)],
            dst_ref=recv.at[p, goal],
            send_sem=z_send.at[spot],
            recv_sem=z_recv.at[0 if recv is down_recv else 1, p, goal],
            device_id={"batch": to},
            device_id_type=MESH,
        )

    def z_wait(p, goal, recv):
        z_copy(p, goal, recv, below if recv is down_recv else above, 0).wait_recv()

    def add_windows(p):
        remote, own = core_copies(p)
        for copy in own:
            copy.wait()
        for copy in remote:
            copy.wait_recv()
        for r in range(2**n):

            def one(zz, carry):
                at_slot = (p,) + digits(r) + (zz,)
                acc[at_slot] += first_recv[at_slot]
                return carry

            lax.fori_loop(0, depth, one, 0)

    def add_bits(p, s):
        for part, copy in enumerate(bit_copies(p, s)):
            copy.wait_recv()
            kept = place(p, part, s, mine[order(part)[s] + 1])
            free = [i for i, v in enumerate(kept[1 : 1 + n]) if isinstance(v, slice)]
            for r in range(2 ** len(free)):
                chosen = [(r // 2**j) % 2 for j in reversed(range(len(free)))]
                to = list(kept)
                for i, v in zip(free, chosen):
                    to[1 + i] = v

                def one(zz, carry):
                    dst = tuple(to[: 1 + n]) + (zz, to[-1])
                    acc[dst] += bit_recvs[s][(p, part) + tuple(chosen) + (zz,)]
                    return carry

                lax.fori_loop(0, depth, one, 0)

    last = n + depth - 1
    for t in range(phases + last + 1):
        for stage in reversed(range(last + 1)):
            p = t - stage
            if not 0 <= p < phases:
                continue
            if stage == 0:
                remote, own = core_copies(p)
                for copy in remote + own:
                    copy.start()
            elif stage <= n:
                if stage == 1:
                    add_windows(p)
                else:
                    add_bits(p, stage - 2)
                for copy in bit_copies(p, stage - 1):
                    copy.start()
            else:
                u = stage - n - 1
                if u == 0:
                    if n == 0:
                        add_windows(p)
                    else:
                        add_bits(p, n - 1)
                for cond, goal, relays, recv, to, spot in z_moves(p, u):

                    @pl.when(cond)
                    def _():
                        @pl.when(relays)
                        def _():
                            z_wait(p, goal, recv)
                            acc[(p,) + settled + (goal,)] += recv[p, goal]

                        z_copy(p, goal, recv, to, spot).start()

    square_ref[...] = jnp.zeros_like(square_ref)
    index = blk + z * 2**bits
    low = (index * span) % ROW
    inside = lax.broadcasted_iota(jnp.int32, (SUB, LANE), 0) * LANE + lax.broadcasted_iota(
        jnp.int32, (SUB, LANE), 1
    )
    for p in range(phases):
        for recv, here in ((down_recv, z < depth - 1), (up_recv, z > 0)):

            @pl.when(here)
            def _():
                z_wait(p, z, recv)
                acc[(p,) + settled + (z,)] += recv[p, z]

        def one(i, carry):
            value = acc[(p,) + settled + (z, i)]
            out_ref[p * 2 * half + i] = value
            spot = inside + (p * 2 * half + i) * ROW
            held = jnp.where((spot >= low) & (spot < low + span), value, 0.0)
            square_ref[...] += held * held
            return carry

        lax.fori_loop(0, 2 * half, one, 0)

    sums[0] = square_ref[...]
    for b in range(bits):
        copy = pltpu.make_async_remote_copy(
            src_ref=sums.at[b],
            dst_ref=sums.at[bits + 1 + b],
            send_sem=ring_send.at[b],
            recv_sem=ring_recv.at[b],
            device_id={"blk": partner[b]},
            device_id_type=MESH,
        )
        copy.start()
        copy.wait()
        sums[b + 1] = sums[b] + sums[bits + 1 + b]
    ring[z] = sums[bits]
    for u in range(depth - 1):
        moves = (
            ((z + u < depth) & (z > 0), lax.min(z + u, depth - 1), below, 0, (z < depth - 1) & (z + 1 + u < depth), lax.min(z + 1 + u, depth - 1)),
            ((z - u >= 0) & (z < depth - 1), lax.max(z - u, 0), above, 1, (z > 0) & (z - 1 - u >= 0), lax.max(z - 1 - u, 0)),
        )

        def hop(origin, to, way):
            return pltpu.make_async_remote_copy(
                src_ref=ring.at[origin],
                dst_ref=ring.at[origin],
                send_sem=ring_send.at[bits + u * 2 + way],
                recv_sem=ring_recv.at[bits + u * 2 + way],
                device_id={"batch": to},
                device_id_type=MESH,
            )

        for cond, origin, to, way, gets, source in moves:

            @pl.when(cond)
            def _():
                hop(origin, to, way).start()

        for cond, origin, to, way, gets, source in moves:

            @pl.when(gets)
            def _():
                hop(source, to, way).wait_recv()

            @pl.when(cond)
            def _():
                hop(origin, to, way).wait_send()

    total = ring[0]
    for zz in range(1, depth):
        total = total + ring[zz]
    norm_ref[...] = jnp.broadcast_to(jnp.sqrt(jnp.sum(total, keepdims=True)), (SUB, LANE))

    for p in range(phases):
        for copy in core_copies(p, False)[0]:
            copy.wait_send()
        for s in range(n):
            for copy in bit_copies(p, s):
                copy.wait_send()
        for u in range(depth - 1):
            for cond, goal, relays, recv, to, spot in z_moves(p, u):

                @pl.when(cond)
                def _():
                    z_copy(p, goal, recv, to, spot).wait_send()


def window_tiles(span, phases):
    need = (span - 1) // ROW + 2
    return -(-need // (2 * phases)) * 2 * phases


def reduce_call(flat, span, phases):
    depth, count = lax.axis_size("batch"), lax.axis_size("blk")
    bits = count.bit_length() - 1
    n = bits - 1
    half = window_tiles(span, phases) // (2 * phases)
    tile = (SUB, LANE)
    dma = pltpu.SemaphoreType.DMA
    spots = phases * 2**n * depth
    return pl.pallas_call(
        functools.partial(reduce_kernel, depth, bits, phases, half, span),
        name="reduce_gradients",
        in_specs=[pl.BlockSpec(memory_space=pl.ANY)],
        out_specs=[pl.BlockSpec(memory_space=pltpu.VMEM)] * 2,
        out_shape=[
            jax.ShapeDtypeStruct((phases * 2 * half,) + tile, f32),
            jax.ShapeDtypeStruct(tile, f32),
        ],
        scratch_shapes=[
            pltpu.VMEM((phases,) + (2,) * n + (depth, 2 * half) + tile, f32),
            pltpu.VMEM((phases,) + (2,) * n + (depth, 2 * half) + tile, f32),
        ]
        + [pltpu.VMEM((phases, 2) + (2,) * (n - 1 - s) + (depth, half) + tile, f32) for s in range(n)]
        + [pltpu.VMEM((phases, depth, 2 * half) + tile, f32)] * 2
        + [
            pltpu.VMEM((depth,) + tile, f32),
            pltpu.VMEM((2 * bits + 1,) + tile, f32),
            pltpu.VMEM(tile, f32),
            dma((spots,)),
            dma((spots,)),
            dma((spots,)),
            dma((phases * n * 2,)),
            dma((phases * n * 2,)),
            dma((phases * (depth - 1) * 2,)),
            dma((2, phases, depth)),
            dma((bits + 2 * (depth - 1),)),
            dma((bits + 2 * (depth - 1),)),
        ],
        compiler_params=pltpu.CompilerParams(
            vmem_limit_bytes=VMEM_BYTES, collective_id=1, has_side_effects=True
        ),
    )(flat)


def owned_params(params, counts, base, high):
    norm_gain, in_weight, out_weight = params[0], params[1], params[-1]
    per = in_weight.shape[1] // ROW
    small = jnp.concatenate([v.reshape(-1, ROW).astype(f32) for v in params[2:-1]], 0)
    starts = [0, norm_gain.size // ROW]
    starts.append(starts[1] + in_weight.size // ROW)
    starts.append(starts[2] + small.shape[0])
    rows = min(high // per + 2, in_weight.shape[0])
    first = jnp.clip((base - starts[1]) // per, 0, in_weight.shape[0] - rows)
    in_part = lax.dynamic_slice_in_dim(in_weight, first, rows).astype(f32).reshape(rows * per, ROW)
    deep = min(high, out_weight.shape[0])
    begin = jnp.clip(base - starts[3], 0, out_weight.shape[0] - deep)
    out_part = lax.dynamic_slice_in_dim(out_weight, begin, deep).astype(f32)
    place = base + lax.iota(jnp.int32, high)[:, None]
    total = jnp.broadcast_to(norm_gain.reshape(1, -1), (high, ROW))
    for part, origin, low in (
        (in_part, starts[1] + first * per, starts[1]),
        (small, starts[2], starts[2]),
        (out_part, starts[3] + begin, starts[3]),
    ):
        padded = jnp.pad(part, ((high, high), (0, 0)))
        offset = jnp.clip(base - origin + high, 0, part.shape[0] + high)
        total = jnp.where(place >= low, lax.dynamic_slice_in_dim(padded, offset, high), total)
    return total


def exchange(totals, state):
    count = lax.axis_size("blk")
    index = lax.axis_index("blk")
    decay, end, leave = totals[:state], totals[state : 2 * state], totals[2 * state :]
    pre_decay, pre_state = jnp.ones_like(decay), jnp.zeros_like(end)
    post_decay, post_state = jnp.ones_like(decay), jnp.zeros_like(end)
    bit = 1
    while bit < count:
        pairs = [(i, i ^ bit) for i in range(count)]
        far = lax.ppermute(jnp.concatenate([decay, end, leave], 0), "blk", pairs)
        far_decay, far_end, far_leave = far[:state], far[state : 2 * state], far[2 * state :]
        upper = (index & bit) != 0
        pre_state = jnp.where(upper, pre_state + pre_decay * far_end, pre_state)
        pre_decay = jnp.where(upper, pre_decay * far_decay, pre_decay)
        post_state = jnp.where(upper, post_state, post_state + post_decay * far_leave)
        post_decay = jnp.where(upper, post_decay, post_decay * far_decay)
        end = jnp.where(upper, end + decay * far_end, far_end + far_decay * end)
        leave = jnp.where(upper, far_leave + far_decay * leave, leave + decay * far_leave)
        decay = decay * far_decay
        bit *= 2
    return pre_state, post_state


def local(
    tokens,
    out_cot,
    norm_gain,
    in_weight,
    conv_weight,
    conv_bias,
    xproj_weight,
    dt_weight,
    dt_bias,
    a_log,
    d_skip,
    out_weight,
    moment_one,
    moment_two,
):
    contract = (((0,), (0,)), ((), ()))
    backward = (((1,), (1,)), ((), ()))
    token_rows = interleave(tokens[0])
    cot_low = interleave(out_cot[0])
    source = token_rows.astype(f32)
    length = source.shape[0]
    inner = dt_bias.shape[0]
    state = a_log.shape[0]
    rank = dt_weight.shape[0]
    width = conv_weight.shape[0]
    halo = (width - 1) * SUB
    scale = lax.rsqrt(jnp.mean(source * source, axis=-1, keepdims=True) + EPS)
    normed = (source * scale * norm_gain).astype(bf16)
    stream = jnp.dot(normed, in_weight[:, :inner], preferred_element_type=f32)
    ends = stream[length - halo :].reshape(width - 1, SUB, inner)
    tail = shifted(ends[:, SUB - 1], "blk", 1)
    gating = jnp.dot(normed, in_weight[:, inner:], preferred_element_type=f32)
    grad_gated = lax.dot_general(cot_low, out_weight, backward, preferred_element_type=f32)
    head = jnp.concatenate([tail[:, None], ends[:, : SUB - 1]], 1).reshape(halo, inner)
    longer = jnp.concatenate([head, stream], 0)

    def delayed(lag):
        return longer[halo - lag * SUB : halo - lag * SUB + length]

    conv_sum = conv_bias + conv_weight[width - 1] * stream
    for offset in range(width - 1):
        conv_sum = conv_sum + conv_weight[offset] * delayed(width - 1 - offset)
    conv_low = (conv_sum * jax.nn.sigmoid(conv_sum)).astype(bf16)
    conv_val = conv_low.astype(f32)
    selectors = jnp.dot(conv_low, xproj_weight, preferred_element_type=f32)
    step_low = selectors[:, :rank].astype(bf16)
    step_pre = jnp.dot(step_low, dt_weight, preferred_element_type=f32) + dt_bias
    step_size = jax.nn.softplus(step_pre)
    drive = step_size * conv_val
    gate_sig = jax.nn.sigmoid(gating)
    gate_val = gating * gate_sig
    grad_scanned = grad_gated * gate_val
    rates = -jnp.exp(a_log)
    rates_wide = jnp.repeat(rates * LOG2E, SUB, axis=0)

    pre_decay, pre_state, post_decay, post_state, totals = summary_call(
        step_size, drive, grad_scanned, selectors, rates_wide, rank
    )
    entry, arriving = exchange(totals, state)
    scan_out, prior, readout_grads = forward_call(
        step_size, drive, grad_scanned, selectors, rates_wide, pre_decay, pre_state, entry, rank
    )
    scanned = scan_out + d_skip * conv_val
    gated = (scanned * gate_val).astype(bf16)
    output = jnp.dot(gated, out_weight, preferred_element_type=f32)
    result = restore((source + output).astype(bf16))[None]
    grad_out_weight = lax.dot_general(gated, cot_low, contract, preferred_element_type=f32)
    grad_gating = (grad_gated * scanned * (gate_sig * (1.0 + gating * (1.0 - gate_sig)))).astype(bf16)
    grad_in_gate = lax.dot_general(normed, grad_gating, contract, preferred_element_type=f32)
    grad_d_skip = jnp.sum(grad_scanned * conv_val, 0)

    through, feed, inject_grads, rate_grads = backward_call(
        step_size, drive, grad_scanned, selectors, rates_wide, post_decay, post_state, arriving, prior, rank
    )
    grad_a_log = LN2 * jnp.sum(rate_grads.reshape(state, SUB, inner), 1)
    step_sig = jax.nn.sigmoid(step_pre)
    tiny = step_size < 1e-30
    ratio = jnp.where(tiny, 1.0, step_sig / jnp.where(tiny, 1.0, step_size))
    grad_pre = LN2 * through * ratio + conv_val * feed * step_sig
    grad_dt_bias = jnp.sum(grad_pre, 0)
    grad_pre_low = grad_pre.astype(bf16)
    grad_dt_weight = lax.dot_general(step_low, grad_pre_low, contract, preferred_element_type=f32)
    grad_step_low = lax.dot_general(grad_pre_low, dt_weight, backward, preferred_element_type=f32)
    grad_selectors = jnp.concatenate(
        [grad_step_low, inject_grads[:, :state], readout_grads[:, :state]], 1
    ).astype(bf16)
    grad_xproj = lax.dot_general(conv_low, grad_selectors, contract, preferred_element_type=f32)
    grad_conv_out = (
        grad_scanned * d_skip
        + step_size * feed
        + lax.dot_general(grad_selectors, xproj_weight, backward, preferred_element_type=f32)
    )
    grad_conv = grad_conv_out * silu_slope(conv_sum)
    begins = grad_conv[:halo].reshape(width - 1, SUB, inner)
    ahead = shifted(begins[:, 0], "blk", -1)
    foot = jnp.concatenate([begins[:, 1:], ahead[:, None]], 1).reshape(halo, inner)
    further = jnp.concatenate([grad_conv, foot], 0)
    grad_stream = conv_weight[width - 1] * grad_conv
    tap_grads = []
    for offset in range(width - 1):
        lead = width - 1 - offset
        grad_stream = grad_stream + conv_weight[offset] * further[lead * SUB : lead * SUB + length]
        tap_grads.append(jnp.sum(grad_conv * delayed(lead), 0))
    tap_grads.append(jnp.sum(grad_conv * stream, 0))
    grad_conv_weight = jnp.stack(tap_grads, 0)
    grad_conv_bias = jnp.sum(grad_conv, 0)
    grad_stream_low = grad_stream.astype(bf16)
    grad_in_stream = lax.dot_general(normed, grad_stream_low, contract, preferred_element_type=f32)
    grad_normed = lax.dot_general(
        jnp.concatenate([grad_stream_low, grad_gating], 1), in_weight, backward, preferred_element_type=f32
    )
    grad_gain = jnp.sum(grad_normed * source * scale, 0)
    weighted = grad_normed * norm_gain
    grad_source = (
        scale * weighted
        - source * scale**3 * jnp.mean(weighted * source, axis=-1, keepdims=True)
        + cot_low.astype(f32)
    )
    grad_tokens = restore(grad_source.astype(bf16))[None]
    span = moment_one.shape[0]
    small = jnp.concatenate(
        [
            value.reshape(-1, ROW)
            for value in (
                grad_conv_weight,
                grad_conv_bias,
                grad_xproj,
                grad_dt_weight,
                grad_dt_bias,
                grad_a_log,
                grad_d_skip,
            )
        ],
        0,
    ).reshape(-1, SUB, LANE)
    params = (
        norm_gain,
        in_weight,
        conv_weight,
        conv_bias,
        xproj_weight,
        dt_weight,
        dt_bias,
        a_log,
        d_skip,
        out_weight,
    )
    counts = [value.size for value in params]
    lower = sum(counts[:6])
    upper = sum(counts[:9])
    phases = 4 if span >= 16 * ROW * 4 else 1
    high = window_tiles(span, phases)
    flat = flatten_call(
        grad_in_stream, grad_in_gate, grad_out_weight, grad_gain.reshape(1, SUB, LANE), small, sum(counts) // ROW + high
    )
    reduced, norm = reduce_call(flat, span, phases)
    grad_norm = norm[0, 0]
    begin = lax.axis_index(("batch", "blk")) * span
    shard = lax.dynamic_slice_in_dim(reduced.reshape(-1), begin % ROW, span)
    owned = owned_params(params, counts, begin // ROW, high)
    owned = lax.dynamic_slice_in_dim(owned.reshape(-1), begin % ROW, span)
    place = begin + lax.iota(jnp.int32, span)
    keep = jnp.where((place >= lower) & (place < upper), 0.0, 1.0).astype(f32)
    clipped = shard * jnp.minimum(1.0, CLIP / (grad_norm + 1e-06))
    new_one = BETA_ONE * moment_one + (1.0 - BETA_ONE) * clipped
    new_two = BETA_TWO * moment_two + (1.0 - BETA_TWO) * clipped * clipped
    first = new_one / (1.0 - BETA_ONE**ADAM_STEP)
    second = new_two / (1.0 - BETA_TWO**ADAM_STEP)
    param_step = -RATE * (first / (jnp.sqrt(second) + ADAM_EPS) + DECAY * keep * owned)
    return (result, grad_tokens, shard, grad_norm, param_step, new_one, new_two)


def solution(mesh):
    return jax.shard_map(
        local,
        mesh=mesh,
        in_specs=(P("batch", "blk", None),) * 2 + (P(),) * 10 + (P(("batch", "blk")),) * 2,
        out_specs=(P("batch", "blk", None),) * 2
        + (P(("batch", "blk")), P(), P(("batch", "blk")), P(("batch", "blk")), P(("batch", "blk"))),
        check_vma=False,
    )
```

```python
import functools
import math

import jax
import jax.numpy as jnp
from jax import lax
from jax.experimental import pallas as pl
from jax.experimental.pallas import tpu as pltpu
from jax.sharding import PartitionSpec as P

ADAM_STEP = 100
EPS = 1e-05
RATE = 0.002
BETA_ONE = 0.9
BETA_TWO = 0.95
ADAM_EPS = 1e-08
DECAY = 0.1
CLIP = 1.0

LOG2E = 1.0 / math.log(2.0)
LN2 = math.log(2.0)
SUB = 8
LANE = 128
ROW = 1024
VMEM_BYTES = 56 * 2**20

MESH = pl.DeviceIdType.MESH

f32 = jnp.float32
bf16 = jnp.bfloat16


def shifted(x, axis, by):
    count = lax.axis_size(axis)
    pairs = [(i, i + by) for i in range(count) if 0 <= i + by < count]
    return lax.ppermute(x, axis, pairs)


def silu_slope(value):
    sig = jax.nn.sigmoid(value)
    return sig * (1.0 + value * (1.0 - sig))


def interleave(x):
    rows, width = x.shape
    return x.reshape(SUB, rows // SUB, width).transpose(1, 0, 2).reshape(rows, width)


def restore(x):
    rows, width = x.shape
    return x.reshape(rows // SUB, SUB, width).transpose(1, 0, 2).reshape(rows, width)


def at(start, size):
    return pl.ds(pl.multiple_of(start, size), size)


def spread(sel_ref, spots_ref, out_ref):
    out_ref[...] = jnp.dot(sel_ref[...], spots_ref[...], preferred_element_type=f32)


def gather_lanes(src_ref, spots_ref, out_ref):
    value = src_ref[...]
    high = value.astype(bf16)
    low = (value - high.astype(f32)).astype(bf16)
    spots = spots_ref[0:LANE, 0 : value.shape[1]]
    back = (((1,), (1,)), ((), ()))
    out_ref[...] = lax.dot_general(high, spots, back, preferred_element_type=f32) + lax.dot_general(
        low, spots, back, preferred_element_type=f32
    )


def split_selectors(values):
    high = lax.reduce_precision(values, 8, 7)
    middle = lax.reduce_precision(values - high, 8, 7)
    terms = jnp.concatenate([high, middle, values - high - middle], 1)
    count = values.shape[1]
    terms = jnp.pad(terms, ((0, 0), (0, LANE - 3 * count))).astype(bf16)
    row = lax.broadcasted_iota(jnp.int32, (LANE, count * LANE), 0)
    col = lax.broadcasted_iota(jnp.int32, (LANE, count * LANE), 1) // LANE
    spots = ((row % count == col) & (row < 3 * count)).astype(bf16)
    return terms, spots


def summary_kernel(
    shape,
    step_ref,
    drive_ref,
    grad_ref,
    sel_ref,
    spots_ref,
    rates_ref,
    pre_decay_ref,
    pre_state_ref,
    post_decay_ref,
    post_state_ref,
    totals_ref,
    end_ref,
    exit_ref,
    prod_ref,
    select_ref,
):
    tiles, state, inner, cols, group = shape
    turn = pl.program_id(0)

    @pl.when(turn == 0)
    def _():
        end_ref[...] = jnp.zeros_like(end_ref)
        exit_ref[...] = jnp.zeros_like(exit_ref)
        prod_ref[...] = jnp.ones_like(prod_ref)

    spread(sel_ref, spots_ref, select_ref)

    def columns(c, carry):
        lanes = [at((c * cols + k) * LANE, LANE) for k in range(cols)]
        for first in range(0, state, group):
            spots = [(n, k) for n in range(group) for k in range(cols)]
            where = [(slice((first + n) * SUB, (first + n + 1) * SUB), lanes[k]) for n, k in spots]
            rates = [rates_ref[w] for w in where]

            def advance(i, carry):
                ends, exits, prods = carry
                here = at(i * SUB, SUB)
                step = [step_ref[here, l] for l in lanes]
                drive = [drive_ref[here, l] for l in lanes]
                grad = [grad_ref[here, l] for l in lanes]
                inject = [select_ref[here, (first + n) * LANE : (first + n + 1) * LANE] for n in range(group)]
                readout = [
                    select_ref[here, (state + first + n) * LANE : (state + first + n + 1) * LANE] for n in range(group)
                ]
                new = ([], [], [])
                for s, (n, k) in enumerate(spots):
                    decay = jnp.exp2(step[k] * rates[s])
                    prod = prods[s] * decay
                    new[0].append(ends[s] * decay + drive[k] * inject[n])
                    new[1].append(exits[s] + prod * (grad[k] * readout[n]))
                    new[2].append(prod)
                return tuple(tuple(x) for x in new)

            start = tuple(tuple(ref[w] for w in where) for ref in (end_ref, exit_ref, prod_ref))
            ends, exits, prods = lax.fori_loop(0, tiles, advance, start, unroll=16)
            for s, w in enumerate(where):
                end_ref[w] = ends[s]
                exit_ref[w] = exits[s]
                prod_ref[w] = prods[s]
        return carry

    lax.fori_loop(0, inner // (LANE * cols), columns, 0)

    @pl.when(turn == pl.num_programs(0) - 1)
    def _():
        row = lax.broadcasted_iota(jnp.int32, (SUB, LANE), 0)

        def columns(c, carry):
            lanes = at(c * LANE, LANE)
            for n in range(state):
                here = (slice(n * SUB, (n + 1) * SUB), lanes)
                for way, src, decay_out, state_out, total_row in (
                    (1, end_ref, pre_decay_ref, pre_state_ref, 1),
                    (-1, exit_ref, post_decay_ref, post_state_ref, 2),
                ):
                    decay, value = prod_ref[here], src[here]

                    def seen(by):
                        return row >= by if way > 0 else row < SUB - by

                    for by in (1, 2, 4):
                        far_decay = pltpu.roll(decay, by if way > 0 else SUB - by, 0)
                        far_value = pltpu.roll(value, by if way > 0 else SUB - by, 0)
                        value = jnp.where(seen(by), value + decay * far_value, value)
                        decay = jnp.where(seen(by), decay * far_decay, decay)
                    last = SUB - 1 if way > 0 else 0
                    totals_ref[pl.ds(n, 1), lanes] = decay[last : last + 1]
                    totals_ref[pl.ds(total_row * state + n, 1), lanes] = value[last : last + 1]
                    turn_by = 1 if way > 0 else SUB - 1
                    decay_out[here] = jnp.where(seen(1), pltpu.roll(decay, turn_by, 0), 1.0)
                    state_out[here] = jnp.where(seen(1), pltpu.roll(value, turn_by, 0), 0.0)
            return carry

        lax.fori_loop(0, inner // LANE, columns, 0)


def forward_kernel(
    shape,
    step_ref,
    drive_ref,
    grad_ref,
    sel_ref,
    spots_ref,
    rates_ref,
    pre_decay_ref,
    pre_state_ref,
    entry_ref,
    conv_ref,
    gating_ref,
    grad_gated_ref,
    skip_ref,
    prior_ref,
    readout_grad_ref,
    gated_ref,
    grad_gating_ref,
    skip_grad_ref,
    state_ref,
    select_ref,
    sums_ref,
    scanned_ref,
):
    tiles, state, inner, cols, group = shape

    @pl.when(pl.program_id(0) == 0)
    def _():
        skip_grad_ref[...] = jnp.zeros_like(skip_grad_ref)
        for n in range(state):
            here = slice(n * SUB, (n + 1) * SUB)
            state_ref[here, :] = pre_state_ref[here, :] + pre_decay_ref[here, :] * entry_ref[n : n + 1, :]

    spread(sel_ref, spots_ref, select_ref)
    sums_ref[...] = jnp.zeros_like(sums_ref)

    def columns(c, carry):
        lanes = [at((c * cols + k) * LANE, LANE) for k in range(cols)]
        for first in range(0, state, group):
            spots = [(n, k) for n in range(group) for k in range(cols)]
            where = [(slice((first + n) * SUB, (first + n + 1) * SUB), lanes[k]) for n, k in spots]
            rates = [rates_ref[w] for w in where]

            def advance(i, states):
                here = at(i * SUB, SUB)
                step = [step_ref[here, l] for l in lanes]
                drive = [drive_ref[here, l] for l in lanes]
                grad = [grad_ref[here, l] for l in lanes]
                outs = [None] * cols
                new = []
                for n in range(group):
                    spot = slice((first + n) * LANE, (first + n + 1) * LANE)
                    inject = select_ref[here, spot]
                    readout = select_ref[here, (state + first + n) * LANE : (state + first + n + 1) * LANE]
                    total = None
                    for k in range(cols):
                        s = n * cols + k
                        decay = jnp.exp2(step[k] * rates[s])
                        fresh = decay * states[s] + drive[k] * inject
                        new.append(fresh)
                        part = readout * fresh
                        outs[k] = part if outs[k] is None else outs[k] + part
                        part = grad[k] * fresh
                        total = part if total is None else total + part
                    sums_ref[here, spot] += total
                    if n % 2 == 1:
                        pair = pl.ds(pl.multiple_of((i * state + first + n - 1) * SUB, 2 * SUB), 2 * SUB)
                        for k in range(cols):
                            prior_ref[pair, lanes[k]] = jnp.concatenate(
                                [states[(n - 1) * cols + k], states[n * cols + k]], 0
                            ).astype(bf16)
                for k in range(cols):
                    if first == 0:
                        scanned_ref[here, lanes[k]] = outs[k]
                    else:
                        scanned_ref[here, lanes[k]] += outs[k]
                return tuple(new)

            states = lax.fori_loop(0, tiles, advance, tuple(state_ref[w] for w in where), unroll=16)
            for s, w in enumerate(where):
                state_ref[w] = states[s]
        return carry

    lax.fori_loop(0, inner // (LANE * cols), columns, 0)
    gather_lanes(sums_ref, spots_ref, readout_grad_ref)

    def finish(c, carry):
        lanes = at(c * 2 * LANE, 2 * LANE)
        skip = skip_ref[:, lanes]

        def pair(i, total):
            here = at(i * 2 * SUB, 2 * SUB)
            conv = conv_ref[here, lanes].astype(f32)
            gating = gating_ref[here, lanes]
            sig = jax.nn.sigmoid(gating)
            gate = gating * sig
            scanned = scanned_ref[here, lanes] + skip * conv
            gated_ref[here, lanes] = (scanned * gate).astype(bf16)
            slope = sig + gate * (1.0 - sig)
            grad_gating_ref[here, lanes] = (grad_gated_ref[here, lanes] * scanned * slope).astype(bf16)
            product = grad_ref[here, lanes] * conv
            return total + product[:SUB] + product[SUB:]

        zero = jnp.zeros((SUB, 2 * LANE), f32)
        skip_grad_ref[:, lanes] += lax.fori_loop(0, tiles // 2, pair, zero, unroll=4)
        return carry

    lax.fori_loop(0, inner // (2 * LANE), finish, 0)


def backward_kernel(
    shape,
    step_ref,
    drive_ref,
    grad_ref,
    sel_ref,
    spots_ref,
    rates_ref,
    post_decay_ref,
    post_state_ref,
    arriving_ref,
    prior_ref,
    conv_sum_ref,
    stream_ref,
    readout_grad_ref,
    step_back_ref,
    select_back_ref,
    taps_ref,
    skip_ref,
    grad_stream_ref,
    grad_pre_ref,
    grad_select_ref,
    rate_grad_ref,
    taps_grad_ref,
    edge_ref,
    carry_ref,
    select_ref,
    sums_ref,
    through_ref,
    feed_ref,
    grad_conv_ref,
    inject_grad_ref,
    probe_ref,
    probe_sems,
):
    tiles, state, inner, cols, group = shape
    blk = lax.axis_index("blk")
    other = blk + 1 - 2 * (blk % 2)

    def probe():
        return pltpu.make_async_remote_copy(
            src_ref=probe_ref.at[0],
            dst_ref=probe_ref.at[1],
            send_sem=probe_sems.at[0],
            recv_sem=probe_sems.at[1],
            device_id={"blk": other},
            device_id_type=MESH,
        )

    @pl.when(pl.program_id(0) == 0)
    def _():
        barrier = pltpu.get_barrier_semaphore()
        pl.semaphore_signal(barrier, inc=1, device_id={"blk": other}, device_id_type=MESH)
        pl.semaphore_wait(barrier, 1)
        probe_ref[0] = jnp.ones((SUB, LANE), f32)
        probe().start()

    @pl.when(pl.program_id(0) == pl.num_programs(0) - 1)
    def _():
        probe().wait()

    block = tiles * SUB
    width = taps_ref.shape[0]
    halo = (width - 1) * SUB

    @pl.when(pl.program_id(0) == 0)
    def _():
        rate_grad_ref[...] = jnp.zeros_like(rate_grad_ref)
        taps_grad_ref[...] = jnp.zeros_like(taps_grad_ref)
        grad_conv_ref[tiles * SUB :, :] = jnp.zeros((grad_conv_ref.shape[0] - tiles * SUB, inner), f32)
        for n in range(state):
            here = slice(n * SUB, (n + 1) * SUB)
            carry_ref[here, :] = post_state_ref[here, :] + post_decay_ref[here, :] * arriving_ref[n : n + 1, :]

    spread(sel_ref, spots_ref, select_ref)
    sums_ref[...] = jnp.zeros_like(sums_ref)

    def columns(c, carry):
        lanes = [at((c * cols + k) * LANE, LANE) for k in range(cols)]
        for first in range(0, state, group):
            spots = [(n, k) for n in range(group) for k in range(cols)]
            where = [(slice((first + n) * SUB, (first + n + 1) * SUB), lanes[k]) for n, k in spots]
            rates = [rates_ref[w] for w in where]

            def retreat(turn, carry):
                carries, rate_grads = carry
                i = tiles - 1 - turn
                here = at(i * SUB, SUB)
                step = [step_ref[here, l] for l in lanes]
                drive = [drive_ref[here, l] for l in lanes]
                grad = [grad_ref[here, l] for l in lanes]
                throughs = [None] * cols
                feeds = [None] * cols
                new = ([], [])
                for n in range(group):
                    spot = slice((first + n) * LANE, (first + n + 1) * LANE)
                    inject = select_ref[here, spot]
                    readout = select_ref[here, (state + first + n) * LANE : (state + first + n + 1) * LANE]
                    if n % 2 == 0:
                        pair = pl.ds(pl.multiple_of((i * state + first + n) * SUB, 2 * SUB), 2 * SUB)
                        pairs = [prior_ref[pair, lanes[k]].astype(f32) for k in range(cols)]
                    total = None
                    for k in range(cols):
                        s = n * cols + k
                        prior = pairs[k][(n % 2) * SUB : (n % 2 + 1) * SUB]
                        power = step[k] * rates[s]
                        adjoint = grad[k] * readout + carries[s]
                        back = jnp.exp2(power) * adjoint
                        through = back * prior * power
                        new[0].append(back)
                        new[1].append(rate_grads[s] + through)
                        throughs[k] = through if throughs[k] is None else throughs[k] + through
                        part = adjoint * inject
                        feeds[k] = part if feeds[k] is None else feeds[k] + part
                        part = adjoint * drive[k]
                        total = part if total is None else total + part
                    sums_ref[here, spot] += total
                for k in range(cols):
                    if first == 0:
                        through_ref[here, lanes[k]] = throughs[k]
                        feed_ref[here, lanes[k]] = feeds[k]
                    else:
                        through_ref[here, lanes[k]] += throughs[k]
                        feed_ref[here, lanes[k]] += feeds[k]
                return tuple(tuple(x) for x in new)

            start = tuple(tuple(ref[w] for w in where) for ref in (carry_ref, rate_grad_ref))
            carries, rate_grads = lax.fori_loop(0, tiles, retreat, start, unroll=16)
            for s, w in enumerate(where):
                carry_ref[w] = carries[s]
                rate_grad_ref[w] = rate_grads[s]
        return carry

    lax.fori_loop(0, inner // (LANE * cols), columns, 0)
    gather_lanes(sums_ref, spots_ref, inject_grad_ref)

    def steps(c, carry):
        lanes = at(c * 2 * LANE, 2 * LANE)

        def pair(i, total):
            here = at(i * 2 * SUB, 2 * SUB)
            step = step_ref[here, lanes]
            series = 1.0 + step * (-1.0 / 2 + step * (1.0 / 6 + step * (-1.0 / 24 + step * (1.0 / 120))))
            near = step < 0.06
            exact = (1.0 - jnp.exp2(step * -LOG2E)) / jnp.where(near, 1.0, step)
            ratio = jnp.where(near, series, exact)
            pre = ratio * (LN2 * through_ref[here, lanes] + drive_ref[here, lanes] * feed_ref[here, lanes])
            grad_pre_ref[here, lanes] = pre.astype(bf16)
            return total + pre[:SUB] + pre[SUB:]

        zero = jnp.zeros((SUB, 2 * LANE), f32)
        taps_grad_ref[(width + 1) * SUB :, lanes] += lax.fori_loop(0, tiles // 2, pair, zero, unroll=4)
        return carry

    lax.fori_loop(0, inner // (2 * LANE), steps, 0)
    lane = lax.broadcasted_iota(jnp.int32, (block, LANE), 1)
    rank = LANE - 2 * state
    grads = jnp.dot(grad_pre_ref[...], step_back_ref[...], preferred_element_type=f32)
    grads = jnp.where(
        lane < state,
        inject_grad_ref[...],
        jnp.where(lane < 2 * state, pltpu.roll(readout_grad_ref[...], state, 1), grads),
    )
    grads = grads.astype(bf16)
    grad_select_ref[...] = grads

    def convs(c, carry):
        lanes = at(c * 2 * LANE, 2 * LANE)
        skip = skip_ref[:, lanes]
        feeds = jnp.dot(grads, select_back_ref[:, lanes], preferred_element_type=f32)
        through_ref[:, lanes] = feeds

        def conv(i, carry):
            here = at(i * SUB, SUB)
            value = conv_sum_ref[here, lanes]
            sig = jax.nn.sigmoid(value)
            slope = sig * (1.0 + value * (1.0 - sig))
            out = grad_ref[here, lanes] * skip + step_ref[here, lanes] * feed_ref[here, lanes] + through_ref[here, lanes]
            grad_conv_ref[here, lanes] = out * slope
            return carry

        lax.fori_loop(0, tiles, conv, 0, unroll=8)
        taps = [jnp.broadcast_to(taps_ref[k : k + 1, lanes], (SUB, 2 * LANE)) for k in range(width)]

        def tap(i, totals):
            totals = list(totals)
            done = []
            for q in range(2):
                parts = [
                    grad_conv_ref[pl.ds(pl.multiple_of((2 * i + q + m) * SUB, SUB), SUB), lanes] for m in range(width)
                ]
                stream = stream_ref[pl.ds(pl.multiple_of((2 * i + q) * SUB, SUB), SUB), lanes]
                grad = taps[width - 1] * parts[0]
                totals[width - 1] = totals[width - 1] + parts[0] * stream
                totals[width] = totals[width] + parts[0]
                for m in range(1, width):
                    grad = grad + taps[width - 1 - m] * parts[m]
                    totals[width - 1 - m] = totals[width - 1 - m] + parts[m] * stream
                done.append(grad)
            grad_stream_ref[at(i * 2 * SUB, 2 * SUB), lanes] = jnp.concatenate(done, 0).astype(bf16)
            return tuple(totals)

        zero = jnp.zeros((SUB, 2 * LANE), f32)
        totals = lax.fori_loop(0, tiles // 2, tap, (zero,) * (width + 1), unroll=4)
        for k in range(width + 1):
            taps_grad_ref[k * SUB : (k + 1) * SUB, lanes] += totals[k]
        return carry

    lax.fori_loop(0, inner // (2 * LANE), convs, 0)

    @pl.when(pl.program_id(0) == 0)
    def _():
        edge_ref[halo:, :] = grad_conv_ref[block - halo : block, :]

    edge_ref[:halo, :] = grad_conv_ref[:halo, :]
    grad_conv_ref[block:, :] = grad_conv_ref[:halo, :]


def scan_shapes(rows, state, inner):
    tiles = min(16, rows // SUB)
    count = rows // (SUB * tiles)
    return tiles, count


def summary_call(step, drive, grad, sel, spots, rates):
    rows, inner = step.shape
    state = rates.shape[0] // SUB
    tiles, count = scan_shapes(rows, state, inner)
    wide = pl.BlockSpec((tiles * SUB, inner), lambda t: (t, 0))
    table = pl.BlockSpec(spots.shape, lambda t: (0, 0))
    thin = pl.BlockSpec((tiles * SUB, sel.shape[1]), lambda t: (t, 0))
    whole = pl.BlockSpec((state * SUB, inner), lambda t: (0, 0))
    total = pl.BlockSpec((3 * state, inner), lambda t: (0, 0))
    shape = (tiles, state, inner, 2, 4)
    big = jax.ShapeDtypeStruct((state * SUB, inner), f32)
    return pl.pallas_call(
        functools.partial(summary_kernel, shape),
        name="scan_summary",
        grid=(count,),
        in_specs=[wide, wide, wide, thin, table, whole],
        out_specs=[whole] * 4 + [total],
        out_shape=[big] * 4 + [jax.ShapeDtypeStruct((3 * state, inner), f32)],
        scratch_shapes=[pltpu.VMEM((state * SUB, inner), f32)] * 3
        + [pltpu.VMEM((tiles * SUB, 2 * state * LANE), f32)],
        compiler_params=pltpu.CompilerParams(vmem_limit_bytes=VMEM_BYTES),
    )(step, drive, grad, sel, spots, rates)


def forward_call(step, drive, grad, sel, spots, rates, pre_decay, pre_state, entry, conv, gating, grad_gated, skip):
    rows, inner = step.shape
    state = rates.shape[0] // SUB
    tiles, count = scan_shapes(rows, state, inner)
    wide = pl.BlockSpec((tiles * SUB, inner), lambda t: (t, 0))
    table = pl.BlockSpec(spots.shape, lambda t: (0, 0))
    thin = pl.BlockSpec((tiles * SUB, sel.shape[1]), lambda t: (t, 0))
    whole = pl.BlockSpec((state * SUB, inner), lambda t: (0, 0), pipeline_mode=pl.Buffered(1))
    line = pl.BlockSpec((1, inner), lambda t: (0, 0))
    short = pl.BlockSpec((state, inner), lambda t: (0, 0))
    shape = (tiles, state, inner, 2, 8)
    return pl.pallas_call(
        functools.partial(forward_kernel, shape),
        name="scan_forward",
        grid=(count,),
        in_specs=[wide, wide, wide, thin, table, whole, whole, whole, short, wide, wide, wide, line],
        out_specs=[
            pl.BlockSpec((tiles * state * SUB, inner), lambda t: (t, 0)),
            pl.BlockSpec((tiles * SUB, LANE), lambda t: (t, 0)),
            wide,
            wide,
            pl.BlockSpec((SUB, inner), lambda t: (0, 0)),
        ],
        out_shape=[
            jax.ShapeDtypeStruct((rows * state, inner), bf16),
            jax.ShapeDtypeStruct((rows, LANE), f32),
            jax.ShapeDtypeStruct((rows, inner), bf16),
            jax.ShapeDtypeStruct((rows, inner), bf16),
            jax.ShapeDtypeStruct((SUB, inner), f32),
        ],
        scratch_shapes=[pltpu.VMEM((state * SUB, inner), f32)]
        + [
            pltpu.VMEM((tiles * SUB, 2 * state * LANE), f32),
            pltpu.VMEM((tiles * SUB, state * LANE), f32),
            pltpu.VMEM((tiles * SUB, inner), f32),
        ],
        compiler_params=pltpu.CompilerParams(vmem_limit_bytes=VMEM_BYTES),
    )(step, drive, grad, sel, spots, rates, pre_decay, pre_state, entry, conv, gating, grad_gated, skip)


def backward_call(step, drive, grad, sel, spots, rates, post_decay, post_state, arriving, prior, conv_sum, stream, readout_grad, step_back, select_back, taps, skip):
    rows, inner = step.shape
    state = rates.shape[0] // SUB
    tiles, count = scan_shapes(rows, state, inner)

    def back(t):
        return (count - 1 - t, 0)

    wide = pl.BlockSpec((tiles * SUB, inner), back)
    table = pl.BlockSpec(spots.shape, lambda t: (0, 0))
    thin = pl.BlockSpec((tiles * SUB, sel.shape[1]), back)
    whole = pl.BlockSpec((state * SUB, inner), lambda t: (0, 0), pipeline_mode=pl.Buffered(1))
    short = pl.BlockSpec((state, inner), lambda t: (0, 0))
    narrow = pl.BlockSpec((tiles * SUB, LANE), back)
    width = taps.shape[0]
    halo = (width - 1) * SUB

    def fixed(x):
        return pl.BlockSpec(x.shape, lambda t: (0, 0), pipeline_mode=pl.Buffered(1))

    shape = (tiles, state, inner, 2, 4)
    return pl.pallas_call(
        functools.partial(backward_kernel, shape),
        name="scan_backward",
        grid=(count,),
        in_specs=[wide, wide, wide, thin, table, whole, whole, whole, short]
        + [pl.BlockSpec((tiles * state * SUB, inner), back), wide, wide, narrow]
        + [fixed(step_back), fixed(select_back), fixed(taps), fixed(skip)],
        out_specs=[
            wide,
            wide,
            narrow,
            pl.BlockSpec((state * SUB, inner), lambda t: (0, 0)),
            pl.BlockSpec(((width + 2) * SUB, inner), lambda t: (0, 0)),
            pl.BlockSpec((2 * halo, inner), lambda t: (0, 0)),
        ],
        out_shape=[
            jax.ShapeDtypeStruct((rows, inner), bf16),
            jax.ShapeDtypeStruct((rows, inner), bf16),
            jax.ShapeDtypeStruct((rows, LANE), bf16),
            jax.ShapeDtypeStruct((state * SUB, inner), f32),
            jax.ShapeDtypeStruct(((width + 2) * SUB, inner), f32),
            jax.ShapeDtypeStruct((2 * halo, inner), f32),
        ],
        scratch_shapes=[pltpu.VMEM((state * SUB, inner), f32)]
        + [
            pltpu.VMEM((tiles * SUB, 2 * state * LANE), f32),
            pltpu.VMEM((tiles * SUB, state * LANE), f32),
            pltpu.VMEM((tiles * SUB, inner), f32),
            pltpu.VMEM((tiles * SUB, inner), f32),
            pltpu.VMEM((tiles * SUB + halo, inner), f32),
            pltpu.VMEM((tiles * SUB, LANE), f32),
            pltpu.VMEM((2, SUB, LANE), f32),
            pltpu.SemaphoreType.DMA((2,)),
        ],
        compiler_params=pltpu.CompilerParams(vmem_limit_bytes=VMEM_BYTES, collective_id=2, has_side_effects=True),
    )(step, drive, grad, sel, spots, rates, post_decay, post_state, arriving, prior, conv_sum, stream, readout_grad, step_back, select_back, taps, skip)


def turn_tiles(tiles):
    row = lax.broadcasted_iota(jnp.int32, (SUB, LANE), 0)
    for bit in (1, 2, 4):
        upper = (row // bit) % 2 == 1
        new = list(tiles)
        for a in range(SUB):
            if a & bit == 0:
                b = a + bit
                new[a] = jnp.where(upper, pltpu.roll(tiles[b], bit, 0), tiles[a])
                new[b] = jnp.where(upper, tiles[b], pltpu.roll(tiles[a], SUB - bit, 0))
        tiles = new
    return tiles


def flatten_kernel(rows_in, rows_out, in_base, small_base, out_base, stream_ref, gate_ref, out_w_ref, gain_ref, small_ref, flat_ref, in_buf, out_buf, sems):
    turn = pl.program_id(0)
    count = pl.num_programs(0)
    slot = turn % 2
    half = stream_ref.shape[1] // LANE
    wide = 2 * half

    def copies(step, slot):
        size_in, size_out = rows_in * wide // SUB, rows_out
        return (
            pltpu.make_async_copy(
                in_buf.at[slot], flat_ref.at[pl.ds(in_base + step * size_in, size_in)], sems.at[slot]
            ),
            pltpu.make_async_copy(
                out_buf.at[slot], flat_ref.at[pl.ds(out_base + step * size_out, size_out)], sems.at[2 + slot]
            ),
        )

    def extras():
        return (
            pltpu.make_async_copy(gain_ref, flat_ref.at[pl.ds(0, gain_ref.shape[0])], sems.at[4]),
            pltpu.make_async_copy(
                small_ref, flat_ref.at[pl.ds(small_base, small_ref.shape[0])], sems.at[5]
            ),
        )

    @pl.when(turn == 0)
    def _():
        for copy in extras():
            copy.start()

    @pl.when(turn >= 2)
    def _():
        for copy in copies(turn - 2, slot):
            copy.wait()

    def lay(src, rows, first, buf, base, stride):
        tiles = [src[rows, (first + a) * LANE : (first + a + 1) * LANE] for a in range(SUB)]
        for r, tile in enumerate(turn_tiles(tiles)):
            buf[slot, base + r * stride] = tile

    per = wide // SUB
    for r in range(rows_in // SUB):
        rows = slice(r * SUB, (r + 1) * SUB)
        for q in range(per):
            src = stream_ref if q < per // 2 else gate_ref
            lay(src, rows, (q % (per // 2)) * SUB, in_buf, r * wide + q, per)
    for r in range(rows_out // SUB):
        rows = slice(r * SUB, (r + 1) * SUB)
        lay(out_w_ref, rows, 0, out_buf, r * SUB, 1)
    for copy in copies(turn, slot):
        copy.start()

    @pl.when(turn == count - 1)
    def _():
        for copy in copies(turn - 1, 1 - slot):
            copy.wait()
        for copy in copies(turn, slot):
            copy.wait()
        for copy in extras():
            copy.wait()


def flatten_call(stream, gate, out_w, gain, small, total):
    depth, half = stream.shape
    steps = 16
    rows_in, rows_out = depth // steps, out_w.shape[0] // steps
    wide = 2 * half // LANE
    in_base = gain.shape[0]
    small_base = in_base + depth * wide // SUB
    out_base = small_base + small.shape[0]
    return pl.pallas_call(
        functools.partial(flatten_kernel, rows_in, rows_out, in_base, small_base, out_base),
        name="flatten",
        grid=(steps,),
        in_specs=[
            pl.BlockSpec((rows_in, half), lambda t: (t, 0)),
            pl.BlockSpec((rows_in, half), lambda t: (t, 0)),
            pl.BlockSpec((rows_out, out_w.shape[1]), lambda t: (t, 0)),
            pl.BlockSpec(memory_space=pl.ANY),
            pl.BlockSpec(memory_space=pl.ANY),
        ],
        out_specs=pl.BlockSpec(memory_space=pl.ANY),
        out_shape=jax.ShapeDtypeStruct((total, SUB, LANE), f32),
        scratch_shapes=[
            pltpu.VMEM((2, rows_in * wide // SUB, SUB, LANE), f32),
            pltpu.VMEM((2, rows_out, SUB, LANE), f32),
            pltpu.SemaphoreType.DMA((6,)),
        ],
        compiler_params=pltpu.CompilerParams(vmem_limit_bytes=VMEM_BYTES),
    )(stream, gate, out_w, gain, small)


def reduce_kernel(
    depth,
    bits,
    phases,
    half,
    span,
    flat_ref,
    out_ref,
    norm_ref,
    acc,
    first_recv,
    *rest,
):
    n = bits - 1
    bit_recvs = rest[:n]
    down_recv, up_recv, ring, sums, square_ref = rest[n : n + 5]
    local_sem, core_send, core_recv, bit_send, bit_recv, z_send, z_recv, ring_send, ring_recv = rest[n + 5 :]
    blk = lax.axis_index("blk")
    z = lax.axis_index("batch")
    mine = [(blk // 2**b) % 2 for b in range(bits)]
    partner = [blk + (1 - 2 * mine[b]) * 2**b for b in range(bits)]
    below, above = (z + depth - 1) % depth, (z + 1) % depth
    barrier = pltpu.get_barrier_semaphore()
    for b in range(bits):
        pl.semaphore_signal(barrier, inc=1, device_id={"blk": partner[b]}, device_id_type=MESH)
    for other in (below, above):
        pl.semaphore_signal(barrier, inc=1, device_id={"batch": other}, device_id_type=MESH)
    pl.semaphore_wait(barrier, bits + 2)

    def digits(r):
        return tuple((r // 2**i) % 2 for i in reversed(range(n)))

    def window(r, core, zz, p):
        owner = zz * 2**bits + 2 * r + core
        return pl.ds((owner * span) // ROW + p * 2 * half, 2 * half)

    def core_copies(p, own_too=True):
        remote, own = [], []
        for r in range(2**n):
            for zz in range(depth):
                at_slot = (p,) + digits(r) + (zz,)
                spot = (p * 2**n + r) * depth + zz
                remote.append(
                    pltpu.make_async_remote_copy(
                        src_ref=flat_ref.at[window(r, 1 - mine[0], zz, p)],
                        dst_ref=first_recv.at[at_slot],
                        send_sem=core_send.at[spot],
                        recv_sem=core_recv.at[spot],
                        device_id={"blk": partner[0]},
                        device_id_type=MESH,
                    )
                )
                if own_too:
                    own.append(
                        pltpu.make_async_copy(
                            flat_ref.at[window(r, mine[0], zz, p)], acc.at[at_slot], local_sem.at[spot]
                        )
                    )
        return remote, own

    def order(part):
        return list(range(n)) if part == 0 else list(reversed(range(n)))

    def place(p, part, done, pick):
        spots = [slice(None)] * n
        for i in order(part)[:done]:
            spots[i] = mine[i + 1]
        if pick is not None:
            spots[order(part)[done]] = pick
        return (p,) + tuple(reversed(spots)) + (slice(None), slice(part * half, (part + 1) * half))

    def bit_copies(p, s):
        copies = []
        for part in range(2):
            i = order(part)[s]
            spot = (p * n + s) * 2 + part
            copies.append(
                pltpu.make_async_remote_copy(
                    src_ref=acc.at[place(p, part, s, 1 - mine[i + 1])],
                    dst_ref=bit_recvs[s].at[p, part],
                    send_sem=bit_send.at[spot],
                    recv_sem=bit_recv.at[spot],
                    device_id={"blk": partner[i + 1]},
                    device_id_type=MESH,
                )
            )
        return copies

    settled = tuple(reversed([mine[i + 1] for i in range(n)]))

    def z_moves(p, u):
        down = u - (depth - 1 - z)
        up = depth - 1 - (u - z)
        spot = (p * (depth - 1) + u) * 2
        return (
            (
                (down >= 0) & (down < z),
                lax.max(down, 0),
                z < depth - 1,
                down_recv,
                below,
                spot,
            ),
            (
                (u >= z) & (up > z),
                lax.min(up, depth - 1),
                z > 0,
                up_recv,
                above,
                spot + 1,
            ),
        )

    def z_copy(p, goal, recv, to, spot):
        return pltpu.make_async_remote_copy(
            src_ref=acc.at[(p,) + settled + (goal,)],
            dst_ref=recv.at[p, goal],
            send_sem=z_send.at[spot],
            recv_sem=z_recv.at[0 if recv is down_recv else 1, p, goal],
            device_id={"batch": to},
            device_id_type=MESH,
        )

    def z_wait(p, goal, recv):
        z_copy(p, goal, recv, below if recv is down_recv else above, 0).wait_recv()

    def add_windows(p):
        remote, own = core_copies(p)
        for copy in own:
            copy.wait()
        for copy in remote:
            copy.wait_recv()
        for r in range(2**n):

            def one(zz, carry):
                at_slot = (p,) + digits(r) + (zz,)
                acc[at_slot] += first_recv[at_slot]
                return carry

            lax.fori_loop(0, depth, one, 0)

    def add_bits(p, s):
        for part, copy in enumerate(bit_copies(p, s)):
            copy.wait_recv()
            kept = place(p, part, s, mine[order(part)[s] + 1])
            free = [i for i, v in enumerate(kept[1 : 1 + n]) if isinstance(v, slice)]
            for r in range(2 ** len(free)):
                chosen = [(r // 2**j) % 2 for j in reversed(range(len(free)))]
                to = list(kept)
                for i, v in zip(free, chosen):
                    to[1 + i] = v

                def one(zz, carry):
                    dst = tuple(to[: 1 + n]) + (zz, to[-1])
                    acc[dst] += bit_recvs[s][(p, part) + tuple(chosen) + (zz,)]
                    return carry

                lax.fori_loop(0, depth, one, 0)

    last = n + depth - 1
    for t in range(phases + last + 1):
        for stage in reversed(range(last + 1)):
            p = t - stage
            if not 0 <= p < phases:
                continue
            if stage == 0:
                remote, own = core_copies(p)
                for copy in remote + own:
                    copy.start()
            elif stage <= n:
                if stage == 1:
                    add_windows(p)
                else:
                    add_bits(p, stage - 2)
                for copy in bit_copies(p, stage - 1):
                    copy.start()
            else:
                u = stage - n - 1
                if u == 0:
                    if n == 0:
                        add_windows(p)
                    else:
                        add_bits(p, n - 1)
                for cond, goal, relays, recv, to, spot in z_moves(p, u):

                    @pl.when(cond)
                    def _():
                        @pl.when(relays)
                        def _():
                            z_wait(p, goal, recv)
                            acc[(p,) + settled + (goal,)] += recv[p, goal]

                        z_copy(p, goal, recv, to, spot).start()

    square_ref[...] = jnp.zeros_like(square_ref)
    index = blk + z * 2**bits
    low = (index * span) % ROW
    inside = lax.broadcasted_iota(jnp.int32, (SUB, LANE), 0) * LANE + lax.broadcasted_iota(
        jnp.int32, (SUB, LANE), 1
    )
    for p in range(phases):
        for recv, here in ((down_recv, z < depth - 1), (up_recv, z > 0)):

            @pl.when(here)
            def _():
                z_wait(p, z, recv)
                acc[(p,) + settled + (z,)] += recv[p, z]

        def one(i, carry):
            value = acc[(p,) + settled + (z, i)]
            out_ref[p * 2 * half + i] = value
            spot = inside + (p * 2 * half + i) * ROW
            held = jnp.where((spot >= low) & (spot < low + span), value, 0.0)
            square_ref[...] += held * held
            return carry

        lax.fori_loop(0, 2 * half, one, 0)

    sums[0] = square_ref[...]
    for b in range(bits):
        copy = pltpu.make_async_remote_copy(
            src_ref=sums.at[b],
            dst_ref=sums.at[bits + 1 + b],
            send_sem=ring_send.at[b],
            recv_sem=ring_recv.at[b],
            device_id={"blk": partner[b]},
            device_id_type=MESH,
        )
        copy.start()
        copy.wait()
        sums[b + 1] = sums[b] + sums[bits + 1 + b]
    ring[z] = sums[bits]
    for u in range(depth - 1):
        moves = (
            ((z + u < depth) & (z > 0), lax.min(z + u, depth - 1), below, 0, (z < depth - 1) & (z + 1 + u < depth), lax.min(z + 1 + u, depth - 1)),
            ((z - u >= 0) & (z < depth - 1), lax.max(z - u, 0), above, 1, (z > 0) & (z - 1 - u >= 0), lax.max(z - 1 - u, 0)),
        )

        def hop(origin, to, way):
            return pltpu.make_async_remote_copy(
                src_ref=ring.at[origin],
                dst_ref=ring.at[origin],
                send_sem=ring_send.at[bits + u * 2 + way],
                recv_sem=ring_recv.at[bits + u * 2 + way],
                device_id={"batch": to},
                device_id_type=MESH,
            )

        for cond, origin, to, way, gets, source in moves:

            @pl.when(cond)
            def _():
                hop(origin, to, way).start()

        for cond, origin, to, way, gets, source in moves:

            @pl.when(gets)
            def _():
                hop(source, to, way).wait_recv()

            @pl.when(cond)
            def _():
                hop(origin, to, way).wait_send()

    total = ring[0]
    for zz in range(1, depth):
        total = total + ring[zz]
    norm_ref[...] = jnp.broadcast_to(jnp.sqrt(jnp.sum(total, keepdims=True)), (SUB, LANE))

    for p in range(phases):
        for copy in core_copies(p, False)[0]:
            copy.wait_send()
        for s in range(n):
            for copy in bit_copies(p, s):
                copy.wait_send()
        for u in range(depth - 1):
            for cond, goal, relays, recv, to, spot in z_moves(p, u):

                @pl.when(cond)
                def _():
                    z_copy(p, goal, recv, to, spot).wait_send()


def window_tiles(span, phases):
    need = (span - 1) // ROW + 2
    return -(-need // (2 * phases)) * 2 * phases


def reduce_call(flat, span, phases):
    depth, count = lax.axis_size("batch"), lax.axis_size("blk")
    bits = count.bit_length() - 1
    n = bits - 1
    half = window_tiles(span, phases) // (2 * phases)
    tile = (SUB, LANE)
    dma = pltpu.SemaphoreType.DMA
    spots = phases * 2**n * depth
    return pl.pallas_call(
        functools.partial(reduce_kernel, depth, bits, phases, half, span),
        name="reduce_gradients",
        in_specs=[pl.BlockSpec(memory_space=pl.ANY)],
        out_specs=[pl.BlockSpec(memory_space=pltpu.VMEM)] * 2,
        out_shape=[
            jax.ShapeDtypeStruct((phases * 2 * half,) + tile, f32),
            jax.ShapeDtypeStruct(tile, f32),
        ],
        scratch_shapes=[
            pltpu.VMEM((phases,) + (2,) * n + (depth, 2 * half) + tile, f32),
            pltpu.VMEM((phases,) + (2,) * n + (depth, 2 * half) + tile, f32),
        ]
        + [pltpu.VMEM((phases, 2) + (2,) * (n - 1 - s) + (depth, half) + tile, f32) for s in range(n)]
        + [pltpu.VMEM((phases, depth, 2 * half) + tile, f32)] * 2
        + [
            pltpu.VMEM((depth,) + tile, f32),
            pltpu.VMEM((2 * bits + 1,) + tile, f32),
            pltpu.VMEM(tile, f32),
            dma((spots,)),
            dma((spots,)),
            dma((spots,)),
            dma((phases * n * 2,)),
            dma((phases * n * 2,)),
            dma((phases * (depth - 1) * 2,)),
            dma((2, phases, depth)),
            dma((bits + 2 * (depth - 1),)),
            dma((bits + 2 * (depth - 1),)),
        ],
        compiler_params=pltpu.CompilerParams(
            vmem_limit_bytes=VMEM_BYTES, collective_id=1, has_side_effects=True
        ),
    )(flat)


def owned_params(params, counts, base, high):
    norm_gain, in_weight, out_weight = params[0], params[1], params[-1]
    per = in_weight.shape[1] // ROW
    small = jnp.concatenate([v.reshape(-1, ROW).astype(f32) for v in params[2:-1]], 0)
    starts = [0, norm_gain.size // ROW]
    starts.append(starts[1] + in_weight.size // ROW)
    starts.append(starts[2] + small.shape[0])
    rows = min(high // per + 2, in_weight.shape[0])
    first = jnp.clip((base - starts[1]) // per, 0, in_weight.shape[0] - rows)
    in_part = lax.dynamic_slice_in_dim(in_weight, first, rows).astype(f32).reshape(rows * per, ROW)
    deep = min(high, out_weight.shape[0])
    begin = jnp.clip(base - starts[3], 0, out_weight.shape[0] - deep)
    out_part = lax.dynamic_slice_in_dim(out_weight, begin, deep).astype(f32)
    place = base + lax.iota(jnp.int32, high)[:, None]
    total = jnp.broadcast_to(norm_gain.reshape(1, -1), (high, ROW))
    for part, origin, low in (
        (in_part, starts[1] + first * per, starts[1]),
        (small, starts[2], starts[2]),
        (out_part, starts[3] + begin, starts[3]),
    ):
        padded = jnp.pad(part, ((high, high), (0, 0)))
        offset = jnp.clip(base - origin + high, 0, part.shape[0] + high)
        total = jnp.where(place >= low, lax.dynamic_slice_in_dim(padded, offset, high), total)
    return total


def exchange(totals, state):
    count = lax.axis_size("blk")
    index = lax.axis_index("blk")
    decay, end, leave = totals[:state], totals[state : 2 * state], totals[2 * state :]
    pre_decay, pre_state = jnp.ones_like(decay), jnp.zeros_like(end)
    post_decay, post_state = jnp.ones_like(decay), jnp.zeros_like(end)
    bit = 1
    while bit < count:
        pairs = [(i, i ^ bit) for i in range(count)]
        far = lax.ppermute(jnp.concatenate([decay, end, leave], 0), "blk", pairs)
        far_decay, far_end, far_leave = far[:state], far[state : 2 * state], far[2 * state :]
        upper = (index & bit) != 0
        pre_state = jnp.where(upper, pre_state + pre_decay * far_end, pre_state)
        pre_decay = jnp.where(upper, pre_decay * far_decay, pre_decay)
        post_state = jnp.where(upper, post_state, post_state + post_decay * far_leave)
        post_decay = jnp.where(upper, post_decay, post_decay * far_decay)
        end = jnp.where(upper, end + decay * far_end, far_end + far_decay * end)
        leave = jnp.where(upper, far_leave + far_decay * leave, leave + decay * far_leave)
        decay = decay * far_decay
        bit *= 2
    return pre_state, post_state


def local(
    tokens,
    out_cot,
    norm_gain,
    in_weight,
    conv_weight,
    conv_bias,
    xproj_weight,
    dt_weight,
    dt_bias,
    a_log,
    d_skip,
    out_weight,
    moment_one,
    moment_two,
):
    contract = (((0,), (0,)), ((), ()))
    backward = (((1,), (1,)), ((), ()))
    token_rows = interleave(tokens[0])
    cot_low = interleave(out_cot[0])
    source = token_rows.astype(f32)
    length = source.shape[0]
    inner = dt_bias.shape[0]
    state = a_log.shape[0]
    rank = dt_weight.shape[0]
    width = conv_weight.shape[0]
    halo = (width - 1) * SUB
    scale = lax.rsqrt(jnp.mean(source * source, axis=-1, keepdims=True) + EPS)
    normed = (source * scale * norm_gain).astype(bf16)
    stream = jnp.dot(normed, in_weight[:, :inner], preferred_element_type=f32)
    ends = stream[length - halo :].reshape(width - 1, SUB, inner)
    tail = shifted(ends[:, SUB - 1], "blk", 1)
    gating = jnp.dot(normed, in_weight[:, inner:], preferred_element_type=f32)
    grad_gated = lax.dot_general(cot_low, out_weight, backward, preferred_element_type=f32)
    head = jnp.concatenate([tail[:, None], ends[:, : SUB - 1]], 1).reshape(halo, inner)
    longer = jnp.concatenate([head, stream], 0)

    def delayed(lag):
        return longer[halo - lag * SUB : halo - lag * SUB + length]

    conv_sum = conv_bias + conv_weight[width - 1] * stream
    for offset in range(width - 1):
        conv_sum = conv_sum + conv_weight[offset] * delayed(width - 1 - offset)
    conv_low = (conv_sum * jax.nn.sigmoid(conv_sum)).astype(bf16)
    conv_val = conv_low.astype(f32)
    selectors = jnp.dot(conv_low, xproj_weight, preferred_element_type=f32)
    step_low = selectors[:, :rank].astype(bf16)
    terms, spots = split_selectors(selectors[:, rank:])
    step_pre = jnp.dot(step_low, dt_weight, preferred_element_type=f32) + dt_bias
    step_size = jax.nn.softplus(step_pre)
    drive = step_size * conv_val
    gate_sig = jax.nn.sigmoid(gating)
    gate_val = gating * gate_sig
    grad_scanned = grad_gated * gate_val
    rates = -jnp.exp(a_log)
    rates_wide = jnp.repeat(rates * LOG2E, SUB, axis=0)

    pre_decay, pre_state, post_decay, post_state, totals = summary_call(
        step_size, drive, grad_scanned, terms, spots, rates_wide
    )
    entry, arriving = exchange(totals, state)
    prior, readout_grads, gated, grad_gating, skip_grads = forward_call(
        step_size,
        drive,
        grad_scanned,
        terms,
        spots,
        rates_wide,
        pre_decay,
        pre_state,
        entry,
        conv_low,
        gating,
        grad_gated,
        d_skip[None],
    )
    output = jnp.dot(gated, out_weight, preferred_element_type=f32)
    result = restore((source + output).astype(bf16))[None]
    grad_out_weight = lax.dot_general(gated, cot_low, contract, preferred_element_type=f32)
    grad_in_gate = lax.dot_general(normed, grad_gating, contract, preferred_element_type=f32)
    grad_d_skip = jnp.sum(skip_grads, 0)

    spare = LANE - rank - 2 * state
    step_back = jnp.pad(dt_weight, ((2 * state, spare), (0, 0))).T
    select_back = jnp.pad(jnp.roll(xproj_weight, 2 * state, 1), ((0, 0), (0, spare))).T
    grad_stream_low, grad_pre_low, grad_selectors, rate_grads, taps_grads, edges = backward_call(
        step_size,
        drive,
        grad_scanned,
        terms,
        spots,
        rates_wide,
        post_decay,
        post_state,
        arriving,
        prior,
        conv_sum,
        stream,
        readout_grads,
        step_back,
        select_back,
        conv_weight,
        d_skip[None],
    )
    grad_a_log = LN2 * jnp.sum(rate_grads.reshape(state, SUB, inner), 1)
    begins = edges[:halo].reshape(width - 1, SUB, inner)
    ahead = shifted(begins[:, 0], "blk", -1)
    grad_dt_weight = lax.dot_general(step_low, grad_pre_low, contract, preferred_element_type=f32)
    grad_xproj = lax.dot_general(conv_low, grad_selectors, contract, preferred_element_type=f32)
    grad_xproj = jnp.roll(grad_xproj[:, : rank + 2 * state], rank, 1)
    foot = jnp.concatenate([begins[:, 1:], ahead[:, None]], 1)
    lasts = edges[halo:].reshape(width - 1, SUB, inner)
    further = jnp.concatenate([lasts, foot], 0)
    last_stream = stream[length - halo :].reshape(width - 1, SUB, inner)
    grad_last = conv_weight[width - 1] * lasts
    taps_grads = jnp.sum(taps_grads.reshape(width + 2, SUB, inner), 1)
    tap_grads = []
    for offset in range(width - 1):
        lead = width - 1 - offset
        grad_last = grad_last + conv_weight[offset] * further[lead : lead + width - 1]
        over = jnp.sum(last_stream[width - 1 - lead :] * foot[:lead], (0, 1))
        tap_grads.append(taps_grads[offset] + over)
    tap_grads.append(taps_grads[width - 1])
    grad_conv_weight = jnp.stack(tap_grads, 0)
    grad_conv_bias = taps_grads[width]
    grad_dt_bias = taps_grads[width + 1]
    grad_stream_low = lax.dynamic_update_slice_in_dim(
        grad_stream_low, grad_last.reshape(halo, inner).astype(bf16), length - halo, 0
    )
    grad_in_stream = lax.dot_general(normed, grad_stream_low, contract, preferred_element_type=f32)
    grad_normed = lax.dot_general(
        jnp.concatenate([grad_stream_low, grad_gating], 1), in_weight, backward, preferred_element_type=f32
    )
    grad_gain = jnp.sum(grad_normed * source * scale, 0)
    weighted = grad_normed * norm_gain
    grad_source = (
        scale * weighted
        - source * scale**3 * jnp.mean(weighted * source, axis=-1, keepdims=True)
        + cot_low.astype(f32)
    )
    grad_tokens = restore(grad_source.astype(bf16))[None]
    span = moment_one.shape[0]
    small = jnp.concatenate(
        [
            value.reshape(-1, ROW)
            for value in (
                grad_conv_weight,
                grad_conv_bias,
                grad_xproj,
                grad_dt_weight,
                grad_dt_bias,
                grad_a_log,
                grad_d_skip,
            )
        ],
        0,
    ).reshape(-1, SUB, LANE)
    params = (
        norm_gain,
        in_weight,
        conv_weight,
        conv_bias,
        xproj_weight,
        dt_weight,
        dt_bias,
        a_log,
        d_skip,
        out_weight,
    )
    counts = [value.size for value in params]
    lower = sum(counts[:6])
    upper = sum(counts[:9])
    phases = 4 if span >= 16 * ROW * 4 else 1
    high = window_tiles(span, phases)
    flat = flatten_call(
        grad_in_stream, grad_in_gate, grad_out_weight, grad_gain.reshape(1, SUB, LANE), small, sum(counts) // ROW + high
    )
    reduced, norm = reduce_call(flat, span, phases)
    grad_norm = norm[0, 0]
    begin = lax.axis_index(("batch", "blk")) * span
    shard = lax.dynamic_slice_in_dim(reduced.reshape(-1), begin % ROW, span)
    owned = owned_params(params, counts, begin // ROW, high)
    owned = lax.dynamic_slice_in_dim(owned.reshape(-1), begin % ROW, span)
    place = begin + lax.iota(jnp.int32, span)
    keep = jnp.where((place >= lower) & (place < upper), 0.0, 1.0).astype(f32)
    clipped = shard * jnp.minimum(1.0, CLIP / (grad_norm + 1e-06))
    new_one = BETA_ONE * moment_one + (1.0 - BETA_ONE) * clipped
    new_two = BETA_TWO * moment_two + (1.0 - BETA_TWO) * clipped * clipped
    first = new_one / (1.0 - BETA_ONE**ADAM_STEP)
    second = new_two / (1.0 - BETA_TWO**ADAM_STEP)
    param_step = -RATE * (first / (jnp.sqrt(second) + ADAM_EPS) + DECAY * keep * owned)
    return (result, grad_tokens, shard, grad_norm, param_step, new_one, new_two)


def solution(mesh):
    return jax.shard_map(
        local,
        mesh=mesh,
        in_specs=(P("batch", "blk", None),) * 2 + (P(),) * 10 + (P(("batch", "blk")),) * 2,
        out_specs=(P("batch", "blk", None),) * 2
        + (P(("batch", "blk")), P(), P(("batch", "blk")), P(("batch", "blk")), P(("batch", "blk"))),
        check_vma=False,
    )
```

```python
import functools
import math

import jax
import jax.numpy as jnp
from jax import lax
from jax.experimental import pallas as pl
from jax.experimental.pallas import tpu as pltpu
from jax.sharding import PartitionSpec as P

ADAM_STEP = 100
EPS = 1e-05
RATE = 0.002
BETA_ONE = 0.9
BETA_TWO = 0.95
ADAM_EPS = 1e-08
DECAY = 0.1
CLIP = 1.0

LOG2E = 1.0 / math.log(2.0)
LN2 = math.log(2.0)
SUB = 8
LANE = 128
ROW = 1024
VMEM_BYTES = 56 * 2**20

MESH = pl.DeviceIdType.MESH

f32 = jnp.float32
bf16 = jnp.bfloat16


def shifted(x, axis, by):
    count = lax.axis_size(axis)
    pairs = [(i, i + by) for i in range(count) if 0 <= i + by < count]
    return lax.ppermute(x, axis, pairs)


def silu_slope(value):
    sig = jax.nn.sigmoid(value)
    return sig * (1.0 + value * (1.0 - sig))


def interleave(x):
    rows, width = x.shape
    return x.reshape(SUB, rows // SUB, width).transpose(1, 0, 2).reshape(rows, width)


def restore(x):
    rows, width = x.shape
    return x.reshape(rows // SUB, SUB, width).transpose(1, 0, 2).reshape(rows, width)


def at(start, size):
    return pl.ds(pl.multiple_of(start, size), size)


def spread(sel_ref, spots_ref, out_ref):
    out_ref[...] = jnp.dot(sel_ref[...], spots_ref[...], preferred_element_type=f32)


def gather_lanes(src_ref, spots_ref, out_ref):
    value = src_ref[...]
    high = value.astype(bf16)
    low = (value - high.astype(f32)).astype(bf16)
    spots = spots_ref[0:LANE, 0 : value.shape[1]]
    back = (((1,), (1,)), ((), ()))
    out_ref[...] = lax.dot_general(high, spots, back, preferred_element_type=f32) + lax.dot_general(
        low, spots, back, preferred_element_type=f32
    )


def spread_table(count):
    row = lax.broadcasted_iota(jnp.int32, (LANE, count * LANE), 0)
    col = lax.broadcasted_iota(jnp.int32, (LANE, count * LANE), 1) // LANE
    return ((row % count == col) & (row < 3 * count)).astype(bf16)


def summary_kernel(
    shape,
    stream_ref,
    gating_ref,
    grad_gated_ref,
    head_ref,
    taps_ref,
    bias_ref,
    select_in_ref,
    step_in_ref,
    step_bias_ref,
    spots_ref,
    rates_ref,
    conv_sum_ref,
    conv_ref,
    step_ref,
    drive_ref,
    grad_ref,
    low_ref,
    sel_ref,
    pre_decay_ref,
    pre_state_ref,
    post_decay_ref,
    post_state_ref,
    totals_ref,
    end_ref,
    exit_ref,
    prod_ref,
    select_ref,
    longer_ref,
):
    tiles, state, inner, cols, group = shape
    turn = pl.program_id(0)
    block = tiles * SUB
    width = taps_ref.shape[0]
    halo = (width - 1) * SUB

    @pl.when(turn == 0)
    def _():
        end_ref[...] = jnp.zeros_like(end_ref)
        exit_ref[...] = jnp.zeros_like(exit_ref)
        prod_ref[...] = jnp.ones_like(prod_ref)
        longer_ref[:halo, :] = head_ref[...]

    @pl.when(turn > 0)
    def _():
        longer_ref[:halo, :] = longer_ref[block:, :]

    longer_ref[halo:, :] = stream_ref[...]

    def convs(c, carry):
        lanes = at(c * 2 * LANE, 2 * LANE)
        taps = [jnp.broadcast_to(taps_ref[k : k + 1, lanes], (2 * SUB, 2 * LANE)) for k in range(width)]
        bias = bias_ref[:, lanes]

        def pair(i, carry):
            here = at(i * 2 * SUB, 2 * SUB)
            total = bias + taps[width - 1] * stream_ref[here, lanes]
            for k in range(width - 1):
                total = total + taps[k] * longer_ref[pl.ds(pl.multiple_of((2 * i + k) * SUB, SUB), 2 * SUB), lanes]
            conv_sum_ref[here, lanes] = total
            conv_ref[here, lanes] = (total * jax.nn.sigmoid(total)).astype(bf16)
            gating = gating_ref[here, lanes]
            grad_ref[here, lanes] = grad_gated_ref[here, lanes] * (gating * jax.nn.sigmoid(gating))
            return carry

        lax.fori_loop(0, tiles // 2, pair, 0, unroll=4)
        return carry

    lax.fori_loop(0, inner // (2 * LANE), convs, 0)
    lane = lax.broadcasted_iota(jnp.int32, (block, LANE), 1)
    selectors = jnp.dot(conv_ref[...], select_in_ref[...], preferred_element_type=f32)
    low = selectors.astype(bf16)
    low_ref[...] = low
    value = jnp.where(lane < 2 * state, selectors, 0.0)
    high = value.astype(bf16).astype(f32)
    middle = (value - high).astype(bf16).astype(f32)
    rest = value - high - middle
    sel_ref[...] = (high + pltpu.roll(middle, 2 * state, 1) + pltpu.roll(rest, 4 * state, 1)).astype(bf16)

    def steps(c, carry):
        lanes = at(c * 2 * LANE, 2 * LANE)
        bias = step_bias_ref[:, lanes]
        step_ref[:, lanes] = jnp.dot(low, step_in_ref[:, lanes], preferred_element_type=f32)

        def pair(i, carry):
            here = at(i * 2 * SUB, 2 * SUB)
            pre = step_ref[here, lanes] + bias
            step = jnp.maximum(pre, 0.0) + jnp.log1p(jnp.exp(-jnp.abs(pre)))
            step_ref[here, lanes] = step
            drive_ref[here, lanes] = step * conv_ref[here, lanes].astype(f32)
            return carry

        lax.fori_loop(0, tiles // 2, pair, 0, unroll=4)
        return carry

    lax.fori_loop(0, inner // (2 * LANE), steps, 0)
    spread(sel_ref, spots_ref, select_ref)

    def columns(c, carry):
        lanes = [at((c * cols + k) * LANE, LANE) for k in range(cols)]
        for first in range(0, state, group):
            spots = [(n, k) for n in range(group) for k in range(cols)]
            where = [(slice((first + n) * SUB, (first + n + 1) * SUB), lanes[k]) for n, k in spots]
            rates = [rates_ref[w] for w in where]

            def advance(i, carry):
                ends, exits, prods = carry
                here = at(i * SUB, SUB)
                step = [step_ref[here, l] for l in lanes]
                drive = [drive_ref[here, l] for l in lanes]
                grad = [grad_ref[here, l] for l in lanes]
                inject = [select_ref[here, (first + n) * LANE : (first + n + 1) * LANE] for n in range(group)]
                readout = [
                    select_ref[here, (state + first + n) * LANE : (state + first + n + 1) * LANE] for n in range(group)
                ]
                new = ([], [], [])
                for s, (n, k) in enumerate(spots):
                    decay = jnp.exp2(step[k] * rates[s])
                    prod = prods[s] * decay
                    new[0].append(ends[s] * decay + drive[k] * inject[n])
                    new[1].append(exits[s] + prod * (grad[k] * readout[n]))
                    new[2].append(prod)
                return tuple(tuple(x) for x in new)

            start = tuple(tuple(ref[w] for w in where) for ref in (end_ref, exit_ref, prod_ref))
            ends, exits, prods = lax.fori_loop(0, tiles, advance, start, unroll=16)
            for s, w in enumerate(where):
                end_ref[w] = ends[s]
                exit_ref[w] = exits[s]
                prod_ref[w] = prods[s]
        return carry

    lax.fori_loop(0, inner // (LANE * cols), columns, 0)

    @pl.when(turn == pl.num_programs(0) - 1)
    def _():
        row = lax.broadcasted_iota(jnp.int32, (SUB, LANE), 0)

        def columns(c, carry):
            lanes = at(c * LANE, LANE)
            for n in range(state):
                here = (slice(n * SUB, (n + 1) * SUB), lanes)
                for way, src, decay_out, state_out, total_row in (
                    (1, end_ref, pre_decay_ref, pre_state_ref, 1),
                    (-1, exit_ref, post_decay_ref, post_state_ref, 2),
                ):
                    decay, value = prod_ref[here], src[here]

                    def seen(by):
                        return row >= by if way > 0 else row < SUB - by

                    for by in (1, 2, 4):
                        far_decay = pltpu.roll(decay, by if way > 0 else SUB - by, 0)
                        far_value = pltpu.roll(value, by if way > 0 else SUB - by, 0)
                        value = jnp.where(seen(by), value + decay * far_value, value)
                        decay = jnp.where(seen(by), decay * far_decay, decay)
                    last = SUB - 1 if way > 0 else 0
                    totals_ref[pl.ds(n, 1), lanes] = decay[last : last + 1]
                    totals_ref[pl.ds(total_row * state + n, 1), lanes] = value[last : last + 1]
                    turn_by = 1 if way > 0 else SUB - 1
                    decay_out[here] = jnp.where(seen(1), pltpu.roll(decay, turn_by, 0), 1.0)
                    state_out[here] = jnp.where(seen(1), pltpu.roll(value, turn_by, 0), 0.0)
            return carry

        lax.fori_loop(0, inner // LANE, columns, 0)


def forward_kernel(
    shape,
    step_ref,
    drive_ref,
    grad_ref,
    sel_ref,
    spots_ref,
    rates_ref,
    pre_decay_ref,
    pre_state_ref,
    entry_ref,
    conv_ref,
    gating_ref,
    grad_gated_ref,
    skip_ref,
    prior_ref,
    readout_grad_ref,
    gated_ref,
    grad_gating_ref,
    skip_grad_ref,
    state_ref,
    select_ref,
    sums_ref,
    scanned_ref,
):
    tiles, state, inner, cols, group = shape

    @pl.when(pl.program_id(0) == 0)
    def _():
        skip_grad_ref[...] = jnp.zeros_like(skip_grad_ref)
        for n in range(state):
            here = slice(n * SUB, (n + 1) * SUB)
            state_ref[here, :] = pre_state_ref[here, :] + pre_decay_ref[here, :] * entry_ref[n : n + 1, :]

    spread(sel_ref, spots_ref, select_ref)
    sums_ref[...] = jnp.zeros_like(sums_ref)

    def columns(c, carry):
        lanes = [at((c * cols + k) * LANE, LANE) for k in range(cols)]
        for first in range(0, state, group):
            spots = [(n, k) for n in range(group) for k in range(cols)]
            where = [(slice((first + n) * SUB, (first + n + 1) * SUB), lanes[k]) for n, k in spots]
            rates = [rates_ref[w] for w in where]

            def advance(i, states):
                here = at(i * SUB, SUB)
                step = [step_ref[here, l] for l in lanes]
                drive = [drive_ref[here, l] for l in lanes]
                grad = [grad_ref[here, l] for l in lanes]
                outs = [None] * cols
                new = []
                for n in range(group):
                    spot = slice((first + n) * LANE, (first + n + 1) * LANE)
                    inject = select_ref[here, spot]
                    readout = select_ref[here, (state + first + n) * LANE : (state + first + n + 1) * LANE]
                    total = None
                    for k in range(cols):
                        s = n * cols + k
                        decay = jnp.exp2(step[k] * rates[s])
                        fresh = decay * states[s] + drive[k] * inject
                        new.append(fresh)
                        part = readout * fresh
                        outs[k] = part if outs[k] is None else outs[k] + part
                        part = grad[k] * fresh
                        total = part if total is None else total + part
                    sums_ref[here, spot] += total
                    if n % 2 == 1:
                        pair = pl.ds(pl.multiple_of((i * state + first + n - 1) * SUB, 2 * SUB), 2 * SUB)
                        for k in range(cols):
                            prior_ref[pair, lanes[k]] = jnp.concatenate(
                                [states[(n - 1) * cols + k], states[n * cols + k]], 0
                            ).astype(bf16)
                for k in range(cols):
                    if first == 0:
                        scanned_ref[here, lanes[k]] = outs[k]
                    else:
                        scanned_ref[here, lanes[k]] += outs[k]
                return tuple(new)

            states = lax.fori_loop(0, tiles, advance, tuple(state_ref[w] for w in where), unroll=16)
            for s, w in enumerate(where):
                state_ref[w] = states[s]
        return carry

    lax.fori_loop(0, inner // (LANE * cols), columns, 0)
    gather_lanes(sums_ref, spots_ref, readout_grad_ref)

    def finish(c, carry):
        lanes = at(c * 2 * LANE, 2 * LANE)
        skip = skip_ref[:, lanes]

        def pair(i, total):
            here = at(i * 2 * SUB, 2 * SUB)
            conv = conv_ref[here, lanes].astype(f32)
            gating = gating_ref[here, lanes]
            sig = jax.nn.sigmoid(gating)
            gate = gating * sig
            scanned = scanned_ref[here, lanes] + skip * conv
            gated_ref[here, lanes] = (scanned * gate).astype(bf16)
            slope = sig + gate * (1.0 - sig)
            grad_gating_ref[here, lanes] = (grad_gated_ref[here, lanes] * scanned * slope).astype(bf16)
            product = grad_ref[here, lanes] * conv
            return total + product[:SUB] + product[SUB:]

        zero = jnp.zeros((SUB, 2 * LANE), f32)
        skip_grad_ref[:, lanes] += lax.fori_loop(0, tiles // 2, pair, zero, unroll=4)
        return carry

    lax.fori_loop(0, inner // (2 * LANE), finish, 0)


def backward_kernel(
    shape,
    scan_turns,
    regions,
    bits,
    phases,
    stride,
    step_ref,
    drive_ref,
    grad_ref,
    sel_ref,
    spots_ref,
    rates_ref,
    begin_ref,
    prior_ref,
    conv_sum_ref,
    stream_ref,
    readout_grad_ref,
    step_back_ref,
    select_back_ref,
    taps_ref,
    skip_ref,
    flat_ref,
    grad_stream_ref,
    grad_pre_ref,
    grad_select_ref,
    rate_grad_ref,
    taps_grad_ref,
    edge_ref,
    early_ref,
    carry_ref,
    select_ref,
    sums_ref,
    through_ref,
    feed_ref,
    grad_conv_ref,
    inject_grad_ref,
    *refs,
):
    tiles, state, inner, cols, group = shape
    block = tiles * SUB
    width = taps_ref.shape[0]
    halo = (width - 1) * SUB
    turn = pl.program_id(0)
    work = Reducer(regions.depth, bits, phases, stride, regions.early_start, flat_ref, refs)
    turns = scan_turns
    early = max(work.slots - turns, 0)
    for g in range(turns):

        @pl.when(turn == g)
        def _():
            if g == 0:
                work.greet()
            for t in range(0 if g == 0 else g + early, min(g + early + 1, work.slots)):
                work.run(t)

    @pl.when(pl.program_id(0) == 0)
    def _():
        rate_grad_ref[...] = jnp.zeros_like(rate_grad_ref)
        taps_grad_ref[...] = jnp.zeros_like(taps_grad_ref)
        grad_conv_ref[tiles * SUB :, :] = jnp.zeros((grad_conv_ref.shape[0] - tiles * SUB, inner), f32)
        carry_ref[...] = begin_ref[...]

    spread(sel_ref, spots_ref, select_ref)
    sums_ref[...] = jnp.zeros_like(sums_ref)

    def columns(c, carry):
        lanes = [at((c * cols + k) * LANE, LANE) for k in range(cols)]
        for first in range(0, state, group):
            spots = [(n, k) for n in range(group) for k in range(cols)]
            where = [(slice((first + n) * SUB, (first + n + 1) * SUB), lanes[k]) for n, k in spots]
            rates = [rates_ref[w] for w in where]

            def retreat(turn, carry):
                carries, rate_grads = carry
                i = tiles - 1 - turn
                here = at(i * SUB, SUB)
                step = [step_ref[here, l] for l in lanes]
                drive = [drive_ref[here, l] for l in lanes]
                grad = [grad_ref[here, l] for l in lanes]
                throughs = [None] * cols
                feeds = [None] * cols
                new = ([], [])
                for n in range(group):
                    spot = slice((first + n) * LANE, (first + n + 1) * LANE)
                    inject = select_ref[here, spot]
                    readout = select_ref[here, (state + first + n) * LANE : (state + first + n + 1) * LANE]
                    if n % 2 == 0:
                        pair = pl.ds(pl.multiple_of((i * state + first + n) * SUB, 2 * SUB), 2 * SUB)
                        pairs = [prior_ref[pair, lanes[k]].astype(f32) for k in range(cols)]
                    total = None
                    for k in range(cols):
                        s = n * cols + k
                        prior = pairs[k][(n % 2) * SUB : (n % 2 + 1) * SUB]
                        power = step[k] * rates[s]
                        adjoint = grad[k] * readout + carries[s]
                        back = jnp.exp2(power) * adjoint
                        through = back * prior * power
                        new[0].append(back)
                        new[1].append(rate_grads[s] + through)
                        throughs[k] = through if throughs[k] is None else throughs[k] + through
                        part = adjoint * inject
                        feeds[k] = part if feeds[k] is None else feeds[k] + part
                        part = adjoint * drive[k]
                        total = part if total is None else total + part
                    sums_ref[here, spot] += total
                for k in range(cols):
                    if first == 0:
                        through_ref[here, lanes[k]] = throughs[k]
                        feed_ref[here, lanes[k]] = feeds[k]
                    else:
                        through_ref[here, lanes[k]] += throughs[k]
                        feed_ref[here, lanes[k]] += feeds[k]
                return tuple(tuple(x) for x in new)

            start = tuple(tuple(ref[w] for w in where) for ref in (carry_ref, rate_grad_ref))
            carries, rate_grads = lax.fori_loop(0, tiles, retreat, start, unroll=8)
            for s, w in enumerate(where):
                carry_ref[w] = carries[s]
                rate_grad_ref[w] = rate_grads[s]
        return carry

    lax.fori_loop(0, inner // (LANE * cols), columns, 0)
    gather_lanes(sums_ref, spots_ref, inject_grad_ref)

    def steps(c, carry):
        lanes = at(c * 2 * LANE, 2 * LANE)

        def pair(i, total):
            here = at(i * 2 * SUB, 2 * SUB)
            step = step_ref[here, lanes]
            series = 1.0 + step * (-1.0 / 2 + step * (1.0 / 6 + step * (-1.0 / 24 + step * (1.0 / 120))))
            near = step < 0.06
            exact = (1.0 - jnp.exp2(step * -LOG2E)) / jnp.where(near, 1.0, step)
            ratio = jnp.where(near, series, exact)
            pre = ratio * (LN2 * through_ref[here, lanes] + drive_ref[here, lanes] * feed_ref[here, lanes])
            grad_pre_ref[here, lanes] = pre.astype(bf16)
            return total + pre[:SUB] + pre[SUB:]

        zero = jnp.zeros((SUB, 2 * LANE), f32)
        taps_grad_ref[(width + 1) * SUB :, lanes] += lax.fori_loop(0, tiles // 2, pair, zero, unroll=4)
        return carry

    lax.fori_loop(0, inner // (2 * LANE), steps, 0)
    lane = lax.broadcasted_iota(jnp.int32, (block, LANE), 1)
    rank = LANE - 2 * state
    grads = jnp.dot(grad_pre_ref[...], step_back_ref[...], preferred_element_type=f32)
    grads = jnp.where(
        lane < state,
        inject_grad_ref[...],
        jnp.where(lane < 2 * state, pltpu.roll(readout_grad_ref[...], state, 1), grads),
    )
    grads = grads.astype(bf16)
    grad_select_ref[...] = grads

    def convs(c, carry):
        lanes = at(c * 2 * LANE, 2 * LANE)
        skip = skip_ref[:, lanes]
        feeds = jnp.dot(grads, select_back_ref[:, lanes], preferred_element_type=f32)
        through_ref[:, lanes] = feeds

        def conv(i, carry):
            here = at(i * SUB, SUB)
            value = conv_sum_ref[here, lanes]
            sig = jax.nn.sigmoid(value)
            slope = sig * (1.0 + value * (1.0 - sig))
            out = grad_ref[here, lanes] * skip + step_ref[here, lanes] * feed_ref[here, lanes] + through_ref[here, lanes]
            grad_conv_ref[here, lanes] = out * slope
            return carry

        lax.fori_loop(0, tiles, conv, 0, unroll=8)
        taps = [jnp.broadcast_to(taps_ref[k : k + 1, lanes], (SUB, 2 * LANE)) for k in range(width)]

        def tap(i, totals):
            totals = list(totals)
            done = []
            for q in range(2):
                parts = [
                    grad_conv_ref[pl.ds(pl.multiple_of((2 * i + q + m) * SUB, SUB), SUB), lanes] for m in range(width)
                ]
                stream = stream_ref[pl.ds(pl.multiple_of((2 * i + q) * SUB, SUB), SUB), lanes]
                grad = taps[width - 1] * parts[0]
                totals[width - 1] = totals[width - 1] + parts[0] * stream
                totals[width] = totals[width] + parts[0]
                for m in range(1, width):
                    grad = grad + taps[width - 1 - m] * parts[m]
                    totals[width - 1 - m] = totals[width - 1 - m] + parts[m] * stream
                done.append(grad)
            grad_stream_ref[at(i * 2 * SUB, 2 * SUB), lanes] = jnp.concatenate(done, 0).astype(bf16)
            return tuple(totals)

        zero = jnp.zeros((SUB, 2 * LANE), f32)
        totals = lax.fori_loop(0, tiles // 2, tap, (zero,) * (width + 1), unroll=4)
        for k in range(width + 1):
            taps_grad_ref[k * SUB : (k + 1) * SUB, lanes] += totals[k]
        return carry

    lax.fori_loop(0, inner // (2 * LANE), convs, 0)

    @pl.when(pl.program_id(0) == 0)
    def _():
        edge_ref[halo:, :] = grad_conv_ref[block - halo : block, :]

    edge_ref[:halo, :] = grad_conv_ref[:halo, :]
    grad_conv_ref[block:, :] = grad_conv_ref[:halo, :]

    @pl.when(turn == turns - 1)
    def _():
        work.collect(early_ref)


def scan_shapes(rows, state, inner, tiles=16):
    tiles = min(tiles, rows // SUB)
    count = rows // (SUB * tiles)
    return tiles, count


def summary_call(stream, gating, grad_gated, head, taps, bias, select_in, step_in, step_bias, spots, rates):
    rows, inner = stream.shape
    state = rates.shape[0] // SUB
    tiles, count = scan_shapes(rows, state, inner)
    halo = head.shape[0]
    wide = pl.BlockSpec((tiles * SUB, inner), lambda t: (t, 0))
    thin = pl.BlockSpec((tiles * SUB, LANE), lambda t: (t, 0))
    whole = pl.BlockSpec((state * SUB, inner), lambda t: (0, 0))
    total = pl.BlockSpec((3 * state, inner), lambda t: (0, 0))
    shape = (tiles, state, inner, 2, 4)
    big = jax.ShapeDtypeStruct((state * SUB, inner), f32)
    full = jax.ShapeDtypeStruct((rows, inner), f32)
    slim = jax.ShapeDtypeStruct((rows, LANE), bf16)

    def fixed(x):
        return pl.BlockSpec(x.shape, lambda t: (0, 0), pipeline_mode=pl.Buffered(1))

    constants = (head, taps, bias, select_in, step_in, step_bias, spots, rates)
    return pl.pallas_call(
        functools.partial(summary_kernel, shape),
        name="scan_summary",
        grid=(count,),
        in_specs=[wide, wide, wide] + [fixed(x) for x in constants],
        out_specs=[wide] * 5 + [thin] * 2 + [whole] * 4 + [total],
        out_shape=[full, jax.ShapeDtypeStruct((rows, inner), bf16), full, full, full, slim, slim]
        + [big] * 4
        + [jax.ShapeDtypeStruct((3 * state, inner), f32)],
        scratch_shapes=[pltpu.VMEM((state * SUB, inner), f32)] * 3
        + [
            pltpu.VMEM((tiles * SUB, 2 * state * LANE), f32),
            pltpu.VMEM((halo + tiles * SUB, inner), f32),
        ],
        compiler_params=pltpu.CompilerParams(vmem_limit_bytes=VMEM_BYTES),
    )(stream, gating, grad_gated, *constants)


def forward_call(step, drive, grad, sel, spots, rates, pre_decay, pre_state, entry, conv, gating, grad_gated, skip):
    rows, inner = step.shape
    state = rates.shape[0] // SUB
    tiles, count = scan_shapes(rows, state, inner)
    wide = pl.BlockSpec((tiles * SUB, inner), lambda t: (t, 0))
    table = pl.BlockSpec(spots.shape, lambda t: (0, 0))
    thin = pl.BlockSpec((tiles * SUB, sel.shape[1]), lambda t: (t, 0))
    whole = pl.BlockSpec((state * SUB, inner), lambda t: (0, 0), pipeline_mode=pl.Buffered(1))
    line = pl.BlockSpec((1, inner), lambda t: (0, 0))
    short = pl.BlockSpec((state, inner), lambda t: (0, 0))
    shape = (tiles, state, inner, 2, 8)
    return pl.pallas_call(
        functools.partial(forward_kernel, shape),
        name="scan_forward",
        grid=(count,),
        in_specs=[wide, wide, wide, thin, table, whole, whole, whole, short, wide, wide, wide, line],
        out_specs=[
            pl.BlockSpec((tiles * state * SUB, inner), lambda t: (t, 0)),
            pl.BlockSpec((tiles * SUB, LANE), lambda t: (t, 0)),
            wide,
            wide,
            pl.BlockSpec((SUB, inner), lambda t: (0, 0)),
        ],
        out_shape=[
            jax.ShapeDtypeStruct((rows * state, inner), bf16),
            jax.ShapeDtypeStruct((rows, LANE), f32),
            jax.ShapeDtypeStruct((rows, inner), bf16),
            jax.ShapeDtypeStruct((rows, inner), bf16),
            jax.ShapeDtypeStruct((SUB, inner), f32),
        ],
        scratch_shapes=[pltpu.VMEM((state * SUB, inner), f32)]
        + [
            pltpu.VMEM((tiles * SUB, 2 * state * LANE), f32),
            pltpu.VMEM((tiles * SUB, state * LANE), f32),
            pltpu.VMEM((tiles * SUB, inner), f32),
        ],
        compiler_params=pltpu.CompilerParams(vmem_limit_bytes=VMEM_BYTES),
    )(step, drive, grad, sel, spots, rates, pre_decay, pre_state, entry, conv, gating, grad_gated, skip)


def backward_call(step, drive, grad, sel, spots, rates, begin, prior, conv_sum, stream, readout_grad, step_back, select_back, taps, skip, flat, regions):
    rows, inner = step.shape
    state = rates.shape[0] // SUB
    tiles, count = scan_shapes(rows, state, inner, 8)
    bits = regions.count.bit_length() - 1
    phases = regions.early_phases()
    stride = 1

    def back(t):
        return (count - 1 - t, 0)

    wide = pl.BlockSpec((tiles * SUB, inner), back)
    table = pl.BlockSpec(spots.shape, lambda t: (0, 0), pipeline_mode=pl.Buffered(1))
    thin = pl.BlockSpec((tiles * SUB, sel.shape[1]), back)
    whole = pl.BlockSpec((state * SUB, inner), lambda t: (0, 0), pipeline_mode=pl.Buffered(1))
    narrow = pl.BlockSpec((tiles * SUB, LANE), back)
    width = taps.shape[0]
    halo = (width - 1) * SUB

    def fixed(x):
        return pl.BlockSpec(x.shape, lambda t: (0, 0), pipeline_mode=pl.Buffered(1))

    shape = (tiles, state, inner, 2, 4)
    return pl.pallas_call(
        functools.partial(backward_kernel, shape, count, regions, bits, phases, stride),
        name="scan_backward",
        grid=(count,),
        in_specs=[wide, wide, wide, thin, table, whole, whole]
        + [pl.BlockSpec((tiles * state * SUB, inner), back), wide, wide, narrow]
        + [fixed(step_back), fixed(select_back), fixed(taps), fixed(skip)]
        + [pl.BlockSpec(memory_space=pl.ANY)],
        out_specs=[
            wide,
            wide,
            narrow,
            pl.BlockSpec((state * SUB, inner), lambda t: (0, 0)),
            pl.BlockSpec(((width + 2) * SUB, inner), lambda t: (0, 0)),
            pl.BlockSpec((2 * halo, inner), lambda t: (0, 0)),
            pl.BlockSpec((regions.slot, SUB, LANE), lambda t: (0, 0, 0)),
        ],
        out_shape=[
            jax.ShapeDtypeStruct((rows, inner), bf16),
            jax.ShapeDtypeStruct((rows, inner), bf16),
            jax.ShapeDtypeStruct((rows, LANE), bf16),
            jax.ShapeDtypeStruct((state * SUB, inner), f32),
            jax.ShapeDtypeStruct(((width + 2) * SUB, inner), f32),
            jax.ShapeDtypeStruct((2 * halo, inner), f32),
            jax.ShapeDtypeStruct((regions.slot, SUB, LANE), f32),
        ],
        scratch_shapes=[pltpu.VMEM((state * SUB, inner), f32)]
        + [
            pltpu.VMEM((tiles * SUB, 2 * state * LANE), f32),
            pltpu.VMEM((tiles * SUB, state * LANE), f32),
            pltpu.VMEM((tiles * SUB, inner), f32),
            pltpu.VMEM((tiles * SUB, inner), f32),
            pltpu.VMEM((tiles * SUB + halo, inner), f32),
            pltpu.VMEM((tiles * SUB, LANE), f32),
        ]
        + Reducer.scratch(regions.depth, bits, phases),
        compiler_params=pltpu.CompilerParams(
            vmem_limit_bytes=62 * 2**20, collective_id=2, has_side_effects=True
        ),
    )(step, drive, grad, sel, spots, rates, begin, prior, conv_sum, stream, readout_grad, step_back, select_back, taps, skip, flat)


def turn_tiles(tiles):
    row = lax.broadcasted_iota(jnp.int32, (SUB, LANE), 0)
    for bit in (1, 2, 4):
        upper = (row // bit) % 2 == 1
        new = list(tiles)
        for a in range(SUB):
            if a & bit == 0:
                b = a + bit
                new[a] = jnp.where(upper, pltpu.roll(tiles[b], bit, 0), tiles[a])
                new[b] = jnp.where(upper, tiles[b], pltpu.roll(tiles[a], SUB - bit, 0))
        tiles = new
    return tiles


def product_kernel(steps, shapes, *refs):
    out_ref, held_ref = refs[-2:]
    contract = (((0,), (0,)), ((), ()))
    for turn, (rows, width) in enumerate(shapes):
        left_ref, right_ref = refs[2 * turn : 2 * turn + 2]
        per = width // ROW

        @pl.when(pl.program_id(0) // steps == turn)
        def _():
            for q in range(per):
                held_ref[:rows] = lax.dot_general(
                    left_ref[...], right_ref[:, q * ROW : (q + 1) * ROW], contract, preferred_element_type=f32
                )

                def one(r, carry):
                    tiles = [held_ref[at(r * SUB, SUB), a * LANE : (a + 1) * LANE] for a in range(SUB)]
                    for b, tile in enumerate(turn_tiles(tiles)):
                        out_ref[(r * SUB + b) * per + q] = tile
                    return carry

                lax.fori_loop(0, rows // SUB, one, 0, unroll=4)


def product_call(*pairs):
    steps = 8
    shapes = [(left.shape[1] // steps, right.shape[1]) for left, right in pairs]
    size = shapes[0][0] * shapes[0][1] // ROW

    def block(k):
        return lambda t: (0, jnp.clip(t - k * steps, 0, steps - 1))

    specs = []
    for k, (left, right) in enumerate(pairs):
        specs.append(pl.BlockSpec((left.shape[0], left.shape[1] // steps), block(k)))
        specs.append(pl.BlockSpec(right.shape, lambda t: (0, 0), pipeline_mode=pl.Buffered(1)))
    return pl.pallas_call(
        functools.partial(product_kernel, steps, shapes),
        name="flat_product",
        grid=(steps * len(pairs),),
        in_specs=specs,
        out_specs=pl.BlockSpec((size, SUB, LANE), lambda t: (t, 0, 0)),
        out_shape=jax.ShapeDtypeStruct((size * steps * len(pairs), SUB, LANE), f32),
        scratch_shapes=[pltpu.VMEM((max(rows for rows, _ in shapes), ROW), f32)],
        compiler_params=pltpu.CompilerParams(vmem_limit_bytes=VMEM_BYTES),
    )(*[x for pair in pairs for x in pair])


class Regions:
    def __init__(self, depth, count, span, gain, in_shape, small, out_shape):
        self.depth, self.count, self.span = depth, count, span
        self.per = in_shape[1] // ROW
        self.in_rows = in_shape[0]
        self.in_base = gain
        self.small_base = gain + in_shape[0] * self.per
        self.out_base = self.small_base + small
        self.out_rows = out_shape[0] * out_shape[1] // ROW
        self.need = (span - 1) // ROW + 2
        self.lines = min((self.need + self.per - 2) // self.per + 1, self.in_rows)
        self.half = self.lines * self.per // 2
        self.pieces = -(-self.need // self.half)
        self.slot = self.pieces * self.half

    def base(self, owner):
        return owner * self.span // ROW

    def in_first(self, owner):
        line = lax.max(self.base(owner) - self.in_base, 0) // self.per
        return lax.min(line, self.in_rows - self.lines)

    def out_first(self, owner):
        return lax.max(lax.min(self.base(owner) - self.out_base, self.out_rows - self.slot), 0)

    def meets_in(self, z):
        return z * self.count * self.span // ROW < self.small_base

    def meets_out(self, z):
        return ((z + 1) * self.count * self.span - 1) // ROW >= self.out_base

    def early_start(self, z, owner):
        if not self.meets_out(z):
            return self.in_first(owner) * (self.per // 2)
        out = self.in_rows * self.per // 2 + self.out_first(owner)
        if not self.meets_in(z):
            return out
        inside = self.base(owner) < self.small_base
        return jnp.where(inside, self.in_first(owner) * (self.per // 2), out)

    def early_phases(self):
        phases = []
        cut = 2 if self.half % 4 == 0 else 1
        size = self.half // cut
        for z in range(self.depth):
            for piece in range((self.pieces if self.meets_out(z) else 1) * cut):
                phases.append((z, piece * size, size))
        return phases

    def late_phases(self):
        cut = 2 if self.half % 4 == 0 else 1
        size = self.half // cut
        return [(z, piece * size, size) for z in range(self.depth) if self.meets_in(z) for piece in range(cut)]


class Reducer:
    def __init__(self, depth, bits, phases, stride, start, src_ref, refs):
        self.depth, self.bits, self.phases, self.stride = depth, bits, phases, stride
        self.start, self.src = start, src_ref
        self.n = bits - 1
        self.half = phases[0][2] // 2
        self.acc, self.first = refs[:2]
        self.bit_recvs = refs[2 : 2 + self.n]
        self.down, self.up = refs[2 + self.n : 4 + self.n]
        (
            self.local_sem,
            self.core_send,
            self.core_recv,
            self.bit_send,
            self.bit_recv,
            self.z_send,
            self.z_recv,
        ) = refs[4 + self.n : 11 + self.n]
        self.blk, self.z = lax.axis_index("blk"), lax.axis_index("batch")
        self.mine = [(self.blk // 2**b) % 2 for b in range(bits)]
        self.partner = [self.blk + (1 - 2 * self.mine[b]) * 2**b for b in range(bits)]
        self.last = self.n + depth - 1
        self.slots = stride * (len(phases) - 1) + self.last + 1

    @staticmethod
    def scratch(depth, bits, phases):
        n, count, size = bits - 1, len(phases), phases[0][2]
        tile = (SUB, LANE)
        dma = pltpu.SemaphoreType.DMA
        return (
            [pltpu.VMEM((count,) + (2,) * n + (size,) + tile, f32)] * 2
            + [pltpu.VMEM((count, 2) + (2,) * (n - 1 - s) + (size // 2,) + tile, f32) for s in range(n)]
            + [pltpu.VMEM((count, size) + tile, f32)] * 2
            + [dma((count * 2**n,))] * 3
            + [dma((max(count * n * 2, 1),))] * 2
            + [dma((count,)), dma((2 * count,))]
        )

    def greet(self):
        barrier = pltpu.get_barrier_semaphore()
        for other in self.partner:
            pl.semaphore_signal(barrier, inc=1, device_id={"blk": other}, device_id_type=MESH)
        for by in (1, self.depth - 1):
            other = lax.rem(self.z + by, self.depth)
            pl.semaphore_signal(barrier, inc=1, device_id={"batch": other}, device_id_type=MESH)
        pl.semaphore_wait(barrier, self.bits + 2)

    def digits(self, r):
        return tuple((r // 2**i) % 2 for i in reversed(range(self.n)))

    def window(self, p, r, core):
        goal, offset, size = self.phases[p]
        owner = goal * 2**self.bits + 2 * r + core
        return pl.ds(self.start(goal, owner) + offset, size)

    def core_copies(self, p, own=False):
        copies = []
        for r in range(2**self.n):
            spot = p * 2**self.n + r
            where = (p,) + self.digits(r)
            if own:
                copies.append(
                    pltpu.make_async_copy(
                        self.src.at[self.window(p, r, self.mine[0])], self.acc.at[where], self.local_sem.at[spot]
                    )
                )
            else:
                copies.append(
                    pltpu.make_async_remote_copy(
                        src_ref=self.src.at[self.window(p, r, 1 - self.mine[0])],
                        dst_ref=self.first.at[where],
                        send_sem=self.core_send.at[spot],
                        recv_sem=self.core_recv.at[spot],
                        device_id={"blk": self.partner[0]},
                        device_id_type=MESH,
                    )
                )
        return copies

    def order(self, part):
        return list(range(self.n)) if part == 0 else list(reversed(range(self.n)))

    def place(self, p, part, done, pick):
        spots = [slice(None)] * self.n
        for i in self.order(part)[:done]:
            spots[i] = self.mine[i + 1]
        spots[self.order(part)[done]] = pick
        return (p,) + tuple(reversed(spots)) + (slice(part * self.half, (part + 1) * self.half),)

    def bit_copies(self, p, s):
        copies = []
        for part in range(2):
            i = self.order(part)[s]
            spot = (p * self.n + s) * 2 + part
            copies.append(
                pltpu.make_async_remote_copy(
                    src_ref=self.acc.at[self.place(p, part, s, 1 - self.mine[i + 1])],
                    dst_ref=self.bit_recvs[s].at[p, part],
                    send_sem=self.bit_send.at[spot],
                    recv_sem=self.bit_recv.at[spot],
                    device_id={"blk": self.partner[i + 1]},
                    device_id_type=MESH,
                )
            )
        return copies

    def settled(self, p):
        return (p,) + tuple(reversed([self.mine[i + 1] for i in range(self.n)]))

    def z_copy(self, p, up):
        return pltpu.make_async_remote_copy(
            src_ref=self.acc.at[self.settled(p)],
            dst_ref=(self.up if up else self.down).at[p],
            send_sem=self.z_send.at[p],
            recv_sem=self.z_recv.at[2 * p + up],
            device_id={"batch": lax.rem(self.z + (1 if up else self.depth - 1), self.depth)},
            device_id_type=MESH,
        )

    def add(self, dst, dst_at, src, src_at):
        dst[dst_at] += src[src_at]

    def finish_core(self, p):
        for copy in self.core_copies(p, True):
            copy.wait()
        for copy in self.core_copies(p):
            copy.wait_recv()
        for r in range(2**self.n):
            where = (p,) + self.digits(r)
            self.add(self.acc, where, self.first, where)

    def finish_bit(self, p, s):
        for part, copy in enumerate(self.bit_copies(p, s)):
            copy.wait_recv()
            kept = self.place(p, part, s, self.mine[self.order(part)[s] + 1])
            free = [i for i in range(1, 1 + self.n) if isinstance(kept[i], slice)]
            for r in range(2 ** len(free)):
                chosen = tuple((r // 2**j) % 2 for j in reversed(range(len(free))))
                to = list(kept)
                for i, v in zip(free, chosen):
                    to[i] = v
                self.add(self.acc, tuple(to), self.bit_recvs[s], (p, part) + chosen)

    def take(self, p, up):
        self.z_copy(p, up).wait_recv()
        self.add(self.acc, self.settled(p), self.up if up else self.down, p)

    def z_moves(self, p, u):
        goal = self.phases[p][0]
        moves = []
        if self.depth - 1 - u > goal:
            moves.append((self.depth - 1 - u, False))
        if u < goal:
            moves.append((u, True))
        return moves

    def act(self, p, stage):
        n = self.n
        if stage == 0:
            for copy in self.core_copies(p) + self.core_copies(p, True):
                copy.start()
            return
        if stage == 1:
            self.finish_core(p)
        elif stage <= n + 1:
            self.finish_bit(p, stage - 2)
        if stage <= n:
            for copy in self.bit_copies(p, stage - 1):
                copy.start()
            return
        u = stage - n - 1
        for mover, up in self.z_moves(p, u):

            @pl.when(self.z == mover)
            def _():
                if u > 0:
                    self.take(p, up)
                self.z_copy(p, up).start()

    def run(self, t):
        for stage in reversed(range(self.last + 1)):
            p, odd = divmod(t - stage, self.stride)
            if odd == 0 and 0 <= p < len(self.phases):
                self.act(p, stage)

    def collect(self, out_ref):
        for p, (goal, offset, size) in enumerate(self.phases):

            @pl.when(self.z == goal)
            def _():
                if goal < self.depth - 1:
                    self.take(p, False)
                if goal > 0:
                    self.take(p, True)
                out_ref[offset : offset + size] = self.acc[self.settled(p)]

        for p in range(len(self.phases)):
            for copy in self.core_copies(p):
                copy.wait_send()
            for s in range(self.n):
                for copy in self.bit_copies(p, s):
                    copy.wait_send()
            for u in range(self.depth - 1):
                for mover, up in self.z_moves(p, u):

                    @pl.when(self.z == mover)
                    def _():
                        self.z_copy(p, up).wait_send()


def put_restored(value, turn_ref, out_ref, block):
    rows, width = value.shape
    tiles = rows // SUB
    step = out_ref.shape[0] // SUB
    for a in range(width // LANE):
        turn_ref[a] = value[:, a * LANE : (a + 1) * LANE]
    for j in range(SUB):
        here = pl.ds(pl.multiple_of(j * step + block * tiles, tiles), tiles)
        for a in range(width // LANE):
            part = turn_ref[a, pl.ds(j, tiles, stride=SUB), :]
            out_ref[here, a * LANE : (a + 1) * LANE] = part.astype(bf16)


def late_kernel(
    regions,
    bits,
    phases,
    blocks,
    flat_ref,
    early_ref,
    gain_ref,
    *refs,
):
    depth, span = regions.depth, regions.span
    sources, refs = refs[:7], refs[7:]
    window_ref, totals_ref, result_ref, grad_ref = refs[:4]
    held, refs = refs[4:11], refs[11:]
    gate_back, stream_back, in_w, token, cot, gated, out_w = held
    late_ref, turn_ref, gain_sum, sums, ring, load_sem, ring_send, ring_recv = refs[:8]
    work = Reducer(depth, bits, phases, 1, lambda z, owner: regions.in_first(owner) * (regions.per // 2), flat_ref, refs[8:])
    blk, z = work.blk, work.z
    inner = gated.shape[1]
    loads = [pltpu.make_async_copy(src, dst, load_sem.at[i]) for i, (src, dst) in enumerate(zip(sources, held))]
    for load in loads:
        load.start()
    work.greet()
    gain_sum[...] = jnp.zeros_like(gain_sum)
    size = token.shape[0] // blocks
    across = (((1,), (1,)), ((), ()))

    def slot(t, carry):
        for k in range(work.slots):

            @pl.when(t == k)
            def _():
                work.run(k)
                if k == 0:
                    for load in loads:
                        load.wait()

        @pl.when(t < blocks)
        def _():
            here = pl.ds(pl.multiple_of(t * size, size), size)
            source = token[here, :].astype(f32)
            output = jnp.dot(gated[here, :], out_w[...], preferred_element_type=f32)
            put_restored(source + output, turn_ref, result_ref, t)
            grad_normed = lax.dot_general(
                stream_back[here, :], in_w[:, :inner], across, preferred_element_type=f32
            ) + lax.dot_general(gate_back[here, :], in_w[:, inner:], across, preferred_element_type=f32)
            scale = lax.rsqrt(jnp.mean(source * source, axis=-1, keepdims=True) + EPS)
            scaled = source * scale
            part = grad_normed * scaled
            gain_sum[...] += jnp.sum(part.reshape(size // SUB, SUB, part.shape[1]), 0)
            weighted = grad_normed * gain_ref[...]
            mean = jnp.mean(weighted * source, axis=-1, keepdims=True)
            back = scale * weighted - source * (scale * scale * scale) * mean + cot[here, :].astype(f32)
            put_restored(back, turn_ref, grad_ref, t)

        return carry

    lax.fori_loop(0, max(work.slots, blocks), slot, 0)
    late_ref[...] = jnp.zeros_like(late_ref)
    work.collect(late_ref)

    owner = z * 2**bits + blk
    base = regions.base(owner)
    inside = lax.broadcasted_iota(jnp.int32, (SUB, LANE), 0) * LANE + lax.broadcasted_iota(
        jnp.int32, (SUB, LANE), 1
    )
    sums[0, 0] = jnp.zeros((SUB, LANE), f32)
    gain = jnp.sum(gain_sum[...], 0, keepdims=True)
    for a in range(SUB):
        sums[0, 1, a : a + 1, :] = gain[:, a * LANE : (a + 1) * LANE]
    half = regions.per // 2
    window_ref[...] = jnp.zeros_like(window_ref)

    def keep(value, row):
        place = row - base

        @pl.when((place >= 0) & (place < regions.need))
        def _():
            spot = inside + (row * ROW - owner * span)
            own = jnp.where((spot >= 0) & (spot < span), value, 0.0)
            sums[0, 0] += own * own
            window_ref[place] = value

    @pl.when(base < regions.small_base)
    def _():
        def line(d, carry):
            row = regions.in_base + (regions.in_first(owner) + d) * regions.per
            for q in range(half):
                keep(late_ref[d * half + q], row + q)
                keep(early_ref[d * half + q], row + half + q)
            return carry

        lax.fori_loop(0, regions.lines, line, 0)

    @pl.when(base >= regions.small_base)
    def _():
        def line(i, carry):
            keep(early_ref[i], regions.out_base + regions.out_first(owner) + i)
            return carry

        lax.fori_loop(0, regions.slot, line, 0)

    for b in range(bits):
        copy = pltpu.make_async_remote_copy(
            src_ref=sums.at[b],
            dst_ref=sums.at[bits + 1 + b],
            send_sem=ring_send.at[b],
            recv_sem=ring_recv.at[b],
            device_id={"blk": work.partner[b]},
            device_id_type=MESH,
        )
        copy.start()
        copy.wait()
        sums[b + 1] = sums[b] + sums[bits + 1 + b]
    ring[z] = sums[bits]
    for u in range(depth - 1):
        moves = (
            ((z + u < depth) & (z > 0), lax.min(z + u, depth - 1), depth - 1, 0),
            ((z - u >= 0) & (z < depth - 1), lax.max(z - u, 0), 1, 1),
        )
        gets = (
            ((z < depth - 1) & (z + 1 + u < depth), lax.min(z + 1 + u, depth - 1), depth - 1, 0),
            ((z > 0) & (z - 1 - u >= 0), lax.max(z - 1 - u, 0), 1, 1),
        )

        def hop(origin, by, way):
            return pltpu.make_async_remote_copy(
                src_ref=ring.at[origin],
                dst_ref=ring.at[origin],
                send_sem=ring_send.at[bits + u * 2 + way],
                recv_sem=ring_recv.at[bits + u * 2 + way],
                device_id={"batch": lax.rem(z + by, depth)},
                device_id_type=MESH,
            )

        for cond, origin, by, way in moves:

            @pl.when(cond)
            def _():
                hop(origin, by, way).start()

        for cond, origin, by, way in gets:

            @pl.when(cond)
            def _():
                hop(origin, by, way).wait_recv()

        for cond, origin, by, way in moves:

            @pl.when(cond)
            def _():
                hop(origin, by, way).wait_send()

    total = ring[0]
    for zz in range(1, depth):
        total = total + ring[zz]
    totals_ref[...] = total

    @pl.when(base < regions.in_base)
    def _():
        window_ref[0] = total[1]


def late_call(flat, early, gain, sources, regions):
    bits = regions.count.bit_length() - 1
    depth = regions.depth
    phases = regions.late_phases()
    tile = (SUB, LANE)
    dma = pltpu.SemaphoreType.DMA
    hops = bits + 2 * (depth - 1)
    vmem = pl.BlockSpec(memory_space=pltpu.VMEM)
    far = pl.BlockSpec(memory_space=pl.ANY)
    rows, model = sources[3].shape
    blocks = 8
    return pl.pallas_call(
        functools.partial(late_kernel, regions, bits, phases, blocks),
        name="reduce_late",
        in_specs=[far, vmem, vmem] + [far] * len(sources),
        out_specs=[vmem] * 4,
        out_shape=[
            jax.ShapeDtypeStruct((regions.need,) + tile, f32),
            jax.ShapeDtypeStruct((2,) + tile, f32),
            jax.ShapeDtypeStruct((rows, model), bf16),
            jax.ShapeDtypeStruct((rows, model), bf16),
        ],
        scratch_shapes=[pltpu.VMEM(x.shape, x.dtype) for x in sources]
        + [
            pltpu.VMEM((regions.half,) + tile, f32),
            pltpu.VMEM((model // LANE, rows // blocks, LANE), f32),
            pltpu.VMEM((SUB, model), f32),
            pltpu.VMEM((2 * bits + 1, 2) + tile, f32),
            pltpu.VMEM((depth, 2) + tile, f32),
            dma((len(sources),)),
            dma((hops,)),
            dma((hops,)),
        ]
        + Reducer.scratch(depth, bits, phases),
        compiler_params=pltpu.CompilerParams(
            vmem_limit_bytes=62 * 2**20, collective_id=1, has_side_effects=True
        ),
    )(flat, early, gain, *sources)


def share(regions, gain, in_part, small, out_part, owner):
    base, high = regions.base(owner), regions.need
    place = (base + lax.iota(jnp.int32, high))[:, None, None]
    total = jnp.broadcast_to(gain, (high, SUB, LANE))
    for part, origin, low in (
        (in_part, regions.in_base + regions.in_first(owner) * regions.per, regions.in_base),
        (small, regions.small_base, regions.small_base),
        (out_part, regions.out_base + regions.out_first(owner), regions.out_base),
    ):
        padded = jnp.pad(part, ((high, high), (0, 0), (0, 0)))
        offset = jnp.clip(base - origin + high, 0, part.shape[0] + high)
        total = jnp.where(place >= low, lax.dynamic_slice_in_dim(padded, offset, high), total)
    return lax.dynamic_slice_in_dim(total.reshape(-1), owner * regions.span % ROW, regions.span)


def exchange(totals, state):
    count = lax.axis_size("blk")
    index = lax.axis_index("blk")
    decay, end, leave = totals[:state], totals[state : 2 * state], totals[2 * state :]
    pre_decay, pre_state = jnp.ones_like(decay), jnp.zeros_like(end)
    post_decay, post_state = jnp.ones_like(decay), jnp.zeros_like(end)
    bit = 1
    while bit < count:
        pairs = [(i, i ^ bit) for i in range(count)]
        far = lax.ppermute(jnp.concatenate([decay, end, leave], 0), "blk", pairs)
        far_decay, far_end, far_leave = far[:state], far[state : 2 * state], far[2 * state :]
        upper = (index & bit) != 0
        pre_state = jnp.where(upper, pre_state + pre_decay * far_end, pre_state)
        pre_decay = jnp.where(upper, pre_decay * far_decay, pre_decay)
        post_state = jnp.where(upper, post_state, post_state + post_decay * far_leave)
        post_decay = jnp.where(upper, post_decay, post_decay * far_decay)
        end = jnp.where(upper, end + decay * far_end, far_end + far_decay * end)
        leave = jnp.where(upper, far_leave + far_decay * leave, leave + decay * far_leave)
        decay = decay * far_decay
        bit *= 2
    return pre_state, post_state


def local(
    tokens,
    out_cot,
    norm_gain,
    in_weight,
    conv_weight,
    conv_bias,
    xproj_weight,
    dt_weight,
    dt_bias,
    a_log,
    d_skip,
    out_weight,
    moment_one,
    moment_two,
):
    contract = (((0,), (0,)), ((), ()))
    backward = (((1,), (1,)), ((), ()))
    token_rows = interleave(tokens[0])
    cot_low = interleave(out_cot[0])
    source = token_rows.astype(f32)
    length = source.shape[0]
    inner = dt_bias.shape[0]
    state = a_log.shape[0]
    rank = dt_weight.shape[0]
    width = conv_weight.shape[0]
    halo = (width - 1) * SUB
    scale = lax.rsqrt(jnp.mean(source * source, axis=-1, keepdims=True) + EPS)
    normed = (source * scale * norm_gain).astype(bf16)
    stream = jnp.dot(normed, in_weight[:, :inner], preferred_element_type=f32)
    ends = stream[length - halo :].reshape(width - 1, SUB, inner)
    tail = shifted(ends[:, SUB - 1], "blk", 1)
    gating = jnp.dot(normed, in_weight[:, inner:], preferred_element_type=f32)
    grad_gated = lax.dot_general(cot_low, out_weight, backward, preferred_element_type=f32)
    head = jnp.concatenate([tail[:, None], ends[:, : SUB - 1]], 1).reshape(halo, inner)
    rates = -jnp.exp(a_log)
    rates_wide = jnp.repeat(rates * LOG2E, SUB, axis=0)
    spots = spread_table(2 * state)
    spare = LANE - rank - 2 * state
    select_in = jnp.pad(jnp.roll(xproj_weight, 2 * state, 1), ((0, 0), (0, spare)))
    step_in = jnp.pad(dt_weight, ((2 * state, spare), (0, 0)))
    (
        conv_sum,
        conv_low,
        step_size,
        drive,
        grad_scanned,
        sel_low,
        terms,
        pre_decay,
        pre_state,
        post_decay,
        post_state,
        totals,
    ) = summary_call(
        stream,
        gating,
        grad_gated,
        head,
        conv_weight,
        conv_bias[None],
        select_in,
        step_in,
        dt_bias[None],
        spots,
        rates_wide,
    )
    entry, arriving = exchange(totals, state)
    prior, readout_grads, gated, grad_gating, skip_grads = forward_call(
        step_size,
        drive,
        grad_scanned,
        terms,
        spots,
        rates_wide,
        pre_decay,
        pre_state,
        entry,
        conv_low,
        gating,
        grad_gated,
        d_skip[None],
    )
    grad_d_skip = jnp.sum(skip_grads, 0)

    span = moment_one.shape[0]
    small_rows = sum(
        value.size for value in (conv_weight, conv_bias, xproj_weight, dt_weight, dt_bias, a_log, d_skip)
    ) // ROW
    regions = Regions(
        lax.axis_size("batch"),
        lax.axis_size("blk"),
        span,
        norm_gain.size // ROW,
        in_weight.shape,
        small_rows,
        out_weight.shape,
    )
    flat_early = product_call((normed, grad_gating), (gated, cot_low))
    step_back = step_in.T
    select_back = select_in.T
    grad_stream_low, grad_pre_low, grad_selectors, rate_grads, taps_grads, edges, early = backward_call(
        step_size,
        drive,
        grad_scanned,
        terms,
        spots,
        rates_wide,
        post_state + post_decay * jnp.repeat(arriving, SUB, axis=0),
        prior,
        conv_sum,
        stream,
        readout_grads,
        step_back,
        select_back,
        conv_weight,
        d_skip[None],
        flat_early,
        regions,
    )
    grad_a_log = LN2 * jnp.sum(rate_grads.reshape(state, SUB, inner), 1)
    begins = edges[:halo].reshape(width - 1, SUB, inner)
    ahead = shifted(begins[:, 0], "blk", -1)
    grad_dt_weight = lax.dot_general(sel_low, grad_pre_low, contract, preferred_element_type=f32)[
        2 * state : 2 * state + rank
    ]
    grad_xproj = lax.dot_general(grad_selectors, conv_low, contract, preferred_element_type=f32)
    foot = jnp.concatenate([begins[:, 1:], ahead[:, None]], 1)
    lasts = edges[halo:].reshape(width - 1, SUB, inner)
    further = jnp.concatenate([lasts, foot], 0)
    last_stream = stream[length - halo :].reshape(width - 1, SUB, inner)
    grad_last = conv_weight[width - 1] * lasts
    taps_grads = jnp.sum(taps_grads.reshape(width + 2, SUB, inner), 1)
    tap_grads = []
    for offset in range(width - 1):
        lead = width - 1 - offset
        grad_last = grad_last + conv_weight[offset] * further[lead : lead + width - 1]
        over = jnp.sum(last_stream[width - 1 - lead :] * foot[:lead], (0, 1))
        tap_grads.append(taps_grads[offset] + over)
    tap_grads.append(taps_grads[width - 1])
    grad_conv_weight = jnp.stack(tap_grads, 0)
    grad_conv_bias = taps_grads[width]
    grad_dt_bias = taps_grads[width + 1]
    grad_stream_low = lax.dynamic_update_slice_in_dim(
        grad_stream_low, grad_last.reshape(halo, inner).astype(bf16), length - halo, 0
    )
    thin = (grad_xproj, grad_dt_weight, grad_a_log, grad_conv_weight, grad_conv_bias, grad_dt_bias, grad_d_skip)
    thin = jnp.concatenate([value.reshape(-1, inner) for value in thin], 0)
    grad_stream_low, thin = lax.optimization_barrier((grad_stream_low, thin))
    thin = lax.psum(jnp.pad(thin, ((0, -thin.shape[0] % SUB), (0, 0))), ("batch", "blk"))
    parts = []
    for value in (LANE, rank, state, width, 1, 1, 1):
        start = sum(part.shape[0] for part in parts)
        parts.append(thin[start : start + value])
    used = rank + 2 * state
    xproj = jnp.roll(parts[0][:used], rank, 0).T
    order = (parts[3], parts[4], xproj, parts[1], parts[5], parts[2], parts[6])
    small = jnp.concatenate([value.reshape(-1, ROW) for value in order], 0)
    window, totals, result, grad_tokens = late_call(
        product_call((normed, grad_stream_low)),
        early,
        norm_gain[None],
        (grad_gating, grad_stream_low, in_weight, token_rows, cot_low, gated, out_weight),
        regions,
    )
    result, grad_tokens = result[None], grad_tokens[None]
    grad_norm = jnp.sqrt(jnp.sum(totals[0]) + jnp.sum(totals[1] * totals[1]) + jnp.sum(small * small))
    owner = lax.axis_index(("batch", "blk"))
    begin = owner * span
    base, high = regions.base(owner), regions.need
    place = (base + lax.iota(jnp.int32, high))[:, None, None]
    padded = jnp.pad(small.reshape(-1, SUB, LANE), ((high, high), (0, 0), (0, 0)))
    offset = jnp.clip(base - regions.small_base + high, 0, small_rows + high)
    window = jnp.where(
        (place >= regions.small_base) & (place < regions.out_base),
        lax.dynamic_slice_in_dim(padded, offset, high),
        window,
    )
    shard = lax.dynamic_slice_in_dim(window.reshape(-1), begin % ROW, span)
    in_part = lax.dynamic_slice_in_dim(in_weight, regions.in_first(owner), regions.lines)
    out_part = lax.dynamic_slice_in_dim(out_weight, regions.out_first(owner), regions.slot)
    small_params = (conv_weight, conv_bias, xproj_weight, dt_weight, dt_bias, a_log, d_skip)
    small_params = jnp.concatenate([value.reshape(-1, ROW).astype(f32) for value in small_params], 0)
    owned = share(
        regions,
        norm_gain.reshape(-1, SUB, LANE),
        in_part.astype(f32).reshape(-1, SUB, LANE),
        small_params.reshape(-1, SUB, LANE),
        out_part.astype(f32).reshape(-1, SUB, LANE),
        owner,
    )
    lower = norm_gain.size + in_weight.size + sum(
        value.size for value in (conv_weight, conv_bias, xproj_weight, dt_weight)
    )
    upper = lower + dt_bias.size + a_log.size + d_skip.size
    place = begin + lax.iota(jnp.int32, span)
    keep = jnp.where((place >= lower) & (place < upper), 0.0, 1.0).astype(f32)
    clipped = shard * jnp.minimum(1.0, CLIP / (grad_norm + 1e-06))
    new_one = BETA_ONE * moment_one + (1.0 - BETA_ONE) * clipped
    new_two = BETA_TWO * moment_two + (1.0 - BETA_TWO) * clipped * clipped
    first = new_one / (1.0 - BETA_ONE**ADAM_STEP)
    second = new_two / (1.0 - BETA_TWO**ADAM_STEP)
    param_step = -RATE * (first / (jnp.sqrt(second) + ADAM_EPS) + DECAY * keep * owned)
    return (result, grad_tokens, shard, grad_norm, param_step, new_one, new_two)


def solution(mesh):
    return jax.shard_map(
        local,
        mesh=mesh,
        in_specs=(P("batch", "blk", None),) * 2 + (P(),) * 10 + (P(("batch", "blk")),) * 2,
        out_specs=(P("batch", "blk", None),) * 2
        + (P(("batch", "blk")), P(), P(("batch", "blk")), P(("batch", "blk")), P(("batch", "blk"))),
        check_vma=False,
    )
```

```python
import functools
import math

import jax
import jax.numpy as jnp
from jax import lax
from jax.experimental import pallas as pl
from jax.experimental.pallas import tpu as pltpu
from jax.sharding import PartitionSpec as P

ADAM_STEP = 100
EPS = 1e-05
RATE = 0.002
BETA_ONE = 0.9
BETA_TWO = 0.95
ADAM_EPS = 1e-08
DECAY = 0.1
CLIP = 1.0

LOG2E = 1.0 / math.log(2.0)
LN2 = math.log(2.0)
SUB = 8
LANE = 128
ROW = 1024
VMEM_BYTES = 56 * 2**20

MESH = pl.DeviceIdType.MESH

f32 = jnp.float32
bf16 = jnp.bfloat16


def shifted(x, axis, by):
    count = lax.axis_size(axis)
    pairs = [(i, i + by) for i in range(count) if 0 <= i + by < count]
    return lax.ppermute(x, axis, pairs)


def silu_slope(value):
    sig = jax.nn.sigmoid(value)
    return sig * (1.0 + value * (1.0 - sig))


def interleave(x):
    rows, width = x.shape
    return x.reshape(SUB, rows // SUB, width).transpose(1, 0, 2).reshape(rows, width)


def restore(x):
    rows, width = x.shape
    return x.reshape(rows // SUB, SUB, width).transpose(1, 0, 2).reshape(rows, width)


def at(start, size):
    return pl.ds(pl.multiple_of(start, size), size)


def spread(sel_ref, spots_ref, out_ref):
    out_ref[...] = jnp.dot(sel_ref[...], spots_ref[...], preferred_element_type=f32)


def gather_lanes(src_ref, spots_ref, out_ref):
    spots = spots_ref[0:LANE, 0 : src_ref.shape[1]]
    back = (((1,), (1,)), ((), ()))
    out_ref[...] = lax.dot_general(src_ref[...].astype(bf16), spots, back, preferred_element_type=f32)


def spread_table(count):
    row = lax.broadcasted_iota(jnp.int32, (LANE, count * LANE), 0)
    col = lax.broadcasted_iota(jnp.int32, (LANE, count * LANE), 1) // LANE
    return ((row % count == col) & (row < 3 * count)).astype(bf16)


def summary_kernel(
    shape,
    stream_ref,
    gating_ref,
    grad_gated_ref,
    head_ref,
    taps_ref,
    bias_ref,
    select_in_ref,
    step_in_ref,
    step_bias_ref,
    spots_ref,
    rates_ref,
    conv_sum_ref,
    conv_ref,
    step_ref,
    drive_ref,
    grad_ref,
    low_ref,
    sel_ref,
    pre_decay_ref,
    pre_state_ref,
    post_decay_ref,
    post_state_ref,
    totals_ref,
    end_ref,
    exit_ref,
    prod_ref,
    select_ref,
    longer_ref,
    wide_ref,
):
    tiles, state, inner, cols, group = shape
    turn = pl.program_id(0)
    block = tiles * SUB
    width = taps_ref.shape[0]
    halo = (width - 1) * SUB

    @pl.when(turn == 0)
    def _():
        end_ref[...] = jnp.zeros_like(end_ref)
        exit_ref[...] = jnp.zeros_like(exit_ref)
        prod_ref[...] = jnp.ones_like(prod_ref)
        longer_ref[:halo, :] = head_ref[...]

    @pl.when(turn > 0)
    def _():
        longer_ref[:halo, :] = longer_ref[block:, :]

    longer_ref[halo:, :] = stream_ref[...]

    def convs(c, carry):
        lanes = at(c * 2 * LANE, 2 * LANE)
        taps = [jnp.broadcast_to(taps_ref[k : k + 1, lanes], (2 * SUB, 2 * LANE)) for k in range(width)]
        bias = bias_ref[:, lanes]

        def pair(i, carry):
            here = at(i * 2 * SUB, 2 * SUB)
            total = bias + taps[width - 1] * stream_ref[here, lanes]
            for k in range(width - 1):
                total = total + taps[k] * longer_ref[pl.ds(pl.multiple_of((2 * i + k) * SUB, SUB), 2 * SUB), lanes]
            conv_sum_ref[here, lanes] = total
            conv_ref[here, lanes] = (total * jax.nn.sigmoid(total)).astype(bf16)
            gating = gating_ref[here, lanes]
            grad_ref[here, lanes] = grad_gated_ref[here, lanes] * (gating * jax.nn.sigmoid(gating))
            return carry

        lax.fori_loop(0, tiles // 2, pair, 0, unroll=8)
        return carry

    lax.fori_loop(0, inner // (2 * LANE), convs, 0)
    lane = lax.broadcasted_iota(jnp.int32, (block, LANE), 1)
    rank = step_in_ref.shape[0]
    used = rank + 2 * state
    wide_ref[...] = jnp.zeros_like(wide_ref)
    wide_ref[:, :used] = jnp.dot(conv_ref[...], select_in_ref[...], preferred_element_type=f32)
    selectors = wide_ref[...]
    low_ref[...] = selectors.astype(bf16)
    low = low_ref[:, :rank]
    value = jnp.where(lane < 2 * state, pltpu.roll(selectors, LANE - rank, 1), 0.0)
    high = value.astype(bf16).astype(f32)
    middle = (value - high).astype(bf16).astype(f32)
    rest = value - high - middle
    sel_ref[...] = (high + pltpu.roll(middle, 2 * state, 1) + pltpu.roll(rest, 4 * state, 1)).astype(bf16)

    step_ref[...] = jnp.dot(low, step_in_ref[...], preferred_element_type=f32)

    def steps(c, carry):
        lanes = at(c * 2 * LANE, 2 * LANE)
        bias = step_bias_ref[:, lanes]

        def pair(i, carry):
            here = at(i * 2 * SUB, 2 * SUB)
            pre = step_ref[here, lanes] + bias
            step = jnp.maximum(pre, 0.0) + jnp.log1p(jnp.exp(-jnp.abs(pre)))
            step_ref[here, lanes] = step
            drive_ref[here, lanes] = step * conv_ref[here, lanes].astype(f32)
            return carry

        lax.fori_loop(0, tiles // 2, pair, 0, unroll=8)
        return carry

    lax.fori_loop(0, inner // (2 * LANE), steps, 0)
    spread(sel_ref, spots_ref, select_ref)

    def columns(c, carry):
        lanes = [at((c * cols + k) * LANE, LANE) for k in range(cols)]
        for first in range(0, state, group):
            spots = [(n, k) for n in range(group) for k in range(cols)]
            where = [(slice((first + n) * SUB, (first + n + 1) * SUB), lanes[k]) for n, k in spots]
            rates = [rates_ref[w] for w in where]

            def advance(i, carry):
                ends, exits, prods = carry
                here = at(i * SUB, SUB)
                step = [step_ref[here, l] for l in lanes]
                drive = [drive_ref[here, l] for l in lanes]
                grad = [grad_ref[here, l] for l in lanes]
                inject = [select_ref[here, (first + n) * LANE : (first + n + 1) * LANE] for n in range(group)]
                readout = [
                    select_ref[here, (state + first + n) * LANE : (state + first + n + 1) * LANE] for n in range(group)
                ]
                new = ([], [], [])
                for s, (n, k) in enumerate(spots):
                    decay = jnp.exp2(step[k] * rates[s])
                    prod = prods[s] * decay
                    new[0].append(ends[s] * decay + drive[k] * inject[n])
                    new[1].append(exits[s] + prod * (grad[k] * readout[n]))
                    new[2].append(prod)
                return tuple(tuple(x) for x in new)

            start = tuple(tuple(ref[w] for w in where) for ref in (end_ref, exit_ref, prod_ref))
            ends, exits, prods = lax.fori_loop(0, tiles, advance, start, unroll=16)
            for s, w in enumerate(where):
                end_ref[w] = ends[s]
                exit_ref[w] = exits[s]
                prod_ref[w] = prods[s]
        return carry

    lax.fori_loop(0, inner // (LANE * cols), columns, 0)

    @pl.when(turn == pl.num_programs(0) - 1)
    def _():
        row = lax.broadcasted_iota(jnp.int32, (SUB, LANE), 0)

        def columns(c, carry):
            lanes = at(c * LANE, LANE)
            for n in range(state):
                here = (slice(n * SUB, (n + 1) * SUB), lanes)
                for way, src, decay_out, state_out, total_row in (
                    (1, end_ref, pre_decay_ref, pre_state_ref, 1),
                    (-1, exit_ref, post_decay_ref, post_state_ref, 2),
                ):
                    decay, value = prod_ref[here], src[here]

                    def seen(by):
                        return row >= by if way > 0 else row < SUB - by

                    for by in (1, 2, 4):
                        far_decay = pltpu.roll(decay, by if way > 0 else SUB - by, 0)
                        far_value = pltpu.roll(value, by if way > 0 else SUB - by, 0)
                        value = jnp.where(seen(by), value + decay * far_value, value)
                        decay = jnp.where(seen(by), decay * far_decay, decay)
                    last = SUB - 1 if way > 0 else 0
                    totals_ref[pl.ds(n, 1), lanes] = decay[last : last + 1]
                    totals_ref[pl.ds(total_row * state + n, 1), lanes] = value[last : last + 1]
                    turn_by = 1 if way > 0 else SUB - 1
                    decay_out[here] = jnp.where(seen(1), pltpu.roll(decay, turn_by, 0), 1.0)
                    state_out[here] = jnp.where(seen(1), pltpu.roll(value, turn_by, 0), 0.0)
            return carry

        lax.fori_loop(0, inner // LANE, columns, 0)


def forward_kernel(
    shape,
    step_ref,
    drive_ref,
    grad_ref,
    sel_ref,
    spots_ref,
    rates_ref,
    pre_decay_ref,
    pre_state_ref,
    entry_ref,
    conv_ref,
    gating_ref,
    grad_gated_ref,
    skip_ref,
    prior_ref,
    readout_grad_ref,
    gated_ref,
    grad_gating_ref,
    skip_grad_ref,
    state_ref,
    select_ref,
    sums_ref,
    scanned_ref,
):
    tiles, state, inner, cols, group = shape

    @pl.when(pl.program_id(0) == 0)
    def _():
        skip_grad_ref[...] = jnp.zeros_like(skip_grad_ref)
        for n in range(state):
            here = slice(n * SUB, (n + 1) * SUB)
            state_ref[here, :] = pre_state_ref[here, :] + pre_decay_ref[here, :] * entry_ref[n : n + 1, :]

    spread(sel_ref, spots_ref, select_ref)
    sums_ref[...] = jnp.zeros_like(sums_ref)

    def columns(c, carry):
        lanes = [at((c * cols + k) * LANE, LANE) for k in range(cols)]
        for first in range(0, state, group):
            spots = [(n, k) for n in range(group) for k in range(cols)]
            where = [(slice((first + n) * SUB, (first + n + 1) * SUB), lanes[k]) for n, k in spots]
            rates = [rates_ref[w] for w in where]

            def advance(i, states):
                here = at(i * SUB, SUB)
                step = [step_ref[here, l] for l in lanes]
                drive = [drive_ref[here, l] for l in lanes]
                grad = [grad_ref[here, l] for l in lanes]
                outs = [None] * cols
                new = []
                for n in range(group):
                    spot = slice((first + n) * LANE, (first + n + 1) * LANE)
                    inject = select_ref[here, spot]
                    readout = select_ref[here, (state + first + n) * LANE : (state + first + n + 1) * LANE]
                    total = None
                    for k in range(cols):
                        s = n * cols + k
                        decay = jnp.exp2(step[k] * rates[s])
                        fresh = decay * states[s] + drive[k] * inject
                        new.append(fresh)
                        part = readout * fresh
                        outs[k] = part if outs[k] is None else outs[k] + part
                        part = grad[k] * fresh
                        total = part if total is None else total + part
                    sums_ref[here, spot] += total
                    if n % 2 == 1:
                        pair = pl.ds(pl.multiple_of((i * state + first + n - 1) * SUB, 2 * SUB), 2 * SUB)
                        for k in range(cols):
                            prior_ref[pair, lanes[k]] = jnp.concatenate(
                                [states[(n - 1) * cols + k], states[n * cols + k]], 0
                            ).astype(bf16)
                for k in range(cols):
                    if first == 0:
                        scanned_ref[here, lanes[k]] = outs[k]
                    else:
                        scanned_ref[here, lanes[k]] += outs[k]
                return tuple(new)

            states = lax.fori_loop(0, tiles, advance, tuple(state_ref[w] for w in where), unroll=16)
            for s, w in enumerate(where):
                state_ref[w] = states[s]
        return carry

    lax.fori_loop(0, inner // (LANE * cols), columns, 0)
    gather_lanes(sums_ref, spots_ref, readout_grad_ref)

    def finish(c, carry):
        lanes = at(c * 2 * LANE, 2 * LANE)
        skip = skip_ref[:, lanes]

        def pair(i, total):
            here = at(i * 2 * SUB, 2 * SUB)
            conv = conv_ref[here, lanes].astype(f32)
            gating = gating_ref[here, lanes]
            sig = jax.nn.sigmoid(gating)
            gate = gating * sig
            scanned = scanned_ref[here, lanes] + skip * conv
            gated_ref[here, lanes] = (scanned * gate).astype(bf16)
            slope = sig + gate * (1.0 - sig)
            grad_gating_ref[here, lanes] = (grad_gated_ref[here, lanes] * scanned * slope).astype(bf16)
            product = grad_ref[here, lanes] * conv
            return total + product[:SUB] + product[SUB:]

        zero = jnp.zeros((SUB, 2 * LANE), f32)
        skip_grad_ref[:, lanes] += lax.fori_loop(0, tiles // 2, pair, zero, unroll=8)
        return carry

    lax.fori_loop(0, inner // (2 * LANE), finish, 0)


def backward_kernel(
    shape,
    scan_turns,
    regions,
    bits,
    phases,
    step_ref,
    drive_ref,
    grad_ref,
    sel_ref,
    spots_ref,
    rates_ref,
    begin_ref,
    prior_ref,
    conv_sum_ref,
    stream_ref,
    readout_grad_ref,
    step_back_ref,
    select_back_ref,
    taps_ref,
    skip_ref,
    flat_ref,
    grad_stream_ref,
    grad_pre_ref,
    grad_select_ref,
    rate_grad_ref,
    taps_grad_ref,
    edge_ref,
    early_ref,
    carry_ref,
    select_ref,
    sums_ref,
    through_ref,
    feed_ref,
    grad_conv_ref,
    inject_grad_ref,
    low_grad_ref,
    *refs,
):
    tiles, state, inner, cols, group, rank = shape
    block = tiles * SUB
    width = taps_ref.shape[0]
    halo = (width - 1) * SUB
    turn = pl.program_id(0)
    work = Reducer(
        regions.depth,
        bits,
        phases,
        1,
        lambda p, owner: regions.early_start(phases[p][0], owner) + phases[p][1],
        flat_ref,
        refs,
    )
    turns = scan_turns
    early = max(work.slots - turns, 0)
    for g in range(turns):

        @pl.when(turn == g)
        def _():
            if g == 0:
                work.greet()
            for t in range(0 if g == 0 else g + early, min(g + early + 1, work.slots)):
                work.run(t)

    @pl.when(pl.program_id(0) == 0)
    def _():
        rate_grad_ref[...] = jnp.zeros_like(rate_grad_ref)
        taps_grad_ref[...] = jnp.zeros_like(taps_grad_ref)
        grad_conv_ref[tiles * SUB :, :] = jnp.zeros((grad_conv_ref.shape[0] - tiles * SUB, inner), f32)
        carry_ref[...] = begin_ref[...]

    spread(sel_ref, spots_ref, select_ref)
    sums_ref[...] = jnp.zeros_like(sums_ref)

    def columns(c, carry):
        lanes = [at((c * cols + k) * LANE, LANE) for k in range(cols)]
        for first in range(0, state, group):
            spots = [(n, k) for n in range(group) for k in range(cols)]
            where = [(slice((first + n) * SUB, (first + n + 1) * SUB), lanes[k]) for n, k in spots]
            rates = [rates_ref[w] for w in where]

            def retreat(turn, carry):
                carries, rate_grads = carry
                i = tiles - 1 - turn
                here = at(i * SUB, SUB)
                step = [step_ref[here, l] for l in lanes]
                drive = [drive_ref[here, l] for l in lanes]
                grad = [grad_ref[here, l] for l in lanes]
                throughs = [None] * cols
                feeds = [None] * cols
                new = ([], [])
                for n in range(group):
                    spot = slice((first + n) * LANE, (first + n + 1) * LANE)
                    inject = select_ref[here, spot]
                    readout = select_ref[here, (state + first + n) * LANE : (state + first + n + 1) * LANE]
                    if n % 2 == 0:
                        pair = pl.ds(pl.multiple_of((i * state + first + n) * SUB, 2 * SUB), 2 * SUB)
                        pairs = [prior_ref[pair, lanes[k]].astype(f32) for k in range(cols)]
                    total = None
                    for k in range(cols):
                        s = n * cols + k
                        prior = pairs[k][(n % 2) * SUB : (n % 2 + 1) * SUB]
                        power = step[k] * rates[s]
                        adjoint = grad[k] * readout + carries[s]
                        back = jnp.exp2(power) * adjoint
                        through = back * prior * power
                        new[0].append(back)
                        new[1].append(rate_grads[s] + through)
                        throughs[k] = through if throughs[k] is None else throughs[k] + through
                        part = adjoint * inject
                        feeds[k] = part if feeds[k] is None else feeds[k] + part
                        part = adjoint * drive[k]
                        total = part if total is None else total + part
                    sums_ref[here, spot] += total
                for k in range(cols):
                    if first == 0:
                        through_ref[here, lanes[k]] = throughs[k]
                        feed_ref[here, lanes[k]] = feeds[k]
                    else:
                        through_ref[here, lanes[k]] += throughs[k]
                        feed_ref[here, lanes[k]] += feeds[k]
                return tuple(tuple(x) for x in new)

            start = tuple(tuple(ref[w] for w in where) for ref in (carry_ref, rate_grad_ref))
            carries, rate_grads = lax.fori_loop(0, tiles, retreat, start, unroll=8)
            for s, w in enumerate(where):
                carry_ref[w] = carries[s]
                rate_grad_ref[w] = rate_grads[s]
        return carry

    lax.fori_loop(0, inner // (LANE * cols), columns, 0)
    gather_lanes(sums_ref, spots_ref, inject_grad_ref)

    def steps(c, carry):
        lanes = at(c * 2 * LANE, 2 * LANE)

        def pair(i, total):
            here = at(i * 2 * SUB, 2 * SUB)
            step = step_ref[here, lanes]
            series = 1.0 + step * (-1.0 / 2 + step * (1.0 / 6 + step * (-1.0 / 24 + step * (1.0 / 120))))
            near = step < 0.06
            exact = (1.0 - jnp.exp2(step * -LOG2E)) / jnp.where(near, 1.0, step)
            ratio = jnp.where(near, series, exact)
            pre = ratio * (LN2 * through_ref[here, lanes] + drive_ref[here, lanes] * feed_ref[here, lanes])
            grad_pre_ref[here, lanes] = pre.astype(bf16)
            return total + pre[:SUB] + pre[SUB:]

        zero = jnp.zeros((SUB, 2 * LANE), f32)
        taps_grad_ref[(width + 1) * SUB :, lanes] += lax.fori_loop(0, tiles // 2, pair, zero, unroll=8)
        return carry

    lax.fori_loop(0, inner // (2 * LANE), steps, 0)
    lane = lax.broadcasted_iota(jnp.int32, (block, LANE), 1)
    across = (((1,), (1,)), ((), ()))
    low_grad_ref[:, :rank] = lax.dot_general(
        grad_pre_ref[...], step_back_ref[...], across, preferred_element_type=f32
    )
    grads = low_grad_ref[...]
    inject_grad = pltpu.roll(inject_grad_ref[...], rank, 1)
    readout_grad = pltpu.roll(readout_grad_ref[...], rank + state, 1)
    grads = jnp.where(lane < rank, grads, jnp.where(lane < rank + state, inject_grad, readout_grad))
    grads = jnp.where(lane < rank + 2 * state, grads, 0.0)
    grads = grads.astype(bf16)
    grad_select_ref[...] = grads

    through_ref[...] = lax.dot_general(
        grad_select_ref[:, : rank + 2 * state], select_back_ref[...], across, preferred_element_type=f32
    )

    def convs(c, carry):
        lanes = at(c * 2 * LANE, 2 * LANE)
        skip = skip_ref[:, lanes]

        def conv(i, carry):
            here = at(i * SUB, SUB)
            value = conv_sum_ref[here, lanes]
            sig = jax.nn.sigmoid(value)
            slope = sig * (1.0 + value * (1.0 - sig))
            out = grad_ref[here, lanes] * skip + step_ref[here, lanes] * feed_ref[here, lanes] + through_ref[here, lanes]
            grad_conv_ref[here, lanes] = out * slope
            return carry

        lax.fori_loop(0, tiles, conv, 0, unroll=8)
        taps = [jnp.broadcast_to(taps_ref[k : k + 1, lanes], (SUB, 2 * LANE)) for k in range(width)]

        def tap(i, totals):
            totals = list(totals)
            done = []
            for q in range(2):
                parts = [
                    grad_conv_ref[pl.ds(pl.multiple_of((2 * i + q + m) * SUB, SUB), SUB), lanes] for m in range(width)
                ]
                stream = stream_ref[pl.ds(pl.multiple_of((2 * i + q) * SUB, SUB), SUB), lanes]
                grad = taps[width - 1] * parts[0]
                totals[width - 1] = totals[width - 1] + parts[0] * stream
                totals[width] = totals[width] + parts[0]
                for m in range(1, width):
                    grad = grad + taps[width - 1 - m] * parts[m]
                    totals[width - 1 - m] = totals[width - 1 - m] + parts[m] * stream
                done.append(grad)
            grad_stream_ref[at(i * 2 * SUB, 2 * SUB), lanes] = jnp.concatenate(done, 0).astype(bf16)
            return tuple(totals)

        zero = jnp.zeros((SUB, 2 * LANE), f32)
        totals = lax.fori_loop(0, tiles // 2, tap, (zero,) * (width + 1), unroll=8)
        for k in range(width + 1):
            taps_grad_ref[k * SUB : (k + 1) * SUB, lanes] += totals[k]
        return carry

    lax.fori_loop(0, inner // (2 * LANE), convs, 0)

    @pl.when(pl.program_id(0) == 0)
    def _():
        edge_ref[halo:, :] = grad_conv_ref[block - halo : block, :]

    edge_ref[:halo, :] = grad_conv_ref[:halo, :]
    grad_conv_ref[block:, :] = grad_conv_ref[:halo, :]

    @pl.when(turn == turns - 1)
    def _():
        work.collect(early_ref)


def scan_shapes(rows, state, inner, tiles=16):
    tiles = min(tiles, rows // SUB)
    count = rows // (SUB * tiles)
    return tiles, count


def summary_call(stream, gating, grad_gated, head, taps, bias, select_in, step_in, step_bias, spots, rates):
    rows, inner = stream.shape
    state = rates.shape[0] // SUB
    tiles, count = scan_shapes(rows, state, inner)
    halo = head.shape[0]
    wide = pl.BlockSpec((tiles * SUB, inner), lambda t: (t, 0))
    thin = pl.BlockSpec((tiles * SUB, LANE), lambda t: (t, 0))
    whole = pl.BlockSpec((state * SUB, inner), lambda t: (0, 0))
    total = pl.BlockSpec((3 * state, inner), lambda t: (0, 0))
    shape = (tiles, state, inner, 2, 4)
    big = jax.ShapeDtypeStruct((state * SUB, inner), f32)
    full = jax.ShapeDtypeStruct((rows, inner), f32)
    slim = jax.ShapeDtypeStruct((rows, LANE), bf16)

    def fixed(x):
        return pl.BlockSpec(x.shape, lambda t: (0, 0), pipeline_mode=pl.Buffered(1))

    constants = (head, taps, bias, select_in, step_in, step_bias, spots, rates)
    return pl.pallas_call(
        functools.partial(summary_kernel, shape),
        name="scan_summary",
        grid=(count,),
        in_specs=[wide, wide, wide] + [fixed(x) for x in constants],
        out_specs=[wide] * 5 + [thin] * 2 + [whole] * 4 + [total],
        out_shape=[full, jax.ShapeDtypeStruct((rows, inner), bf16), full, full, full, slim, slim]
        + [big] * 4
        + [jax.ShapeDtypeStruct((3 * state, inner), f32)],
        scratch_shapes=[pltpu.VMEM((state * SUB, inner), f32)] * 3
        + [
            pltpu.VMEM((tiles * SUB, 2 * state * LANE), f32),
            pltpu.VMEM((halo + tiles * SUB, inner), f32),
            pltpu.VMEM((tiles * SUB, LANE), f32),
        ],
        compiler_params=pltpu.CompilerParams(vmem_limit_bytes=VMEM_BYTES),
    )(stream, gating, grad_gated, *constants)


def forward_call(step, drive, grad, sel, spots, rates, pre_decay, pre_state, entry, conv, gating, grad_gated, skip):
    rows, inner = step.shape
    state = rates.shape[0] // SUB
    tiles, count = scan_shapes(rows, state, inner)
    wide = pl.BlockSpec((tiles * SUB, inner), lambda t: (t, 0))
    table = pl.BlockSpec(spots.shape, lambda t: (0, 0))
    thin = pl.BlockSpec((tiles * SUB, sel.shape[1]), lambda t: (t, 0))
    whole = pl.BlockSpec((state * SUB, inner), lambda t: (0, 0), pipeline_mode=pl.Buffered(1))
    line = pl.BlockSpec((1, inner), lambda t: (0, 0))
    short = pl.BlockSpec((state, inner), lambda t: (0, 0))
    shape = (tiles, state, inner, 2, 8)
    return pl.pallas_call(
        functools.partial(forward_kernel, shape),
        name="scan_forward",
        grid=(count,),
        in_specs=[wide, wide, wide, thin, table, whole, whole, whole, short, wide, wide, wide, line],
        out_specs=[
            pl.BlockSpec((tiles * state * SUB, inner), lambda t: (t, 0)),
            pl.BlockSpec((tiles * SUB, LANE), lambda t: (t, 0)),
            wide,
            wide,
            pl.BlockSpec((SUB, inner), lambda t: (0, 0)),
        ],
        out_shape=[
            jax.ShapeDtypeStruct((rows * state, inner), bf16),
            jax.ShapeDtypeStruct((rows, LANE), f32),
            jax.ShapeDtypeStruct((rows, inner), bf16),
            jax.ShapeDtypeStruct((rows, inner), bf16),
            jax.ShapeDtypeStruct((SUB, inner), f32),
        ],
        scratch_shapes=[pltpu.VMEM((state * SUB, inner), f32)]
        + [
            pltpu.VMEM((tiles * SUB, 2 * state * LANE), f32),
            pltpu.VMEM((tiles * SUB, state * LANE), f32),
            pltpu.VMEM((tiles * SUB, inner), f32),
        ],
        compiler_params=pltpu.CompilerParams(vmem_limit_bytes=VMEM_BYTES),
    )(step, drive, grad, sel, spots, rates, pre_decay, pre_state, entry, conv, gating, grad_gated, skip)


def backward_call(step, drive, grad, sel, spots, rates, begin, prior, conv_sum, stream, readout_grad, step_back, select_back, taps, skip, flat, regions, rank):
    rows, inner = step.shape
    state = rates.shape[0] // SUB
    tiles, count = scan_shapes(rows, state, inner, 8)
    bits = regions.count.bit_length() - 1
    phases = regions.early_phases()

    def back(t):
        return (count - 1 - t, 0)

    wide = pl.BlockSpec((tiles * SUB, inner), back)
    table = pl.BlockSpec(spots.shape, lambda t: (0, 0), pipeline_mode=pl.Buffered(1))
    thin = pl.BlockSpec((tiles * SUB, sel.shape[1]), back)
    whole = pl.BlockSpec((state * SUB, inner), lambda t: (0, 0), pipeline_mode=pl.Buffered(1))
    narrow = pl.BlockSpec((tiles * SUB, LANE), back)
    width = taps.shape[0]
    halo = (width - 1) * SUB

    def fixed(x):
        return pl.BlockSpec(x.shape, lambda t: (0, 0), pipeline_mode=pl.Buffered(1))

    shape = (tiles, state, inner, 2, 4, rank)
    return pl.pallas_call(
        functools.partial(backward_kernel, shape, count, regions, bits, phases),
        name="scan_backward",
        grid=(count,),
        in_specs=[wide, wide, wide, thin, table, whole, whole]
        + [pl.BlockSpec((tiles * state * SUB, inner), back), wide, wide, narrow]
        + [fixed(step_back), fixed(select_back), fixed(taps), fixed(skip)]
        + [pl.BlockSpec(memory_space=pl.ANY)],
        out_specs=[
            wide,
            wide,
            narrow,
            pl.BlockSpec((state * SUB, inner), lambda t: (0, 0)),
            pl.BlockSpec(((width + 2) * SUB, inner), lambda t: (0, 0)),
            pl.BlockSpec((2 * halo, inner), lambda t: (0, 0)),
            pl.BlockSpec((regions.slot, SUB, LANE), lambda t: (0, 0, 0)),
        ],
        out_shape=[
            jax.ShapeDtypeStruct((rows, inner), bf16),
            jax.ShapeDtypeStruct((rows, inner), bf16),
            jax.ShapeDtypeStruct((rows, LANE), bf16),
            jax.ShapeDtypeStruct((state * SUB, inner), f32),
            jax.ShapeDtypeStruct(((width + 2) * SUB, inner), f32),
            jax.ShapeDtypeStruct((2 * halo, inner), f32),
            jax.ShapeDtypeStruct((regions.slot, SUB, LANE), f32),
        ],
        scratch_shapes=[pltpu.VMEM((state * SUB, inner), f32)]
        + [
            pltpu.VMEM((tiles * SUB, 2 * state * LANE), f32),
            pltpu.VMEM((tiles * SUB, state * LANE), f32),
            pltpu.VMEM((tiles * SUB, inner), f32),
            pltpu.VMEM((tiles * SUB, inner), f32),
            pltpu.VMEM((tiles * SUB + halo, inner), f32),
            pltpu.VMEM((tiles * SUB, LANE), f32),
            pltpu.VMEM((tiles * SUB, LANE), f32),
        ]
        + Reducer.scratch(regions.depth, bits, phases),
        compiler_params=pltpu.CompilerParams(
            vmem_limit_bytes=62 * 2**20, collective_id=2, has_side_effects=True
        ),
    )(step, drive, grad, sel, spots, rates, begin, prior, conv_sum, stream, readout_grad, step_back, select_back, taps, skip, flat)


def turn_tiles(tiles):
    row = lax.broadcasted_iota(jnp.int32, (SUB, LANE), 0)
    for bit in (1, 2, 4):
        upper = (row // bit) % 2 == 1
        new = list(tiles)
        for a in range(SUB):
            if a & bit == 0:
                b = a + bit
                new[a] = jnp.where(upper, pltpu.roll(tiles[b], bit, 0), tiles[a])
                new[b] = jnp.where(upper, tiles[b], pltpu.roll(tiles[a], SUB - bit, 0))
        tiles = new
    return tiles


def pack_columns(src_ref, used, out_ref):
    part = LANE - used
    rows = src_ref.shape[0] // 4
    lane = lax.broadcasted_iota(jnp.int32, (SUB, LANE), 1)
    flat = out_ref

    def one(g, carry):
        quads = [src_ref[pl.ds(g * 4 * SUB + q, SUB, stride=4), :] for q in range(4)]
        for m in range(3):
            first = quads[m] if m == 0 else pltpu.roll(quads[m], LANE - m * part, 1)
            second = pltpu.roll(quads[m + 1], used - m * part, 1)
            flat[pl.ds(g * 3 * SUB + m, SUB, stride=3), :] = jnp.where(lane < used - m * part, first, second)
        return carry

    lax.fori_loop(0, rows // SUB, one, 0, unroll=4)


def row_tile(src_ref, r, q):
    return jnp.concatenate(
        [src_ref[r : r + 1, (q * SUB + a) * LANE : (q * SUB + a + 1) * LANE] for a in range(SUB)], 0
    )


def product_kernel(steps, shapes, used, *refs):
    if used:
        out_ref, held_ref, packed_ref = refs[-3:]
    else:
        out_ref, held_ref = refs[-2:]
    contract = (((0,), (0,)), ((), ()))
    step = pl.program_id(0)

    def lay(src_ref, first, rows, base, per, q):
        def one(r, carry):
            tiles = [
                src_ref[at(r * SUB, SUB), (first + a) * LANE : (first + a + 1) * LANE] for a in range(SUB)
            ]
            for b, tile in enumerate(turn_tiles(tiles)):
                out_ref[base + (r * SUB + b) * per + q] = tile
            return carry

        lax.fori_loop(0, rows // SUB, one, 0, unroll=rows // SUB)

    for turn, (rows, width) in enumerate(shapes):
        left_ref, right_ref = refs[2 * turn : 2 * turn + 2]
        per = width // ROW

        @pl.when(step // steps == turn)
        def _():
            for q in range(per):
                held_ref[q, :rows] = lax.dot_general(
                    left_ref[...], right_ref[:, q * ROW : (q + 1) * ROW], contract, preferred_element_type=f32
                )
                lay(held_ref.at[q], 0, rows, 0, per, q)

    if not used:
        return
    wide_ref, *thin_refs = refs[2 * len(shapes) : -3]
    tiles = packed_ref.shape[0] // SUB

    @pl.when(step == steps * len(shapes))
    def _():
        pack_columns(wide_ref, used, packed_ref)

        def one(i, carry):
            out_ref[i] = packed_ref[at(i * SUB, SUB), :]
            return carry

        out_ref[...] = jnp.zeros_like(out_ref)
        lax.fori_loop(0, tiles, one, 0, unroll=8)
        base = tiles
        for ref in thin_refs:
            rows, per = ref.shape[0], ref.shape[1] // ROW
            for q in range(per):
                if rows % SUB == 0:
                    lay(ref, q * SUB, rows, base, per, q)
                else:
                    for r in range(rows):
                        out_ref[base + r * per + q] = row_tile(ref, r, q)
            base += rows * per


def product_call(*pairs, small=None):
    steps = 4
    shapes = [(left.shape[1] // steps, right.shape[1]) for left, right in pairs]
    size = shapes[0][0] * shapes[0][1] // ROW

    def block(k):
        return lambda t: (0, jnp.clip(t - k * steps, 0, steps - 1))

    specs = []
    for k, (left, right) in enumerate(pairs):
        specs.append(pl.BlockSpec((left.shape[0], left.shape[1] // steps), block(k)))
        specs.append(pl.BlockSpec(right.shape, lambda t: (0, 0), pipeline_mode=pl.Buffered(1)))
    args = [x for pair in pairs for x in pair]
    scratch = [pltpu.VMEM((shapes[0][1] // ROW, max(rows for rows, _ in shapes), ROW), f32)]
    used, extra = 0, 0
    if small is not None:
        wide, thin, used = small
        extra = 1
        scratch.append(pltpu.VMEM((wide.shape[0] * used // LANE, LANE), f32))
        for x in (wide,) + thin:
            specs.append(pl.BlockSpec(x.shape, lambda t: (0, 0), pipeline_mode=pl.Buffered(1)))
            args.append(x)
    grid = steps * len(pairs) + extra
    return pl.pallas_call(
        functools.partial(product_kernel, steps, shapes, used),
        name="flat_product",
        grid=(grid,),
        in_specs=specs,
        out_specs=pl.BlockSpec((size, SUB, LANE), lambda t: (t, 0, 0)),
        out_shape=jax.ShapeDtypeStruct((size * grid, SUB, LANE), f32),
        scratch_shapes=scratch,
        compiler_params=pltpu.CompilerParams(vmem_limit_bytes=VMEM_BYTES),
    )(*args)


class Regions:
    def __init__(self, depth, count, span, gain, in_shape, small, out_shape, small_parts):
        self.depth, self.count, self.span = depth, count, span
        self.per = in_shape[1] // ROW
        self.in_rows = in_shape[0]
        self.in_base = gain
        self.small_base = gain + in_shape[0] * self.per
        self.out_base = self.small_base + small
        self.out_rows = out_shape[0] * out_shape[1] // ROW
        self.need = (span - 1) // ROW + 2
        self.lines = min((self.need + self.per - 2) // self.per + 1, self.in_rows)
        self.half = self.lines * self.per // 2
        self.pieces = -(-self.need // self.half)
        self.slot = self.pieces * self.half
        self.line_rows = min(-(-(self.lines + 15) // 16) * 16, self.in_rows)
        self.slot_rows = min(-(-(self.slot + 15) // 16) * 16, self.out_rows)
        self.small_parts = small_parts
        self.small_tiles = sum(length for _, _, length in small_parts)

    def base(self, owner):
        return owner * self.span // ROW

    def in_first(self, owner):
        line = lax.max(self.base(owner) - self.in_base, 0) // self.per
        return lax.min(line, self.in_rows - self.lines)

    def out_first(self, owner):
        return lax.max(lax.min(self.base(owner) - self.out_base, self.out_rows - self.slot), 0)

    def meets_in(self, z):
        return z * self.count * self.span // ROW < self.small_base

    def meets_out(self, z):
        return ((z + 1) * self.count * self.span - 1) // ROW >= self.out_base

    def early_start(self, z, owner):
        if not self.meets_out(z):
            return self.in_first(owner) * (self.per // 2)
        out = self.in_rows * self.per // 2 + self.out_first(owner)
        if not self.meets_in(z):
            return out
        inside = self.base(owner) < self.small_base
        return jnp.where(inside, self.in_first(owner) * (self.per // 2), out)

    def early_phases(self):
        phases = []
        cut = 2 if self.half % 4 == 0 else 1
        size = self.half // cut
        for z in range(self.depth):
            for piece in range((self.pieces if self.meets_out(z) else 1) * cut):
                phases.append((z, piece * size, size))
        return sorted(phases, key=lambda phase: -max(self.depth - 1 - phase[0], phase[0]))

    def late_phases(self):
        cut = 2 if self.half % 4 == 0 else 1
        size = self.half // cut
        owners = [k for k in range(self.depth * self.count) if self.meets_small(k)]
        goals = {k // self.count for k in owners}
        assert len(goals) == 1
        goal = goals.pop()
        small = [(goal, None, size)] * -(-self.small_tiles // (self.count * size))
        stream = [(z, piece * size, size) for z in range(self.depth) if self.meets_in(z) for piece in range(cut)]
        return small, stream, [k % self.count for k in owners]

    def meets_small(self, owner):
        base = self.base(owner)
        return base < self.out_base and base + self.need > self.small_base

    def late_start(self, phases, p, owner):
        goal, offset, size = phases[p]
        if offset is None:
            return self.in_rows * self.per // 2 + (p * self.count + owner % self.count) * size
        return self.in_first(owner) * (self.per // 2) + offset


class Reducer:
    def __init__(self, depth, bits, phases, gap, start, src_ref, refs):
        self.depth, self.bits, self.phases = depth, bits, phases
        self.start, self.src = start, src_ref
        self.n = bits - 1
        self.half = phases[0][2] // 2
        self.acc, self.first = refs[:2]
        self.bit_recvs = refs[2 : 2 + self.n]
        self.down, self.up = refs[2 + self.n : 4 + self.n]
        (
            self.local_sem,
            self.core_send,
            self.core_recv,
            self.bit_send,
            self.bit_recv,
            self.z_send,
            self.z_recv,
        ) = refs[4 + self.n : 11 + self.n]
        self.blk, self.z = lax.axis_index("blk"), lax.axis_index("batch")
        self.mine = [(self.blk // 2**b) % 2 for b in range(bits)]
        self.partner = [self.blk + (1 - 2 * self.mine[b]) * 2**b for b in range(bits)]
        self.last = self.n + depth - 1
        self.slot = [0] + [1 + 2 * s for s in range(self.n)]
        self.slot += [max(2 * self.n, 1) + gap * u for u in range(depth - 1)]
        self.done = self.slot[-1] + 1
        hops = [max(depth - 1 - goal, goal) for goal, _, _ in phases]
        self.slots = max(p + self.slot[self.n + h] + 1 for p, h in enumerate(hops))

    @staticmethod
    def scratch(depth, bits, phases):
        n, count, size = bits - 1, len(phases), phases[0][2]
        tile = (SUB, LANE)
        dma = pltpu.SemaphoreType.DMA
        return (
            [pltpu.VMEM((count,) + (2,) * n + (size,) + tile, f32)] * 2
            + [pltpu.VMEM((count, 2) + (2,) * (n - 1 - s) + (size // 2,) + tile, f32) for s in range(n)]
            + [pltpu.VMEM((count, size) + tile, f32)] * 2
            + [dma((count,))] * 3
            + [dma((max(count * n, 1),))] * 2
            + [dma((count,)), dma((2 * count,))]
        )

    def greet(self):
        barrier = pltpu.get_barrier_semaphore()
        peers = ("blk", self.blk, 2**self.bits), ("batch", self.z, self.depth)
        for axis, index, count in peers:
            for by in range(1, count):
                other = lax.rem(index + by, count)
                pl.semaphore_signal(barrier, inc=1, device_id={axis: other}, device_id_type=MESH)
        pl.semaphore_wait(barrier, 2**self.bits + self.depth - 2)

    def digits(self, r):
        return tuple((r // 2**i) % 2 for i in reversed(range(self.n)))

    def window(self, p, r, core):
        goal, offset, size = self.phases[p]
        owner = goal * 2**self.bits + 2 * r + core
        return pl.ds(self.start(p, owner), size)

    def core_copies(self, p, own=False):
        copies = []
        for r in range(2**self.n):
            where = (p,) + self.digits(r)
            if own:
                copies.append(
                    pltpu.make_async_copy(
                        self.src.at[self.window(p, r, self.mine[0])], self.acc.at[where], self.local_sem.at[p]
                    )
                )
            else:
                copies.append(
                    pltpu.make_async_remote_copy(
                        src_ref=self.src.at[self.window(p, r, 1 - self.mine[0])],
                        dst_ref=self.first.at[where],
                        send_sem=self.core_send.at[p],
                        recv_sem=self.core_recv.at[p],
                        device_id={"blk": self.partner[0]},
                        device_id_type=MESH,
                    )
                )
        return copies

    def order(self, part):
        return list(range(self.n)) if part == 0 else list(reversed(range(self.n)))

    def place(self, p, part, done, pick):
        spots = [slice(None)] * self.n
        for i in self.order(part)[:done]:
            spots[i] = self.mine[i + 1]
        spots[self.order(part)[done]] = pick
        return (p,) + tuple(reversed(spots)) + (slice(part * self.half, (part + 1) * self.half),)

    def bit_copies(self, p, s):
        copies = []
        for part in range(2):
            i = self.order(part)[s]
            spot = p * self.n + s
            copies.append(
                pltpu.make_async_remote_copy(
                    src_ref=self.acc.at[self.place(p, part, s, 1 - self.mine[i + 1])],
                    dst_ref=self.bit_recvs[s].at[p, part],
                    send_sem=self.bit_send.at[spot],
                    recv_sem=self.bit_recv.at[spot],
                    device_id={"blk": self.partner[i + 1]},
                    device_id_type=MESH,
                )
            )
        return copies

    def settled(self, p):
        return (p,) + tuple(reversed([self.mine[i + 1] for i in range(self.n)]))

    def z_copy(self, p, up):
        return pltpu.make_async_remote_copy(
            src_ref=self.acc.at[self.settled(p)],
            dst_ref=(self.up if up else self.down).at[p],
            send_sem=self.z_send.at[p],
            recv_sem=self.z_recv.at[2 * p + up],
            device_id={"batch": lax.rem(self.z + (1 if up else self.depth - 1), self.depth)},
            device_id_type=MESH,
        )

    def add(self, dst, dst_at, src, src_at):
        dst[dst_at] += src[src_at]

    def all_core(self, p):
        return pltpu.make_async_remote_copy(
            src_ref=self.first.at[p],
            dst_ref=self.first.at[p],
            send_sem=self.core_send.at[p],
            recv_sem=self.core_recv.at[p],
            device_id={"blk": self.partner[0]},
            device_id_type=MESH,
        )

    def all_bit(self, p, s):
        return pltpu.make_async_remote_copy(
            src_ref=self.bit_recvs[s].at[p],
            dst_ref=self.bit_recvs[s].at[p],
            send_sem=self.bit_send.at[p * self.n + s],
            recv_sem=self.bit_recv.at[p * self.n + s],
            device_id={"blk": self.partner[0]},
            device_id_type=MESH,
        )

    def finish_core(self, p):
        pltpu.make_async_copy(self.first.at[p], self.acc.at[p], self.local_sem.at[p]).wait()
        self.all_core(p).wait_recv()
        for r in range(2**self.n):
            where = (p,) + self.digits(r)
            self.add(self.acc, where, self.first, where)

    def finish_bit(self, p, s):
        self.all_bit(p, s).wait_recv()
        for part in range(2):
            kept = self.place(p, part, s, self.mine[self.order(part)[s] + 1])
            free = [i for i in range(1, 1 + self.n) if isinstance(kept[i], slice)]
            for r in range(2 ** len(free)):
                chosen = tuple((r // 2**j) % 2 for j in reversed(range(len(free))))
                to = list(kept)
                for i, v in zip(free, chosen):
                    to[i] = v
                self.add(self.acc, tuple(to), self.bit_recvs[s], (p, part) + chosen)

    def take(self, p, up):
        self.z_copy(p, up).wait_recv()
        self.add(self.acc, self.settled(p), self.up if up else self.down, p)

    def z_moves(self, p, u):
        goal = self.phases[p][0]
        moves = []
        if self.depth - 1 - u > goal:
            moves.append((self.depth - 1 - u, False))
        if u < goal:
            moves.append((u, True))
        return moves

    def act(self, p, stage):
        n = self.n
        if stage == 0:
            for copy in self.core_copies(p) + self.core_copies(p, True):
                copy.start()
            return
        if stage == 1:
            self.finish_core(p)
        elif stage <= n + 1:
            self.finish_bit(p, stage - 2)
        if stage <= n:
            for copy in self.bit_copies(p, stage - 1):
                copy.start()
            return
        u = stage - n - 1
        for mover, up in self.z_moves(p, u):

            @pl.when(self.z == mover)
            def _():
                if u > 0:
                    self.take(p, up)
                self.z_copy(p, up).start()

    def run(self, t):
        for stage in reversed(range(self.last + 1)):
            p = t - self.slot[stage]
            if 0 <= p < len(self.phases):
                self.act(p, stage)

    def finish(self, p):
        goal = self.phases[p][0]
        if goal < self.depth - 1:
            self.take(p, False)
        if goal > 0:
            self.take(p, True)

    def collect(self, out_ref, first=0):
        for p, (goal, offset, size) in list(enumerate(self.phases))[first:]:

            @pl.when(self.z == goal)
            def _():
                self.finish(p)
                out_ref[offset : offset + size] = self.acc[self.settled(p)]

        for p in range(len(self.phases)):
            self.all_core(p).wait_send()
            for s in range(self.n):
                self.all_bit(p, s).wait_send()
            for u in range(self.depth - 1):
                for mover, up in self.z_moves(p, u):

                    @pl.when(self.z == mover)
                    def _():
                        self.z_copy(p, up).wait_send()


def put_restored(value, turn_ref, out_ref, block):
    rows, width = value.shape
    tiles = rows // SUB
    step = out_ref.shape[0] // SUB
    for a in range(width // LANE):
        turn_ref[a] = value[:, a * LANE : (a + 1) * LANE]
    for j in range(SUB):
        here = pl.ds(pl.multiple_of(j * step + block * tiles, tiles), tiles)
        for a in range(width // LANE):
            part = turn_ref[a, pl.ds(j, tiles, stride=SUB), :]
            out_ref[here, a * LANE : (a + 1) * LANE] = part.astype(bf16)


def late_kernel(
    regions,
    bits,
    small_phases,
    stream_phases,
    targets,
    blocks,
    flat_ref,
    early_ref,
    gain_ref,
    *refs,
):
    depth, span = regions.depth, regions.span
    sources, weights, refs = refs[:7], refs[7:14], refs[14:]
    window_ref, totals_ref, result_ref, grad_ref, params_ref = refs[:5]
    held, refs = refs[5:12], refs[12:]
    gate_back, stream_back, in_w, token, cot, gated, out_w = held
    late_ref, small_ref, wide_window, turn_ref, gain_sum, sums, ring = refs[:7]
    columns_ref, packed_ref, small_params = refs[7:10]
    load_sem, ring_send, ring_recv, small_send, small_recv = refs[10:15]
    phases = small_phases + stream_phases
    few = len(small_phases)
    work = Reducer(
        depth, bits, phases, 2, lambda p, owner: regions.late_start(phases, p, owner), flat_ref, refs[15:]
    )
    blk, z = work.blk, work.z
    inner = gated.shape[2]
    size = token.shape[0] // blocks
    loads = [
        pltpu.make_async_copy(src, dst, load_sem.at[i])
        for i, (src, dst) in enumerate(zip(sources, held))
        if src.shape == dst.shape
    ]

    def pieces(t):
        here = pl.ds(pl.multiple_of(t * size, size), size)
        return [
            pltpu.make_async_copy(src.at[here], dst.at[t % 2], load_sem.at[len(held) + 2 * i + t % 2])
            for i, (src, dst) in enumerate(zip(sources, held))
            if src.shape != dst.shape
        ]

    for load in loads + pieces(0):
        load.start()
    work.greet()
    gain_sum[...] = jnp.zeros_like(gain_sum)
    across = (((1,), (1,)), ((), ()))

    goal = small_phases[0][0]
    owner = z * 2**bits + blk
    base = regions.base(owner)
    margin = (wide_window.shape[0] - regions.need) // 2

    def spread_rows(src_ref, first, rows, put):
        per = src_ref.shape[1] // ROW

        def one(r, carry):
            here = pl.ds(pl.multiple_of(first + r * 2 * SUB, 2 * SUB), 2 * SUB)
            for q in range(per):
                both = src_ref[here, q * ROW : (q + 1) * ROW].astype(f32)
                for side in range(2):
                    half = both[side * SUB : (side + 1) * SUB]
                    tiles = turn_tiles([half[:, a * LANE : (a + 1) * LANE] for a in range(SUB)])
                    for b, tile in enumerate(tiles):
                        put((first + r * 2 * SUB + side * SUB + b) * per + q, tile)
            return carry

        lax.fori_loop(0, rows // (2 * SUB), one, 0)

    def lay_params():
        conv_w, conv_b, select_w, step_w, step_b, rate, skip = weights
        used = select_w.shape[1]
        part = columns_ref.shape[0]
        for c in range(select_w.shape[0] // part):
            columns_ref[:, :used] = select_w[c * part : (c + 1) * part].astype(f32)
            pack_columns(columns_ref, used, packed_ref.at[c * part * used // LANE : (c + 1) * part * used // LANE])
        spot = 0
        for ref in (conv_w, conv_b, select_w, step_w, step_b, rate, skip):
            count = ref.shape[0] * ref.shape[1] // ROW
            if ref is select_w:

                def one(i, carry, spot=spot):
                    small_params[spot + i] = packed_ref[at(i * SUB, SUB), :]
                    return carry

                lax.fori_loop(0, count, one, 0, unroll=8)
            elif ref is step_w:

                def put(i, tile, spot=spot):
                    small_params[spot + i] = tile

                spread_rows(step_w, 0, step_w.shape[0], put)
            else:
                per = ref.shape[1] // ROW
                for i in range(count):
                    small_params[spot + i] = row_tile(ref, i // per, i % per)
            spot += count

    def place_params():
        params_ref[...] = jnp.zeros_like(params_ref)
        wide_window[...] = jnp.zeros_like(wide_window)

        @pl.when(base < regions.small_base)
        def _():
            first = regions.in_first(owner) // (2 * SUB) * (2 * SUB)
            first = lax.min(first, regions.in_rows - regions.line_rows)

            def put(i, tile):
                wide_window[regions.in_base + i - base + margin] = tile

            spread_rows(in_w, first, regions.line_rows, put)

        @pl.when(base >= regions.small_base)
        def _():
            first = regions.out_first(owner) // (2 * SUB) * (2 * SUB)
            first = lax.min(first, regions.out_rows - regions.slot_rows)

            def put(i, tile):
                wide_window[regions.out_base + i - base + margin] = tile

            spread_rows(out_w, first, regions.slot_rows, put)

        @pl.when((base < regions.out_base) & (base + regions.need > regions.small_base))
        def _():
            def line(i, carry):
                row = base + i
                tile = lax.max(lax.min(row - regions.small_base, small_params.shape[0] - 1), 0)
                here = (row >= regions.small_base) & (row < regions.out_base)
                wide_window[margin + i] = jnp.where(here, small_params[tile], wide_window[margin + i])
                return carry

            lax.fori_loop(0, regions.need, line, 0, unroll=2)

        params_ref[...] = wide_window[margin : margin + regions.need]

        @pl.when(base < regions.in_base)
        def _():
            params_ref[0] = row_tile(gain_ref, 0, 0)

    def hand_out(p, target):
        return pltpu.make_async_remote_copy(
            src_ref=small_ref.at[p, blk],
            dst_ref=small_ref.at[p, blk],
            send_sem=small_send.at[p, targets.index(target)],
            recv_sem=small_recv.at[p, blk],
            device_id={"blk": target},
            device_id_type=MESH,
        )

    def give_small(p):
        @pl.when(z == goal)
        def _():
            work.finish(p)
            small_ref[p, blk] = work.acc[work.settled(p)]
            for target in targets:

                @pl.when(blk != target)
                def _():
                    hand_out(p, target).start()

    def slot(t, carry):
        for k in range(work.slots):

            @pl.when(t == k)
            def _():
                if 0 <= k - work.done < few:
                    give_small(k - work.done)
                work.run(k)
                if k == 0:
                    for load in loads:
                        load.wait()

        @pl.when(t < blocks)
        def _():
            here = pl.ds(pl.multiple_of(t * size, size), size)
            part = t % 2
            for piece in pieces(t):
                piece.wait()

            @pl.when(t + 1 < blocks)
            def _():
                for piece in pieces(t + 1):
                    piece.start()

            source = token[here, :].astype(f32)
            output = jnp.dot(gated[part], out_w[...], preferred_element_type=f32)
            put_restored(source + output, turn_ref, result_ref, t)
            grad_normed = lax.dot_general(
                stream_back[part], in_w[:, :inner], across, preferred_element_type=f32
            ) + lax.dot_general(gate_back[part], in_w[:, inner:], across, preferred_element_type=f32)
            scale = lax.rsqrt(jnp.mean(source * source, axis=-1, keepdims=True) + EPS)
            scaled = source * scale
            product = grad_normed * scaled
            gain_sum[...] += jnp.sum(product.reshape(size // SUB, SUB, product.shape[1]), 0)
            weighted = grad_normed * gain_ref[...]
            mean = jnp.mean(weighted * source, axis=-1, keepdims=True)
            back = scale * weighted - source * (scale * scale * scale) * mean + cot[here, :].astype(f32)
            put_restored(back, turn_ref, grad_ref, t)

        @pl.when(t == blocks)
        def _():
            lay_params()

        @pl.when(t == blocks + 1)
        def _():
            place_params()

        return carry

    lax.fori_loop(0, max(work.slots, blocks + 2), slot, 0)
    for p in range(few):
        if p + work.done >= work.slots:
            give_small(p)
    late_ref[...] = jnp.zeros_like(late_ref)
    work.collect(late_ref, few)
    for target in targets:
        for p in range(few):

            @pl.when((z == goal) & (blk != target))
            def _():
                hand_out(p, target).wait_send()

            for source in range(2**bits):
                if source != target:

                    @pl.when((z == goal) & (blk == target))
                    def _():
                        pltpu.make_async_remote_copy(
                            src_ref=small_ref.at[p, source],
                            dst_ref=small_ref.at[p, source],
                            send_sem=small_send.at[p, 0],
                            recv_sem=small_recv.at[p, source],
                            device_id={"blk": source},
                            device_id_type=MESH,
                        ).wait_recv()

    inside = lax.broadcasted_iota(jnp.int32, (SUB, LANE), 0) * LANE + lax.broadcasted_iota(
        jnp.int32, (SUB, LANE), 1
    )
    sums[blk, 0] = jnp.zeros((SUB, LANE), f32)
    gain = jnp.sum(gain_sum[...], 0, keepdims=True)
    for a in range(SUB):
        sums[blk, 1, a : a + 1, :] = gain[:, a * LANE : (a + 1) * LANE]
    half = regions.per // 2
    wide_window[...] = jnp.zeros_like(wide_window)

    def own(value, row):
        spot = inside + (row * ROW - owner * span)
        return jnp.where((spot >= 0) & (spot < span), value, 0.0)

    def keep(total, value, row):
        wide_window[row - base + margin] = value
        part = own(value, row)
        return total + part * part

    zero = jnp.zeros((SUB, LANE), f32)

    @pl.when(base < regions.small_base)
    def _():
        def line(d, total):
            row = regions.in_base + (regions.in_first(owner) + d) * regions.per
            for q in range(half):
                total = keep(total, late_ref[d * half + q], row + q)
                total = keep(total, early_ref[d * half + q], row + half + q)
            return total

        sums[blk, 0] += lax.fori_loop(0, regions.lines, line, zero, unroll=2)

    @pl.when(base >= regions.small_base)
    def _():
        def line(i, total):
            return keep(total, early_ref[i], regions.out_base + regions.out_first(owner) + i)

        sums[blk, 0] += lax.fori_loop(0, regions.slot, line, zero, unroll=4)

    size = small_phases[0][2]

    @pl.when((base < regions.out_base) & (base + regions.need > regions.small_base))
    def _():
        def line(i, total):
            row = base + i
            tile = 0
            for first, spot, length in regions.small_parts:
                offset = row - regions.small_base - first
                tile = jnp.where(offset >= 0, spot + lax.min(offset, length - 1), tile)
            lot = tile // size
            value = small_ref[lot // 2**bits, lot % 2**bits, tile % size]
            here = (row >= regions.small_base) & (row < regions.out_base)
            wide_window[margin + i] = jnp.where(here, value, wide_window[margin + i])
            part = jnp.where(here, own(value, row), 0.0)
            return total + part * part

        sums[blk, 0] += lax.fori_loop(0, regions.need, line, zero, unroll=2)

    window_ref[...] = wide_window[margin : margin + regions.need]

    def everyone(slots, axis, index, count, first_sem):
        copies = [
            pltpu.make_async_remote_copy(
                src_ref=slots.at[index],
                dst_ref=slots.at[index],
                send_sem=ring_send.at[first_sem + by],
                recv_sem=ring_recv.at[first_sem + by],
                device_id={axis: lax.rem(index + by, count)},
                device_id_type=MESH,
            )
            for by in range(1, count)
        ]
        for copy in copies:
            copy.start()
        for copy in copies:
            copy.wait()
        total = slots[0]
        for k in range(1, count):
            total = total + slots[k]
        return total

    ring[z] = everyone(sums, "blk", blk, 2**bits, 0)
    total = everyone(ring, "batch", z, depth, 2**bits)
    totals_ref[...] = total

    @pl.when(base < regions.in_base)
    def _():
        window_ref[0] = total[1]


def late_call(flat, early, gain, sources, weights, regions):
    bits = regions.count.bit_length() - 1
    depth = regions.depth
    small_phases, stream_phases, targets = regions.late_phases()
    phases = small_phases + stream_phases
    few, size = len(small_phases), phases[0][2]
    margin = max(regions.slot_rows, regions.line_rows * regions.per) + SUB
    wide, used = weights[2].shape
    small_count = sum(x.size for x in weights) // ROW
    tile = (SUB, LANE)
    dma = pltpu.SemaphoreType.DMA
    hops = 2**bits + depth
    vmem = pl.BlockSpec(memory_space=pltpu.VMEM)
    far = pl.BlockSpec(memory_space=pl.ANY)
    rows, model = sources[3].shape
    blocks = 8
    return pl.pallas_call(
        functools.partial(late_kernel, regions, bits, small_phases, stream_phases, targets, blocks),
        name="reduce_late",
        in_specs=[far, vmem, vmem] + [far] * len(sources) + [vmem] * len(weights),
        out_specs=[vmem] * 5,
        out_shape=[
            jax.ShapeDtypeStruct((regions.need,) + tile, f32),
            jax.ShapeDtypeStruct((2,) + tile, f32),
            jax.ShapeDtypeStruct((rows, model), bf16),
            jax.ShapeDtypeStruct((rows, model), bf16),
            jax.ShapeDtypeStruct((regions.need,) + tile, f32),
        ],
        scratch_shapes=[
            pltpu.VMEM((2, rows // blocks, x.shape[1]) if n in (0, 1, 5) else x.shape, x.dtype)
            for n, x in enumerate(sources)
        ]
        + [
            pltpu.VMEM((regions.half,) + tile, f32),
            pltpu.VMEM((few, 2**bits, size) + tile, f32),
            pltpu.VMEM((regions.need + 2 * margin,) + tile, f32),
            pltpu.VMEM((model // LANE, rows // blocks, LANE), f32),
            pltpu.VMEM((SUB, model), f32),
            pltpu.VMEM((2**bits, 2) + tile, f32),
            pltpu.VMEM((depth, 2) + tile, f32),
            pltpu.VMEM((wide // blocks, LANE), f32),
            pltpu.VMEM((wide * used // LANE, LANE), f32),
            pltpu.VMEM((small_count,) + tile, f32),
            dma((3 * len(sources),)),
            dma((hops,)),
            dma((hops,)),
            dma((few, len(targets))),
            dma((few, 2**bits)),
        ]
        + Reducer.scratch(depth, bits, phases),
        compiler_params=pltpu.CompilerParams(
            vmem_limit_bytes=62 * 2**20, collective_id=1, has_side_effects=True
        ),
    )(flat, early, gain, *sources, *weights)


def exchange_kernel(bits, state, totals_ref, entry_ref, arriving_ref, here, far, pre, post, send_sem, recv_sem):
    blk = lax.axis_index("blk")
    mine = [(blk // 2**b) % 2 for b in range(bits)]
    partner = [blk + (1 - 2 * mine[b]) * 2**b for b in range(bits)]
    barrier = pltpu.get_barrier_semaphore()
    for other in partner:
        pl.semaphore_signal(barrier, inc=1, device_id={"blk": other}, device_id_type=MESH)
    pl.semaphore_wait(barrier, bits)
    first, second, third = (slice(k * state, (k + 1) * state) for k in range(3))
    here[0] = totals_ref[...]
    entry_ref[...] = jnp.zeros_like(entry_ref)
    arriving_ref[...] = jnp.zeros_like(arriving_ref)
    pre[...] = jnp.ones_like(pre)
    post[...] = jnp.ones_like(post)
    for b in range(bits):
        if b < bits - 1:
            src, dst = here.at[b], far.at[b]
        else:
            src = here.at[b, pl.ds(pl.multiple_of((1 + mine[b]) * state, state), state)]
            dst = far.at[b, first]
        copy = pltpu.make_async_remote_copy(
            src_ref=src,
            dst_ref=dst,
            send_sem=send_sem.at[b],
            recv_sem=recv_sem.at[b],
            device_id={"blk": partner[b]},
            device_id_type=MESH,
        )
        copy.start()
        copy.wait()
        if b == bits - 1:

            @pl.when(mine[b] == 1)
            def _():
                entry_ref[...] += pre[...] * far[b, first]

            @pl.when(mine[b] == 0)
            def _():
                arriving_ref[...] += post[...] * far[b, first]

            continue

        @pl.when(mine[b] == 1)
        def _():
            entry_ref[...] += pre[...] * far[b, second]
            pre[...] *= far[b, first]
            here[b + 1, second] = here[b, second] + here[b, first] * far[b, second]
            here[b + 1, third] = far[b, third] + far[b, first] * here[b, third]

        @pl.when(mine[b] == 0)
        def _():
            arriving_ref[...] += post[...] * far[b, third]
            post[...] *= far[b, first]
            here[b + 1, second] = far[b, second] + far[b, first] * here[b, second]
            here[b + 1, third] = here[b, third] + here[b, first] * far[b, third]

        here[b + 1, first] = here[b, first] * far[b, first]


def exchange(totals, state):
    bits = lax.axis_size("blk").bit_length() - 1
    rows, inner = totals.shape
    vmem = pl.BlockSpec(memory_space=pltpu.VMEM)
    return pl.pallas_call(
        functools.partial(exchange_kernel, bits, state),
        name="exchange",
        in_specs=[vmem],
        out_specs=[vmem] * 2,
        out_shape=[jax.ShapeDtypeStruct((state, inner), f32)] * 2,
        scratch_shapes=[pltpu.VMEM((bits, rows, inner), f32)] * 2
        + [pltpu.VMEM((state, inner), f32)] * 2
        + [pltpu.SemaphoreType.DMA((bits,))] * 2,
        compiler_params=pltpu.CompilerParams(
            vmem_limit_bytes=VMEM_BYTES, collective_id=3, has_side_effects=True
        ),
    )(totals)


def local(
    tokens,
    out_cot,
    norm_gain,
    in_weight,
    conv_weight,
    conv_bias,
    xproj_weight,
    dt_weight,
    dt_bias,
    a_log,
    d_skip,
    out_weight,
    moment_one,
    moment_two,
):
    contract = (((0,), (0,)), ((), ()))
    backward = (((1,), (1,)), ((), ()))
    token_rows = interleave(tokens[0])
    cot_low = interleave(out_cot[0])
    source = token_rows.astype(f32)
    length = source.shape[0]
    inner = dt_bias.shape[0]
    state = a_log.shape[0]
    rank = dt_weight.shape[0]
    width = conv_weight.shape[0]
    halo = (width - 1) * SUB
    scale = lax.rsqrt(jnp.mean(source * source, axis=-1, keepdims=True) + EPS)
    normed = (source * scale * norm_gain).astype(bf16)
    stream = jnp.dot(normed, in_weight[:, :inner], preferred_element_type=f32)
    ends = stream[length - halo :].reshape(width - 1, SUB, inner)
    tail = shifted(ends[:, SUB - 1], "blk", 1)
    gating = jnp.dot(normed, in_weight[:, inner:], preferred_element_type=f32)
    grad_gated = lax.dot_general(cot_low, out_weight, backward, preferred_element_type=f32)
    head = jnp.concatenate([tail[:, None], ends[:, : SUB - 1]], 1).reshape(halo, inner)
    rates = -jnp.exp(a_log)
    rates_wide = jnp.repeat(rates * LOG2E, SUB, axis=0)
    spots = spread_table(2 * state)
    (
        conv_sum,
        conv_low,
        step_size,
        drive,
        grad_scanned,
        sel_low,
        terms,
        pre_decay,
        pre_state,
        post_decay,
        post_state,
        totals,
    ) = summary_call(
        stream,
        gating,
        grad_gated,
        head,
        conv_weight,
        conv_bias[None],
        xproj_weight,
        dt_weight,
        dt_bias[None],
        spots,
        rates_wide,
    )
    entry, arriving = exchange(totals, state)
    prior, readout_grads, gated, grad_gating, skip_grads = forward_call(
        step_size,
        drive,
        grad_scanned,
        terms,
        spots,
        rates_wide,
        pre_decay,
        pre_state,
        entry,
        conv_low,
        gating,
        grad_gated,
        d_skip[None],
    )
    grad_d_skip = jnp.sum(skip_grads, 0)

    span = moment_one.shape[0]
    small_rows = sum(
        value.size for value in (conv_weight, conv_bias, xproj_weight, dt_weight, dt_bias, a_log, d_skip)
    ) // ROW
    lead = (conv_weight.size + conv_bias.size) // ROW
    packed = xproj_weight.size // ROW
    rest = small_rows - lead - packed
    small_parts = ((0, packed, lead), (lead, 0, packed), (lead + packed, packed + lead, rest))
    regions = Regions(
        lax.axis_size("batch"),
        lax.axis_size("blk"),
        span,
        norm_gain.size // ROW,
        in_weight.shape,
        small_rows,
        out_weight.shape,
        small_parts,
    )
    flat_early = product_call((normed, grad_gating), (gated, cot_low))
    grad_stream_low, grad_pre_low, grad_selectors, rate_grads, taps_grads, edges, early = backward_call(
        step_size,
        drive,
        grad_scanned,
        terms,
        spots,
        rates_wide,
        post_state + post_decay * jnp.repeat(arriving, SUB, axis=0),
        prior,
        conv_sum,
        stream,
        readout_grads,
        dt_weight,
        xproj_weight,
        conv_weight,
        d_skip[None],
        flat_early,
        regions,
        rank,
    )
    grad_a_log = LN2 * jnp.sum(rate_grads.reshape(state, SUB, inner), 1)
    begins = edges[:halo].reshape(width - 1, SUB, inner)
    ahead = shifted(begins[:, 0], "blk", -1)
    grad_dt_weight = lax.dot_general(sel_low, grad_pre_low, contract, preferred_element_type=f32)[:rank]
    grad_xproj = lax.dot_general(conv_low, grad_selectors, contract, preferred_element_type=f32)
    foot = jnp.concatenate([begins[:, 1:], ahead[:, None]], 1)
    lasts = edges[halo:].reshape(width - 1, SUB, inner)
    further = jnp.concatenate([lasts, foot], 0)
    last_stream = stream[length - halo :].reshape(width - 1, SUB, inner)
    grad_last = conv_weight[width - 1] * lasts
    taps_grads = jnp.sum(taps_grads.reshape(width + 2, SUB, inner), 1)
    tap_grads = []
    for offset in range(width - 1):
        lead = width - 1 - offset
        grad_last = grad_last + conv_weight[offset] * further[lead : lead + width - 1]
        over = jnp.sum(last_stream[width - 1 - lead :] * foot[:lead], (0, 1))
        tap_grads.append(taps_grads[offset] + over)
    tap_grads.append(taps_grads[width - 1])
    grad_conv_weight = jnp.stack(tap_grads, 0)
    grad_conv_bias = taps_grads[width]
    grad_dt_bias = taps_grads[width + 1]
    grad_stream_low = lax.dynamic_update_slice_in_dim(
        grad_stream_low, grad_last.reshape(halo, inner).astype(bf16), length - halo, 0
    )
    thin = (grad_conv_weight, grad_conv_bias[None], grad_dt_weight, grad_dt_bias[None], grad_a_log, grad_d_skip[None])
    window, totals, result, grad_tokens, owned = late_call(
        product_call((normed, grad_stream_low), small=(grad_xproj, thin, rank + 2 * state)),
        early,
        norm_gain[None],
        (grad_gating, grad_stream_low, in_weight, token_rows, cot_low, gated, out_weight),
        (conv_weight, conv_bias[None], xproj_weight, dt_weight, dt_bias[None], a_log, d_skip[None]),
        regions,
    )
    result, grad_tokens = result[None], grad_tokens[None]
    grad_norm = jnp.sqrt(jnp.sum(totals[0]) + jnp.sum(totals[1] * totals[1]))
    owner = lax.axis_index(("batch", "blk"))
    begin = owner * span
    shard = lax.dynamic_slice_in_dim(window.reshape(-1), begin % ROW, span)
    owned = lax.dynamic_slice_in_dim(owned.reshape(-1), begin % ROW, span)
    lower = norm_gain.size + in_weight.size + sum(
        value.size for value in (conv_weight, conv_bias, xproj_weight, dt_weight)
    )
    upper = lower + dt_bias.size + a_log.size + d_skip.size
    place = begin + lax.iota(jnp.int32, span)
    keep = jnp.where((place >= lower) & (place < upper), 0.0, 1.0).astype(f32)
    clipped = shard * jnp.minimum(1.0, CLIP / (grad_norm + 1e-06))
    new_one = BETA_ONE * moment_one + (1.0 - BETA_ONE) * clipped
    new_two = BETA_TWO * moment_two + (1.0 - BETA_TWO) * clipped * clipped
    first = new_one / (1.0 - BETA_ONE**ADAM_STEP)
    second = new_two / (1.0 - BETA_TWO**ADAM_STEP)
    param_step = -RATE * (first / (jnp.sqrt(second) + ADAM_EPS) + DECAY * keep * owned)
    return (result, grad_tokens, shard, grad_norm, param_step, new_one, new_two)


def solution(mesh):
    return jax.shard_map(
        local,
        mesh=mesh,
        in_specs=(P("batch", "blk", None),) * 2 + (P(),) * 10 + (P(("batch", "blk")),) * 2,
        out_specs=(P("batch", "blk", None),) * 2
        + (P(("batch", "blk")), P(), P(("batch", "blk")), P(("batch", "blk")), P(("batch", "blk"))),
        check_vma=False,
    )
```

```python
import functools
import math

import jax
import jax.numpy as jnp
from jax import lax
from jax.experimental import pallas as pl
from jax.experimental.pallas import tpu as pltpu
from jax.sharding import PartitionSpec as P

ADAM_STEP = 100
EPS = 1e-05
RATE = 0.002
BETA_ONE = 0.9
BETA_TWO = 0.95
ADAM_EPS = 1e-08
DECAY = 0.1
CLIP = 1.0

LOG2E = 1.0 / math.log(2.0)
LN2 = math.log(2.0)
SUB = 8
LANE = 128
ROW = 1024
VMEM_BYTES = 56 * 2**20

MESH = pl.DeviceIdType.MESH

f32 = jnp.float32
bf16 = jnp.bfloat16


def shifted(x, axis, by):
    count = lax.axis_size(axis)
    pairs = [(i, i + by) for i in range(count) if 0 <= i + by < count]
    return lax.ppermute(x, axis, pairs)


def silu_slope(value):
    sig = jax.nn.sigmoid(value)
    return sig * (1.0 + value * (1.0 - sig))


def interleave(x):
    rows, width = x.shape
    return x.reshape(SUB, rows // SUB, width).transpose(1, 0, 2).reshape(rows, width)


def restore(x):
    rows, width = x.shape
    return x.reshape(rows // SUB, SUB, width).transpose(1, 0, 2).reshape(rows, width)


def at(start, size):
    return pl.ds(pl.multiple_of(start, size), size)


def spread(sel_ref, spots_ref, out_ref):
    out_ref[...] = jnp.dot(sel_ref[...], spots_ref[...], preferred_element_type=f32)


def gather_table(out_ref):
    row = lax.broadcasted_iota(jnp.int32, (LANE, LANE), 1)
    for n in range(out_ref.shape[0] // LANE):
        out_ref[n * LANE : (n + 1) * LANE, :] = jnp.where(row == n, 1.0, 0.0).astype(bf16)


def gather_lanes(src_ref, table_ref, out_ref):
    out_ref[...] = jnp.dot(src_ref[...].astype(bf16), table_ref[...], preferred_element_type=f32)


def spread_table(count):
    row = lax.broadcasted_iota(jnp.int32, (LANE, count * LANE), 0)
    col = lax.broadcasted_iota(jnp.int32, (LANE, count * LANE), 1) // LANE
    return ((row % count == col) & (row < 3 * count)).astype(bf16)


def summary_kernel(
    shape,
    stream_ref,
    gating_ref,
    grad_gated_ref,
    head_ref,
    taps_ref,
    bias_ref,
    select_in_ref,
    step_in_ref,
    step_bias_ref,
    spots_ref,
    rates_ref,
    conv_sum_ref,
    conv_ref,
    step_ref,
    drive_ref,
    grad_ref,
    low_ref,
    sel_ref,
    pre_decay_ref,
    pre_state_ref,
    post_decay_ref,
    post_state_ref,
    totals_ref,
    end_ref,
    exit_ref,
    prod_ref,
    select_ref,
    longer_ref,
    wide_ref,
):
    tiles, state, inner, cols, group = shape
    turn = pl.program_id(0)
    block = tiles * SUB
    width = taps_ref.shape[0]
    halo = (width - 1) * SUB

    @pl.when(turn == 0)
    def _():
        end_ref[...] = jnp.zeros_like(end_ref)
        exit_ref[...] = jnp.zeros_like(exit_ref)
        prod_ref[...] = jnp.ones_like(prod_ref)
        longer_ref[:halo, :] = head_ref[...]

    @pl.when(turn > 0)
    def _():
        longer_ref[:halo, :] = longer_ref[block:, :]

    longer_ref[halo:, :] = stream_ref[...]

    def convs(c, carry):
        lanes = at(c * 2 * LANE, 2 * LANE)
        taps = [jnp.broadcast_to(taps_ref[k : k + 1, lanes], (2 * SUB, 2 * LANE)) for k in range(width)]
        bias = bias_ref[:, lanes]

        def pair(i, carry):
            here = at(i * 2 * SUB, 2 * SUB)
            total = bias + taps[width - 1] * stream_ref[here, lanes]
            for k in range(width - 1):
                total = total + taps[k] * longer_ref[pl.ds(pl.multiple_of((2 * i + k) * SUB, SUB), 2 * SUB), lanes]
            conv_sum_ref[here, lanes] = total
            conv_ref[here, lanes] = (total * jax.nn.sigmoid(total)).astype(bf16)
            gating = gating_ref[here, lanes]
            grad_ref[here, lanes] = grad_gated_ref[here, lanes] * (gating * jax.nn.sigmoid(gating))
            return carry

        lax.fori_loop(0, tiles // 2, pair, 0, unroll=tiles // 2)
        return carry

    lax.fori_loop(0, inner // (2 * LANE), convs, 0)
    lane = lax.broadcasted_iota(jnp.int32, (block, LANE), 1)
    rank = step_in_ref.shape[0]
    used = rank + 2 * state
    wide_ref[...] = jnp.zeros_like(wide_ref)
    wide_ref[:, :used] = jnp.dot(conv_ref[...], select_in_ref[...], preferred_element_type=f32)
    selectors = wide_ref[...]
    low_ref[...] = selectors.astype(bf16)
    low = low_ref[:, :rank]
    value = jnp.where(lane < 2 * state, pltpu.roll(selectors, LANE - rank, 1), 0.0)
    high = value.astype(bf16).astype(f32)
    middle = (value - high).astype(bf16).astype(f32)
    rest = value - high - middle
    sel_ref[...] = (high + pltpu.roll(middle, 2 * state, 1) + pltpu.roll(rest, 4 * state, 1)).astype(bf16)

    step_ref[...] = jnp.dot(low, step_in_ref[...], preferred_element_type=f32)

    def steps(c, carry):
        lanes = at(c * 2 * LANE, 2 * LANE)
        bias = step_bias_ref[:, lanes]

        def pair(i, carry):
            here = at(i * 2 * SUB, 2 * SUB)
            pre = step_ref[here, lanes] + bias
            step = jnp.maximum(pre, 0.0) + jnp.log1p(jnp.exp(-jnp.abs(pre)))
            step_ref[here, lanes] = step
            drive_ref[here, lanes] = step * conv_ref[here, lanes].astype(f32)
            return carry

        lax.fori_loop(0, tiles // 2, pair, 0, unroll=tiles // 2)
        return carry

    lax.fori_loop(0, inner // (2 * LANE), steps, 0)
    spread(sel_ref, spots_ref, select_ref)

    def columns(c, carry):
        lanes = [at((c * cols + k) * LANE, LANE) for k in range(cols)]
        for first in range(0, state, group):
            spots = [(n, k) for n in range(group) for k in range(cols)]
            where = [(slice((first + n) * SUB, (first + n + 1) * SUB), lanes[k]) for n, k in spots]
            rates = [rates_ref[w] for w in where]

            def advance(i, carry):
                ends, exits, prods = carry
                here = at(i * SUB, SUB)
                step = [step_ref[here, l] for l in lanes]
                drive = [drive_ref[here, l] for l in lanes]
                grad = [grad_ref[here, l] for l in lanes]
                inject = [select_ref[here, (first + n) * LANE : (first + n + 1) * LANE] for n in range(group)]
                readout = [
                    select_ref[here, (state + first + n) * LANE : (state + first + n + 1) * LANE] for n in range(group)
                ]
                new = ([], [], [])
                for s, (n, k) in enumerate(spots):
                    decay = jnp.exp2(step[k] * rates[s])
                    prod = prods[s] * decay
                    new[0].append(ends[s] * decay + drive[k] * inject[n])
                    new[1].append(exits[s] + prod * (grad[k] * readout[n]))
                    new[2].append(prod)
                return tuple(tuple(x) for x in new)

            start = tuple(tuple(ref[w] for w in where) for ref in (end_ref, exit_ref, prod_ref))
            ends, exits, prods = lax.fori_loop(0, tiles, advance, start, unroll=16)
            for s, w in enumerate(where):
                end_ref[w] = ends[s]
                exit_ref[w] = exits[s]
                prod_ref[w] = prods[s]
        return carry

    lax.fori_loop(0, inner // (LANE * cols), columns, 0)

    @pl.when(turn == pl.num_programs(0) - 1)
    def _():
        row = lax.broadcasted_iota(jnp.int32, (SUB, LANE), 0)

        def columns(c, carry):
            lanes = at(c * LANE, LANE)
            for n in range(state):
                here = (slice(n * SUB, (n + 1) * SUB), lanes)
                for way, src, decay_out, state_out, total_row in (
                    (1, end_ref, pre_decay_ref, pre_state_ref, 1),
                    (-1, exit_ref, post_decay_ref, post_state_ref, 2),
                ):
                    decay, value = prod_ref[here], src[here]

                    def seen(by):
                        return row >= by if way > 0 else row < SUB - by

                    for by in (1, 2, 4):
                        far_decay = pltpu.roll(decay, by if way > 0 else SUB - by, 0)
                        far_value = pltpu.roll(value, by if way > 0 else SUB - by, 0)
                        value = jnp.where(seen(by), value + decay * far_value, value)
                        decay = jnp.where(seen(by), decay * far_decay, decay)
                    last = SUB - 1 if way > 0 else 0
                    totals_ref[pl.ds(n, 1), lanes] = decay[last : last + 1]
                    totals_ref[pl.ds(total_row * state + n, 1), lanes] = value[last : last + 1]
                    turn_by = 1 if way > 0 else SUB - 1
                    decay_out[here] = jnp.where(seen(1), pltpu.roll(decay, turn_by, 0), 1.0)
                    state_out[here] = jnp.where(seen(1), pltpu.roll(value, turn_by, 0), 0.0)
            return carry

        lax.fori_loop(0, inner // LANE, columns, 0)


def forward_kernel(
    shape,
    step_ref,
    drive_ref,
    grad_ref,
    sel_ref,
    spots_ref,
    rates_ref,
    pre_decay_ref,
    pre_state_ref,
    entry_ref,
    conv_ref,
    gating_ref,
    grad_gated_ref,
    skip_ref,
    prior_ref,
    readout_grad_ref,
    gated_ref,
    grad_gating_ref,
    skip_grad_ref,
    state_ref,
    select_ref,
    sums_ref,
    scanned_ref,
    table_ref,
):
    tiles, state, inner, cols, group = shape

    @pl.when(pl.program_id(0) == 0)
    def _():
        skip_grad_ref[...] = jnp.zeros_like(skip_grad_ref)
        gather_table(table_ref)
        for n in range(state):
            here = slice(n * SUB, (n + 1) * SUB)
            state_ref[here, :] = pre_state_ref[here, :] + pre_decay_ref[here, :] * entry_ref[n : n + 1, :]

    spread(sel_ref, spots_ref, select_ref)
    sums_ref[...] = jnp.zeros_like(sums_ref)

    def columns(c, carry):
        lanes = [at((c * cols + k) * LANE, LANE) for k in range(cols)]
        for first in range(0, state, group):
            spots = [(n, k) for n in range(group) for k in range(cols)]
            where = [(slice((first + n) * SUB, (first + n + 1) * SUB), lanes[k]) for n, k in spots]
            rates = [rates_ref[w] for w in where]

            def advance(i, states):
                here = at(i * SUB, SUB)
                step = [step_ref[here, l] for l in lanes]
                drive = [drive_ref[here, l] for l in lanes]
                grad = [grad_ref[here, l] for l in lanes]
                outs = [None] * cols
                new = []
                for n in range(group):
                    spot = slice((first + n) * LANE, (first + n + 1) * LANE)
                    inject = select_ref[here, spot]
                    readout = select_ref[here, (state + first + n) * LANE : (state + first + n + 1) * LANE]
                    total = None
                    for k in range(cols):
                        s = n * cols + k
                        decay = jnp.exp2(step[k] * rates[s])
                        fresh = decay * states[s] + drive[k] * inject
                        new.append(fresh)
                        part = readout * fresh
                        outs[k] = part if outs[k] is None else outs[k] + part
                        part = grad[k] * fresh
                        total = part if total is None else total + part
                    sums_ref[here, spot] += total
                    if n % 2 == 1:
                        pair = pl.ds(pl.multiple_of((i * state + first + n - 1) * SUB, 2 * SUB), 2 * SUB)
                        for k in range(cols):
                            prior_ref[pair, lanes[k]] = jnp.concatenate(
                                [states[(n - 1) * cols + k], states[n * cols + k]], 0
                            ).astype(bf16)
                for k in range(cols):
                    if first == 0:
                        scanned_ref[here, lanes[k]] = outs[k]
                    else:
                        scanned_ref[here, lanes[k]] += outs[k]
                return tuple(new)

            states = lax.fori_loop(0, tiles, advance, tuple(state_ref[w] for w in where), unroll=16)
            for s, w in enumerate(where):
                state_ref[w] = states[s]
        return carry

    lax.fori_loop(0, inner // (LANE * cols), columns, 0)
    gather_lanes(sums_ref, table_ref, readout_grad_ref)

    def finish(c, carry):
        lanes = at(c * 2 * LANE, 2 * LANE)
        skip = skip_ref[:, lanes]

        def pair(i, total):
            here = at(i * 2 * SUB, 2 * SUB)
            conv = conv_ref[here, lanes].astype(f32)
            gating = gating_ref[here, lanes]
            sig = jax.nn.sigmoid(gating)
            gate = gating * sig
            scanned = scanned_ref[here, lanes] + skip * conv
            gated_ref[here, lanes] = (scanned * gate).astype(bf16)
            slope = sig + gate * (1.0 - sig)
            grad_gating_ref[here, lanes] = (grad_gated_ref[here, lanes] * scanned * slope).astype(bf16)
            product = grad_ref[here, lanes] * conv
            return total + product[:SUB] + product[SUB:]

        zero = jnp.zeros((SUB, 2 * LANE), f32)
        skip_grad_ref[:, lanes] += lax.fori_loop(0, tiles // 2, pair, zero, unroll=tiles // 2)
        return carry

    lax.fori_loop(0, inner // (2 * LANE), finish, 0)


def backward_kernel(
    shape,
    scan_turns,
    regions,
    bits,
    phases,
    step_ref,
    drive_ref,
    grad_ref,
    sel_ref,
    spots_ref,
    rates_ref,
    begin_ref,
    prior_ref,
    conv_sum_ref,
    stream_ref,
    readout_grad_ref,
    step_back_ref,
    select_back_ref,
    taps_ref,
    skip_ref,
    flat_ref,
    grad_stream_ref,
    grad_pre_ref,
    grad_select_ref,
    rate_grad_ref,
    taps_grad_ref,
    edge_ref,
    early_ref,
    carry_ref,
    select_ref,
    sums_ref,
    through_ref,
    feed_ref,
    grad_conv_ref,
    inject_grad_ref,
    low_grad_ref,
    table_ref,
    *refs,
):
    tiles, state, inner, cols, group, rank = shape
    block = tiles * SUB
    width = taps_ref.shape[0]
    halo = (width - 1) * SUB
    turn = pl.program_id(0)
    work = Reducer(
        regions.depth,
        bits,
        phases,
        1,
        lambda p, owner: regions.early_start(phases[p][0], owner) + phases[p][1],
        flat_ref,
        refs,
    )
    turns = scan_turns
    early = max(work.slots - turns, 0)
    for g in range(turns):

        @pl.when(turn == g)
        def _():
            if g == 0:
                work.greet()
            for t in range(0 if g == 0 else g + early, min(g + early + 1, work.slots)):
                work.run(t)

    @pl.when(pl.program_id(0) == 0)
    def _():
        gather_table(table_ref)
        rate_grad_ref[...] = jnp.zeros_like(rate_grad_ref)
        taps_grad_ref[...] = jnp.zeros_like(taps_grad_ref)
        grad_conv_ref[tiles * SUB :, :] = jnp.zeros((grad_conv_ref.shape[0] - tiles * SUB, inner), f32)
        carry_ref[...] = begin_ref[...]

    spread(sel_ref, spots_ref, select_ref)
    sums_ref[...] = jnp.zeros_like(sums_ref)

    def columns(c, carry):
        lanes = [at((c * cols + k) * LANE, LANE) for k in range(cols)]
        for first in range(0, state, group):
            spots = [(n, k) for n in range(group) for k in range(cols)]
            where = [(slice((first + n) * SUB, (first + n + 1) * SUB), lanes[k]) for n, k in spots]
            rates = [rates_ref[w] for w in where]

            def retreat(turn, carry):
                carries, rate_grads = carry
                i = tiles - 1 - turn
                here = at(i * SUB, SUB)
                step = [step_ref[here, l] for l in lanes]
                drive = [drive_ref[here, l] for l in lanes]
                grad = [grad_ref[here, l] for l in lanes]
                throughs = [None] * cols
                feeds = [None] * cols
                new = ([], [])
                for n in range(group):
                    spot = slice((first + n) * LANE, (first + n + 1) * LANE)
                    inject = select_ref[here, spot]
                    readout = select_ref[here, (state + first + n) * LANE : (state + first + n + 1) * LANE]
                    if n % 2 == 0:
                        pair = pl.ds(pl.multiple_of((i * state + first + n) * SUB, 2 * SUB), 2 * SUB)
                        pairs = [prior_ref[pair, lanes[k]].astype(f32) for k in range(cols)]
                    total = None
                    for k in range(cols):
                        s = n * cols + k
                        prior = pairs[k][(n % 2) * SUB : (n % 2 + 1) * SUB]
                        power = step[k] * rates[s]
                        adjoint = grad[k] * readout + carries[s]
                        back = jnp.exp2(power) * adjoint
                        through = back * prior * power
                        new[0].append(back)
                        new[1].append(rate_grads[s] + through)
                        throughs[k] = through if throughs[k] is None else throughs[k] + through
                        part = adjoint * inject
                        feeds[k] = part if feeds[k] is None else feeds[k] + part
                        part = adjoint * drive[k]
                        total = part if total is None else total + part
                    sums_ref[here, spot] += total
                for k in range(cols):
                    if first == 0:
                        through_ref[here, lanes[k]] = throughs[k]
                        feed_ref[here, lanes[k]] = feeds[k]
                    else:
                        through_ref[here, lanes[k]] += throughs[k]
                        feed_ref[here, lanes[k]] += feeds[k]
                return tuple(tuple(x) for x in new)

            start = tuple(tuple(ref[w] for w in where) for ref in (carry_ref, rate_grad_ref))
            carries, rate_grads = lax.fori_loop(0, tiles, retreat, start, unroll=8)
            for s, w in enumerate(where):
                carry_ref[w] = carries[s]
                rate_grad_ref[w] = rate_grads[s]
        return carry

    lax.fori_loop(0, inner // (LANE * cols), columns, 0)
    gather_lanes(sums_ref, table_ref, inject_grad_ref)

    def steps(c, carry):
        lanes = at(c * 2 * LANE, 2 * LANE)

        def pair(i, total):
            here = at(i * 2 * SUB, 2 * SUB)
            step = step_ref[here, lanes]
            series = 1.0 + step * (-1.0 / 2 + step * (1.0 / 6 + step * (-1.0 / 24 + step * (1.0 / 120))))
            near = step < 0.06
            exact = (1.0 - jnp.exp2(step * -LOG2E)) / jnp.where(near, 1.0, step)
            ratio = jnp.where(near, series, exact)
            pre = ratio * (LN2 * through_ref[here, lanes] + drive_ref[here, lanes] * feed_ref[here, lanes])
            grad_pre_ref[here, lanes] = pre.astype(bf16)
            return total + pre[:SUB] + pre[SUB:]

        zero = jnp.zeros((SUB, 2 * LANE), f32)
        taps_grad_ref[(width + 1) * SUB :, lanes] += lax.fori_loop(0, tiles // 2, pair, zero, unroll=tiles // 2)
        return carry

    lax.fori_loop(0, inner // (2 * LANE), steps, 0)
    lane = lax.broadcasted_iota(jnp.int32, (block, LANE), 1)
    across = (((1,), (1,)), ((), ()))
    low_grad_ref[:, :rank] = lax.dot_general(
        grad_pre_ref[...], step_back_ref[...], across, preferred_element_type=f32
    )
    grads = low_grad_ref[...]
    inject_grad = pltpu.roll(inject_grad_ref[...], rank, 1)
    readout_grad = pltpu.roll(readout_grad_ref[...], rank + state, 1)
    grads = jnp.where(lane < rank, grads, jnp.where(lane < rank + state, inject_grad, readout_grad))
    grads = jnp.where(lane < rank + 2 * state, grads, 0.0)
    grads = grads.astype(bf16)
    grad_select_ref[...] = grads

    through_ref[...] = lax.dot_general(
        grad_select_ref[:, : rank + 2 * state], select_back_ref[...], across, preferred_element_type=f32
    )

    def convs(c, carry):
        lanes = at(c * 2 * LANE, 2 * LANE)
        skip = skip_ref[:, lanes]

        def conv(i, carry):
            here = at(i * SUB, SUB)
            value = conv_sum_ref[here, lanes]
            sig = jax.nn.sigmoid(value)
            slope = sig * (1.0 + value * (1.0 - sig))
            out = grad_ref[here, lanes] * skip + step_ref[here, lanes] * feed_ref[here, lanes] + through_ref[here, lanes]
            grad_conv_ref[here, lanes] = out * slope
            return carry

        lax.fori_loop(0, tiles, conv, 0, unroll=8)
        taps = [jnp.broadcast_to(taps_ref[k : k + 1, lanes], (SUB, 2 * LANE)) for k in range(width)]

        def tap(i, totals):
            totals = list(totals)
            done = []
            for q in range(2):
                parts = [
                    grad_conv_ref[pl.ds(pl.multiple_of((2 * i + q + m) * SUB, SUB), SUB), lanes] for m in range(width)
                ]
                stream = stream_ref[pl.ds(pl.multiple_of((2 * i + q) * SUB, SUB), SUB), lanes]
                grad = taps[width - 1] * parts[0]
                totals[width - 1] = totals[width - 1] + parts[0] * stream
                totals[width] = totals[width] + parts[0]
                for m in range(1, width):
                    grad = grad + taps[width - 1 - m] * parts[m]
                    totals[width - 1 - m] = totals[width - 1 - m] + parts[m] * stream
                done.append(grad)
            grad_stream_ref[at(i * 2 * SUB, 2 * SUB), lanes] = jnp.concatenate(done, 0).astype(bf16)
            return tuple(totals)

        zero = jnp.zeros((SUB, 2 * LANE), f32)
        totals = lax.fori_loop(0, tiles // 2, tap, (zero,) * (width + 1), unroll=tiles // 2)
        for k in range(width + 1):
            taps_grad_ref[k * SUB : (k + 1) * SUB, lanes] += totals[k]
        return carry

    lax.fori_loop(0, inner // (2 * LANE), convs, 0)

    @pl.when(pl.program_id(0) == 0)
    def _():
        edge_ref[halo:, :] = grad_conv_ref[block - halo : block, :]

    edge_ref[:halo, :] = grad_conv_ref[:halo, :]
    grad_conv_ref[block:, :] = grad_conv_ref[:halo, :]

    @pl.when(turn == turns - 1)
    def _():
        work.collect(early_ref)


def scan_shapes(rows, state, inner, tiles=16):
    tiles = min(tiles, rows // SUB)
    count = rows // (SUB * tiles)
    return tiles, count


def summary_call(stream, gating, grad_gated, head, taps, bias, select_in, step_in, step_bias, spots, rates):
    rows, inner = stream.shape
    state = rates.shape[0] // SUB
    tiles, count = scan_shapes(rows, state, inner)
    halo = head.shape[0]
    wide = pl.BlockSpec((tiles * SUB, inner), lambda t: (t, 0))
    thin = pl.BlockSpec((tiles * SUB, LANE), lambda t: (t, 0))
    whole = pl.BlockSpec((state * SUB, inner), lambda t: (0, 0))
    total = pl.BlockSpec((3 * state, inner), lambda t: (0, 0))
    shape = (tiles, state, inner, 2, 4)
    big = jax.ShapeDtypeStruct((state * SUB, inner), f32)
    full = jax.ShapeDtypeStruct((rows, inner), f32)
    slim = jax.ShapeDtypeStruct((rows, LANE), bf16)

    def fixed(x):
        return pl.BlockSpec(x.shape, lambda t: (0, 0), pipeline_mode=pl.Buffered(1))

    constants = (head, taps, bias, select_in, step_in, step_bias, spots, rates)
    return pl.pallas_call(
        functools.partial(summary_kernel, shape),
        name="scan_summary",
        grid=(count,),
        in_specs=[wide, wide, wide] + [fixed(x) for x in constants],
        out_specs=[wide] * 5 + [thin] * 2 + [whole] * 4 + [total],
        out_shape=[full, jax.ShapeDtypeStruct((rows, inner), bf16), full, full, full, slim, slim]
        + [big] * 4
        + [jax.ShapeDtypeStruct((3 * state, inner), f32)],
        scratch_shapes=[pltpu.VMEM((state * SUB, inner), f32)] * 3
        + [
            pltpu.VMEM((tiles * SUB, 2 * state * LANE), f32),
            pltpu.VMEM((halo + tiles * SUB, inner), f32),
            pltpu.VMEM((tiles * SUB, LANE), f32),
        ],
        compiler_params=pltpu.CompilerParams(vmem_limit_bytes=VMEM_BYTES),
    )(stream, gating, grad_gated, *constants)


def forward_call(step, drive, grad, sel, spots, rates, pre_decay, pre_state, entry, conv, gating, grad_gated, skip):
    rows, inner = step.shape
    state = rates.shape[0] // SUB
    tiles, count = scan_shapes(rows, state, inner)
    wide = pl.BlockSpec((tiles * SUB, inner), lambda t: (t, 0))
    table = pl.BlockSpec(spots.shape, lambda t: (0, 0))
    thin = pl.BlockSpec((tiles * SUB, sel.shape[1]), lambda t: (t, 0))
    whole = pl.BlockSpec((state * SUB, inner), lambda t: (0, 0), pipeline_mode=pl.Buffered(1))
    line = pl.BlockSpec((1, inner), lambda t: (0, 0))
    short = pl.BlockSpec((state, inner), lambda t: (0, 0))
    shape = (tiles, state, inner, 2, 8)
    return pl.pallas_call(
        functools.partial(forward_kernel, shape),
        name="scan_forward",
        grid=(count,),
        in_specs=[wide, wide, wide, thin, table, whole, whole, whole, short, wide, wide, wide, line],
        out_specs=[
            pl.BlockSpec((tiles * state * SUB, inner), lambda t: (t, 0)),
            pl.BlockSpec((tiles * SUB, LANE), lambda t: (t, 0)),
            wide,
            wide,
            pl.BlockSpec((SUB, inner), lambda t: (0, 0)),
        ],
        out_shape=[
            jax.ShapeDtypeStruct((rows * state, inner), bf16),
            jax.ShapeDtypeStruct((rows, LANE), f32),
            jax.ShapeDtypeStruct((rows, inner), bf16),
            jax.ShapeDtypeStruct((rows, inner), bf16),
            jax.ShapeDtypeStruct((SUB, inner), f32),
        ],
        scratch_shapes=[pltpu.VMEM((state * SUB, inner), f32)]
        + [
            pltpu.VMEM((tiles * SUB, 2 * state * LANE), f32),
            pltpu.VMEM((tiles * SUB, state * LANE), f32),
            pltpu.VMEM((tiles * SUB, inner), f32),
            pltpu.VMEM((state * LANE, LANE), bf16),
        ],
        compiler_params=pltpu.CompilerParams(vmem_limit_bytes=VMEM_BYTES),
    )(step, drive, grad, sel, spots, rates, pre_decay, pre_state, entry, conv, gating, grad_gated, skip)


def backward_call(step, drive, grad, sel, spots, rates, begin, prior, conv_sum, stream, readout_grad, step_back, select_back, taps, skip, flat, regions, rank):
    rows, inner = step.shape
    state = rates.shape[0] // SUB
    tiles, count = scan_shapes(rows, state, inner, 8)
    bits = regions.count.bit_length() - 1
    phases = regions.early_phases()

    def back(t):
        return (count - 1 - t, 0)

    wide = pl.BlockSpec((tiles * SUB, inner), back)
    table = pl.BlockSpec(spots.shape, lambda t: (0, 0), pipeline_mode=pl.Buffered(1))
    thin = pl.BlockSpec((tiles * SUB, sel.shape[1]), back)
    whole = pl.BlockSpec((state * SUB, inner), lambda t: (0, 0), pipeline_mode=pl.Buffered(1))
    narrow = pl.BlockSpec((tiles * SUB, LANE), back)
    width = taps.shape[0]
    halo = (width - 1) * SUB

    def fixed(x):
        return pl.BlockSpec(x.shape, lambda t: (0, 0), pipeline_mode=pl.Buffered(1))

    shape = (tiles, state, inner, 2, 4, rank)
    return pl.pallas_call(
        functools.partial(backward_kernel, shape, count, regions, bits, phases),
        name="scan_backward",
        grid=(count,),
        in_specs=[wide, wide, wide, thin, table, whole, whole]
        + [pl.BlockSpec((tiles * state * SUB, inner), back), wide, wide, narrow]
        + [fixed(step_back), fixed(select_back), fixed(taps), fixed(skip)]
        + [pl.BlockSpec(memory_space=pl.ANY)],
        out_specs=[
            wide,
            wide,
            narrow,
            pl.BlockSpec((state * SUB, inner), lambda t: (0, 0)),
            pl.BlockSpec(((width + 2) * SUB, inner), lambda t: (0, 0)),
            pl.BlockSpec((2 * halo, inner), lambda t: (0, 0)),
            pl.BlockSpec((regions.slot, SUB, LANE), lambda t: (0, 0, 0)),
        ],
        out_shape=[
            jax.ShapeDtypeStruct((rows, inner), bf16),
            jax.ShapeDtypeStruct((rows, inner), bf16),
            jax.ShapeDtypeStruct((rows, LANE), bf16),
            jax.ShapeDtypeStruct((state * SUB, inner), f32),
            jax.ShapeDtypeStruct(((width + 2) * SUB, inner), f32),
            jax.ShapeDtypeStruct((2 * halo, inner), f32),
            jax.ShapeDtypeStruct((regions.slot, SUB, LANE), f32),
        ],
        scratch_shapes=[pltpu.VMEM((state * SUB, inner), f32)]
        + [
            pltpu.VMEM((tiles * SUB, 2 * state * LANE), f32),
            pltpu.VMEM((tiles * SUB, state * LANE), f32),
            pltpu.VMEM((tiles * SUB, inner), f32),
            pltpu.VMEM((tiles * SUB, inner), f32),
            pltpu.VMEM((tiles * SUB + halo, inner), f32),
            pltpu.VMEM((tiles * SUB, LANE), f32),
            pltpu.VMEM((tiles * SUB, LANE), f32),
            pltpu.VMEM((state * LANE, LANE), bf16),
        ]
        + Reducer.scratch(regions.depth, bits, phases),
        compiler_params=pltpu.CompilerParams(
            vmem_limit_bytes=62 * 2**20, collective_id=2, has_side_effects=True
        ),
    )(step, drive, grad, sel, spots, rates, begin, prior, conv_sum, stream, readout_grad, step_back, select_back, taps, skip, flat)


def turn_tiles(tiles):
    row = lax.broadcasted_iota(jnp.int32, (SUB, LANE), 0)
    for bit in (1, 2, 4):
        upper = (row // bit) % 2 == 1
        new = list(tiles)
        for a in range(SUB):
            if a & bit == 0:
                b = a + bit
                new[a] = jnp.where(upper, pltpu.roll(tiles[b], bit, 0), tiles[a])
                new[b] = jnp.where(upper, tiles[b], pltpu.roll(tiles[a], SUB - bit, 0))
        tiles = new
    return tiles


def pack_columns(src_ref, used, out_ref):
    part = LANE - used
    rows = src_ref.shape[0] // 4
    lane = lax.broadcasted_iota(jnp.int32, (SUB, LANE), 1)
    flat = out_ref

    def one(g, carry):
        quads = [src_ref[pl.ds(g * 4 * SUB + q, SUB, stride=4), :] for q in range(4)]
        for m in range(3):
            first = quads[m] if m == 0 else pltpu.roll(quads[m], LANE - m * part, 1)
            second = pltpu.roll(quads[m + 1], used - m * part, 1)
            flat[pl.ds(g * 3 * SUB + m, SUB, stride=3), :] = jnp.where(lane < used - m * part, first, second)
        return carry

    lax.fori_loop(0, rows // SUB, one, 0, unroll=4)


def row_tile(src_ref, r, q):
    return jnp.concatenate(
        [src_ref[r : r + 1, (q * SUB + a) * LANE : (q * SUB + a + 1) * LANE] for a in range(SUB)], 0
    )


def product_kernel(steps, shapes, used, *refs):
    if used:
        out_ref, held_ref, packed_ref = refs[-3:]
    else:
        out_ref, held_ref = refs[-2:]
    contract = (((0,), (0,)), ((), ()))
    step = pl.program_id(0)

    def lay(src_ref, first, rows, base, per, q):
        def one(r, carry):
            tiles = [
                src_ref[at(r * SUB, SUB), (first + a) * LANE : (first + a + 1) * LANE] for a in range(SUB)
            ]
            for b, tile in enumerate(turn_tiles(tiles)):
                out_ref[base + (r * SUB + b) * per + q] = tile
            return carry

        lax.fori_loop(0, rows // SUB, one, 0, unroll=rows // SUB)

    for turn, (rows, width) in enumerate(shapes):
        left_ref, right_ref = refs[2 * turn : 2 * turn + 2]
        per = width // ROW

        @pl.when(step // steps == turn)
        def _():
            for q in range(per):
                held_ref[q, :rows] = lax.dot_general(
                    left_ref[...], right_ref[:, q * ROW : (q + 1) * ROW], contract, preferred_element_type=f32
                )
                lay(held_ref.at[q], 0, rows, 0, per, q)

    if not used:
        return
    wide_ref, *thin_refs = refs[2 * len(shapes) : -3]
    tiles = packed_ref.shape[0] // SUB

    @pl.when(step == steps * len(shapes))
    def _():
        pack_columns(wide_ref, used, packed_ref)

        def one(i, carry):
            out_ref[i] = packed_ref[at(i * SUB, SUB), :]
            return carry

        out_ref[...] = jnp.zeros_like(out_ref)
        lax.fori_loop(0, tiles, one, 0, unroll=8)
        base = tiles
        for ref in thin_refs:
            rows, per = ref.shape[0], ref.shape[1] // ROW
            for q in range(per):
                if rows % SUB == 0:
                    lay(ref, q * SUB, rows, base, per, q)
                else:
                    for r in range(rows):
                        out_ref[base + r * per + q] = row_tile(ref, r, q)
            base += rows * per


def product_call(*pairs, small=None):
    steps = 4
    shapes = [(left.shape[1] // steps, right.shape[1]) for left, right in pairs]
    size = shapes[0][0] * shapes[0][1] // ROW

    def block(k):
        return lambda t: (0, jnp.clip(t - k * steps, 0, steps - 1))

    specs = []
    for k, (left, right) in enumerate(pairs):
        specs.append(pl.BlockSpec((left.shape[0], left.shape[1] // steps), block(k)))
        specs.append(pl.BlockSpec(right.shape, lambda t: (0, 0), pipeline_mode=pl.Buffered(1)))
    args = [x for pair in pairs for x in pair]
    scratch = [pltpu.VMEM((shapes[0][1] // ROW, max(rows for rows, _ in shapes), ROW), f32)]
    used, extra = 0, 0
    if small is not None:
        wide, thin, used = small
        extra = 1
        scratch.append(pltpu.VMEM((wide.shape[0] * used // LANE, LANE), f32))
        for x in (wide,) + thin:
            specs.append(pl.BlockSpec(x.shape, lambda t: (0, 0), pipeline_mode=pl.Buffered(1)))
            args.append(x)
    grid = steps * len(pairs) + extra
    return pl.pallas_call(
        functools.partial(product_kernel, steps, shapes, used),
        name="flat_product",
        grid=(grid,),
        in_specs=specs,
        out_specs=pl.BlockSpec((size, SUB, LANE), lambda t: (t, 0, 0)),
        out_shape=jax.ShapeDtypeStruct((size * grid, SUB, LANE), f32),
        scratch_shapes=scratch,
        compiler_params=pltpu.CompilerParams(vmem_limit_bytes=VMEM_BYTES),
    )(*args)


class Regions:
    def __init__(self, depth, count, span, gain, in_shape, small, out_shape, small_parts):
        self.depth, self.count, self.span = depth, count, span
        self.per = in_shape[1] // ROW
        self.in_rows = in_shape[0]
        self.in_base = gain
        self.small_base = gain + in_shape[0] * self.per
        self.out_base = self.small_base + small
        self.out_rows = out_shape[0] * out_shape[1] // ROW
        self.need = (span - 1) // ROW + 2
        self.lines = min((self.need + self.per - 2) // self.per + 1, self.in_rows)
        self.half = self.lines * self.per // 2
        self.pieces = -(-self.need // self.half)
        self.slot = self.pieces * self.half
        self.line_rows = min(-(-(self.lines + 15) // 16) * 16, self.in_rows)
        self.slot_rows = min(-(-(self.slot + 15) // 16) * 16, self.out_rows)
        self.small_parts = small_parts
        self.small_tiles = sum(length for _, _, length in small_parts)

    def base(self, owner):
        return owner * self.span // ROW

    def in_first(self, owner):
        line = lax.max(self.base(owner) - self.in_base, 0) // self.per
        return lax.min(line, self.in_rows - self.lines)

    def out_first(self, owner):
        return lax.max(lax.min(self.base(owner) - self.out_base, self.out_rows - self.slot), 0)

    def meets_in(self, z):
        return z * self.count * self.span // ROW < self.small_base

    def meets_out(self, z):
        return ((z + 1) * self.count * self.span - 1) // ROW >= self.out_base

    def early_start(self, z, owner):
        if not self.meets_out(z):
            return self.in_first(owner) * (self.per // 2)
        out = self.in_rows * self.per // 2 + self.out_first(owner)
        if not self.meets_in(z):
            return out
        inside = self.base(owner) < self.small_base
        return jnp.where(inside, self.in_first(owner) * (self.per // 2), out)

    def early_phases(self):
        phases = []
        cut = 2 if self.half % 4 == 0 else 1
        size = self.half // cut
        for z in range(self.depth):
            for piece in range((self.pieces if self.meets_out(z) else 1) * cut):
                phases.append((z, piece * size, size))
        return sorted(phases, key=lambda phase: -max(self.depth - 1 - phase[0], phase[0]))

    def late_phases(self):
        cut = 2 if self.half % 4 == 0 else 1
        size = self.half // cut
        owners = [k for k in range(self.depth * self.count) if self.meets_small(k)]
        goals = {k // self.count for k in owners}
        assert len(goals) == 1
        goal = goals.pop()
        small = [(goal, None, size)] * -(-self.small_tiles // (self.count * size))
        stream = [(z, piece * size, size) for z in range(self.depth) if self.meets_in(z) for piece in range(cut)]
        return small, stream, [k % self.count for k in owners]

    def meets_small(self, owner):
        base = self.base(owner)
        return base < self.out_base and base + self.need > self.small_base

    def late_start(self, phases, p, owner):
        goal, offset, size = phases[p]
        if offset is None:
            return self.in_rows * self.per // 2 + (p * self.count + owner % self.count) * size
        return self.in_first(owner) * (self.per // 2) + offset


class Reducer:
    def __init__(self, depth, bits, phases, gap, start, src_ref, refs):
        self.depth, self.bits, self.phases = depth, bits, phases
        self.start, self.src = start, src_ref
        self.n = bits - 1
        self.half = phases[0][2] // 2
        self.acc, self.first = refs[:2]
        self.bit_recvs = refs[2 : 2 + self.n]
        self.down, self.up = refs[2 + self.n : 4 + self.n]
        (
            self.local_sem,
            self.core_send,
            self.core_recv,
            self.bit_send,
            self.bit_recv,
            self.z_send,
            self.z_recv,
        ) = refs[4 + self.n : 11 + self.n]
        self.blk, self.z = lax.axis_index("blk"), lax.axis_index("batch")
        self.mine = [(self.blk // 2**b) % 2 for b in range(bits)]
        self.partner = [self.blk + (1 - 2 * self.mine[b]) * 2**b for b in range(bits)]
        self.last = self.n + depth - 1
        self.slot = [0] + [1 + 2 * s for s in range(self.n)]
        self.slot += [max(2 * self.n, 1) + gap * u for u in range(depth - 1)]
        self.done = self.slot[-1] + 1
        hops = [max(depth - 1 - goal, goal) for goal, _, _ in phases]
        self.slots = max(p + self.slot[self.n + h] + 1 for p, h in enumerate(hops))

    @staticmethod
    def scratch(depth, bits, phases):
        n, count, size = bits - 1, len(phases), phases[0][2]
        tile = (SUB, LANE)
        dma = pltpu.SemaphoreType.DMA
        return (
            [pltpu.VMEM((count,) + (2,) * n + (size,) + tile, f32)] * 2
            + [pltpu.VMEM((count, 2) + (2,) * (n - 1 - s) + (size // 2,) + tile, f32) for s in range(n)]
            + [pltpu.VMEM((count, size) + tile, f32)] * 2
            + [dma((count,))] * 3
            + [dma((max(count * n, 1),))] * 2
            + [dma((count,)), dma((2 * count,))]
        )

    def greet(self):
        barrier = pltpu.get_barrier_semaphore()
        peers = ("blk", self.blk, 2**self.bits), ("batch", self.z, self.depth)
        for axis, index, count in peers:
            for by in range(1, count):
                other = lax.rem(index + by, count)
                pl.semaphore_signal(barrier, inc=1, device_id={axis: other}, device_id_type=MESH)
        pl.semaphore_wait(barrier, 2**self.bits + self.depth - 2)

    def digits(self, r):
        return tuple((r // 2**i) % 2 for i in reversed(range(self.n)))

    def window(self, p, r, core):
        goal, offset, size = self.phases[p]
        owner = goal * 2**self.bits + 2 * r + core
        return pl.ds(self.start(p, owner), size)

    def core_copies(self, p, own=False):
        copies = []
        for r in range(2**self.n):
            where = (p,) + self.digits(r)
            if own:
                copies.append(
                    pltpu.make_async_copy(
                        self.src.at[self.window(p, r, self.mine[0])], self.acc.at[where], self.local_sem.at[p]
                    )
                )
            else:
                copies.append(
                    pltpu.make_async_remote_copy(
                        src_ref=self.src.at[self.window(p, r, 1 - self.mine[0])],
                        dst_ref=self.first.at[where],
                        send_sem=self.core_send.at[p],
                        recv_sem=self.core_recv.at[p],
                        device_id={"blk": self.partner[0]},
                        device_id_type=MESH,
                    )
                )
        return copies

    def order(self, part):
        return list(range(self.n)) if part == 0 else list(reversed(range(self.n)))

    def place(self, p, part, done, pick):
        spots = [slice(None)] * self.n
        for i in self.order(part)[:done]:
            spots[i] = self.mine[i + 1]
        spots[self.order(part)[done]] = pick
        return (p,) + tuple(reversed(spots)) + (slice(part * self.half, (part + 1) * self.half),)

    def bit_copies(self, p, s):
        copies = []
        for part in range(2):
            i = self.order(part)[s]
            spot = p * self.n + s
            copies.append(
                pltpu.make_async_remote_copy(
                    src_ref=self.acc.at[self.place(p, part, s, 1 - self.mine[i + 1])],
                    dst_ref=self.bit_recvs[s].at[p, part],
                    send_sem=self.bit_send.at[spot],
                    recv_sem=self.bit_recv.at[spot],
                    device_id={"blk": self.partner[i + 1]},
                    device_id_type=MESH,
                )
            )
        return copies

    def settled(self, p):
        return (p,) + tuple(reversed([self.mine[i + 1] for i in range(self.n)]))

    def z_copy(self, p, up):
        return pltpu.make_async_remote_copy(
            src_ref=self.acc.at[self.settled(p)],
            dst_ref=(self.up if up else self.down).at[p],
            send_sem=self.z_send.at[p],
            recv_sem=self.z_recv.at[2 * p + up],
            device_id={"batch": lax.rem(self.z + (1 if up else self.depth - 1), self.depth)},
            device_id_type=MESH,
        )

    def add(self, dst, dst_at, src, src_at):
        dst[dst_at] += src[src_at]

    def all_core(self, p):
        return pltpu.make_async_remote_copy(
            src_ref=self.first.at[p],
            dst_ref=self.first.at[p],
            send_sem=self.core_send.at[p],
            recv_sem=self.core_recv.at[p],
            device_id={"blk": self.partner[0]},
            device_id_type=MESH,
        )

    def all_bit(self, p, s):
        return pltpu.make_async_remote_copy(
            src_ref=self.bit_recvs[s].at[p],
            dst_ref=self.bit_recvs[s].at[p],
            send_sem=self.bit_send.at[p * self.n + s],
            recv_sem=self.bit_recv.at[p * self.n + s],
            device_id={"blk": self.partner[0]},
            device_id_type=MESH,
        )

    def finish_core(self, p):
        pltpu.make_async_copy(self.first.at[p], self.acc.at[p], self.local_sem.at[p]).wait()
        self.all_core(p).wait_recv()
        for r in range(2**self.n):
            where = (p,) + self.digits(r)
            self.add(self.acc, where, self.first, where)

    def finish_bit(self, p, s):
        self.all_bit(p, s).wait_recv()
        for part in range(2):
            kept = self.place(p, part, s, self.mine[self.order(part)[s] + 1])
            free = [i for i in range(1, 1 + self.n) if isinstance(kept[i], slice)]
            for r in range(2 ** len(free)):
                chosen = tuple((r // 2**j) % 2 for j in reversed(range(len(free))))
                to = list(kept)
                for i, v in zip(free, chosen):
                    to[i] = v
                self.add(self.acc, tuple(to), self.bit_recvs[s], (p, part) + chosen)

    def take(self, p, up):
        self.z_copy(p, up).wait_recv()
        self.add(self.acc, self.settled(p), self.up if up else self.down, p)

    def z_moves(self, p, u):
        goal = self.phases[p][0]
        moves = []
        if self.depth - 1 - u > goal:
            moves.append((self.depth - 1 - u, False))
        if u < goal:
            moves.append((u, True))
        return moves

    def act(self, p, stage):
        n = self.n
        if stage == 0:
            for copy in self.core_copies(p) + self.core_copies(p, True):
                copy.start()
            return
        if stage == 1:
            self.finish_core(p)
        elif stage <= n + 1:
            self.finish_bit(p, stage - 2)
        if stage <= n:
            for copy in self.bit_copies(p, stage - 1):
                copy.start()
            return
        u = stage - n - 1
        for mover, up in self.z_moves(p, u):

            @pl.when(self.z == mover)
            def _():
                if u > 0:
                    self.take(p, up)
                self.z_copy(p, up).start()

    def run(self, t):
        for stage in reversed(range(self.last + 1)):
            p = t - self.slot[stage]
            if 0 <= p < len(self.phases):
                self.act(p, stage)

    def finish(self, p):
        goal = self.phases[p][0]
        if goal < self.depth - 1:
            self.take(p, False)
        if goal > 0:
            self.take(p, True)

    def collect(self, out_ref, first=0):
        for p, (goal, offset, size) in list(enumerate(self.phases))[first:]:

            @pl.when(self.z == goal)
            def _():
                self.finish(p)
                out_ref[offset : offset + size] = self.acc[self.settled(p)]

        for p in range(len(self.phases)):
            self.all_core(p).wait_send()
            for s in range(self.n):
                self.all_bit(p, s).wait_send()
            for u in range(self.depth - 1):
                for mover, up in self.z_moves(p, u):

                    @pl.when(self.z == mover)
                    def _():
                        self.z_copy(p, up).wait_send()


def put_restored(value, turn_ref, out_ref, block):
    rows, width = value.shape
    tiles = rows // SUB
    step = out_ref.shape[0] // SUB
    for a in range(width // LANE):
        turn_ref[a] = value[:, a * LANE : (a + 1) * LANE]
    for j in range(SUB):
        here = pl.ds(pl.multiple_of(j * step + block * tiles, tiles), tiles)
        for a in range(width // LANE):
            part = turn_ref[a, pl.ds(j, tiles, stride=SUB), :]
            out_ref[here, a * LANE : (a + 1) * LANE] = part.astype(bf16)


def late_kernel(
    regions,
    bits,
    small_phases,
    stream_phases,
    targets,
    blocks,
    flat_ref,
    early_ref,
    gain_ref,
    *refs,
):
    depth, span = regions.depth, regions.span
    sources, weights, refs = refs[:7], refs[7:14], refs[14:]
    window_ref, totals_ref, result_ref, grad_ref, params_ref = refs[:5]
    held, refs = refs[5:12], refs[12:]
    gate_back, stream_back, in_w, token, cot, gated, out_w = held
    late_ref, small_ref, wide_window, turn_ref, gain_sum, sums, ring = refs[:7]
    columns_ref, packed_ref, small_params = refs[7:10]
    load_sem, ring_send, ring_recv, small_send, small_recv = refs[10:15]
    phases = small_phases + stream_phases
    few = len(small_phases)
    work = Reducer(
        depth, bits, phases, 2, lambda p, owner: regions.late_start(phases, p, owner), flat_ref, refs[15:]
    )
    blk, z = work.blk, work.z
    inner = gated.shape[2]
    size = token.shape[0] // blocks
    loads = [
        pltpu.make_async_copy(src, dst, load_sem.at[i])
        for i, (src, dst) in enumerate(zip(sources, held))
        if src.shape == dst.shape
    ]

    def pieces(t):
        here = pl.ds(pl.multiple_of(t * size, size), size)
        return [
            pltpu.make_async_copy(src.at[here], dst.at[t % 2], load_sem.at[len(held) + 2 * i + t % 2])
            for i, (src, dst) in enumerate(zip(sources, held))
            if src.shape != dst.shape
        ]

    for load in loads + pieces(0):
        load.start()
    work.greet()
    gain_sum[...] = jnp.zeros_like(gain_sum)
    across = (((1,), (1,)), ((), ()))

    goal = small_phases[0][0]
    owner = z * 2**bits + blk
    base = regions.base(owner)
    margin = (wide_window.shape[0] - regions.need) // 2

    def spread_rows(src_ref, first, rows, put):
        per = src_ref.shape[1] // ROW

        def one(r, carry):
            here = pl.ds(pl.multiple_of(first + r * 2 * SUB, 2 * SUB), 2 * SUB)
            for q in range(per):
                both = src_ref[here, q * ROW : (q + 1) * ROW].astype(f32)
                for side in range(2):
                    half = both[side * SUB : (side + 1) * SUB]
                    tiles = turn_tiles([half[:, a * LANE : (a + 1) * LANE] for a in range(SUB)])
                    for b, tile in enumerate(tiles):
                        put((first + r * 2 * SUB + side * SUB + b) * per + q, tile)
            return carry

        lax.fori_loop(0, rows // (2 * SUB), one, 0)

    def lay_params():
        conv_w, conv_b, select_w, step_w, step_b, rate, skip = weights
        used = select_w.shape[1]
        part = columns_ref.shape[0]
        for c in range(select_w.shape[0] // part):
            columns_ref[:, :used] = select_w[c * part : (c + 1) * part].astype(f32)
            pack_columns(columns_ref, used, packed_ref.at[c * part * used // LANE : (c + 1) * part * used // LANE])
        spot = 0
        for ref in (conv_w, conv_b, select_w, step_w, step_b, rate, skip):
            count = ref.shape[0] * ref.shape[1] // ROW
            if ref is select_w:

                def one(i, carry, spot=spot):
                    small_params[spot + i] = packed_ref[at(i * SUB, SUB), :]
                    return carry

                lax.fori_loop(0, count, one, 0, unroll=8)
            elif ref is step_w:

                def put(i, tile, spot=spot):
                    small_params[spot + i] = tile

                spread_rows(step_w, 0, step_w.shape[0], put)
            else:
                per = ref.shape[1] // ROW
                for i in range(count):
                    small_params[spot + i] = row_tile(ref, i // per, i % per)
            spot += count

    def place_params():
        params_ref[...] = jnp.zeros_like(params_ref)
        wide_window[...] = jnp.zeros_like(wide_window)

        @pl.when(base < regions.small_base)
        def _():
            first = regions.in_first(owner) // (2 * SUB) * (2 * SUB)
            first = lax.min(first, regions.in_rows - regions.line_rows)

            def put(i, tile):
                wide_window[regions.in_base + i - base + margin] = tile

            spread_rows(in_w, first, regions.line_rows, put)

        @pl.when(base >= regions.small_base)
        def _():
            first = regions.out_first(owner) // (2 * SUB) * (2 * SUB)
            first = lax.min(first, regions.out_rows - regions.slot_rows)

            def put(i, tile):
                wide_window[regions.out_base + i - base + margin] = tile

            spread_rows(out_w, first, regions.slot_rows, put)

        @pl.when((base < regions.out_base) & (base + regions.need > regions.small_base))
        def _():
            def line(i, carry):
                row = base + i
                tile = lax.max(lax.min(row - regions.small_base, small_params.shape[0] - 1), 0)
                here = (row >= regions.small_base) & (row < regions.out_base)
                wide_window[margin + i] = jnp.where(here, small_params[tile], wide_window[margin + i])
                return carry

            lax.fori_loop(0, regions.need, line, 0, unroll=2)

        params_ref[...] = wide_window[margin : margin + regions.need]

        @pl.when(base < regions.in_base)
        def _():
            params_ref[0] = row_tile(gain_ref, 0, 0)

    def hand_out(p, target):
        return pltpu.make_async_remote_copy(
            src_ref=small_ref.at[p, blk],
            dst_ref=small_ref.at[p, blk],
            send_sem=small_send.at[p, targets.index(target)],
            recv_sem=small_recv.at[p, blk],
            device_id={"blk": target},
            device_id_type=MESH,
        )

    def give_small(p):
        @pl.when(z == goal)
        def _():
            work.finish(p)
            small_ref[p, blk] = work.acc[work.settled(p)]
            for target in targets:

                @pl.when(blk != target)
                def _():
                    hand_out(p, target).start()

    def slot(t, carry):
        for k in range(work.slots):

            @pl.when(t == k)
            def _():
                if 0 <= k - work.done < few:
                    give_small(k - work.done)
                work.run(k)
                if k == 0:
                    for load in loads:
                        load.wait()

        @pl.when(t < blocks)
        def _():
            here = pl.ds(pl.multiple_of(t * size, size), size)
            part = t % 2
            for piece in pieces(t):
                piece.wait()

            @pl.when(t + 1 < blocks)
            def _():
                for piece in pieces(t + 1):
                    piece.start()

            source = token[here, :].astype(f32)
            output = jnp.dot(gated[part], out_w[...], preferred_element_type=f32)
            put_restored(source + output, turn_ref, result_ref, t)
            grad_normed = lax.dot_general(
                stream_back[part], in_w[:, :inner], across, preferred_element_type=f32
            ) + lax.dot_general(gate_back[part], in_w[:, inner:], across, preferred_element_type=f32)
            scale = lax.rsqrt(jnp.mean(source * source, axis=-1, keepdims=True) + EPS)
            scaled = source * scale
            product = grad_normed * scaled
            gain_sum[...] += jnp.sum(product.reshape(size // SUB, SUB, product.shape[1]), 0)
            weighted = grad_normed * gain_ref[...]
            mean = jnp.mean(weighted * source, axis=-1, keepdims=True)
            back = scale * weighted - source * (scale * scale * scale) * mean + cot[here, :].astype(f32)
            put_restored(back, turn_ref, grad_ref, t)

        @pl.when(t == blocks)
        def _():
            lay_params()

        @pl.when(t == blocks + 1)
        def _():
            place_params()

        return carry

    lax.fori_loop(0, max(work.slots, blocks + 2), slot, 0)
    for p in range(few):
        if p + work.done >= work.slots:
            give_small(p)
    late_ref[...] = jnp.zeros_like(late_ref)
    work.collect(late_ref, few)
    for target in targets:
        for p in range(few):

            @pl.when((z == goal) & (blk != target))
            def _():
                hand_out(p, target).wait_send()

            for source in range(2**bits):
                if source != target:

                    @pl.when((z == goal) & (blk == target))
                    def _():
                        pltpu.make_async_remote_copy(
                            src_ref=small_ref.at[p, source],
                            dst_ref=small_ref.at[p, source],
                            send_sem=small_send.at[p, 0],
                            recv_sem=small_recv.at[p, source],
                            device_id={"blk": source},
                            device_id_type=MESH,
                        ).wait_recv()

    inside = lax.broadcasted_iota(jnp.int32, (SUB, LANE), 0) * LANE + lax.broadcasted_iota(
        jnp.int32, (SUB, LANE), 1
    )
    sums[blk, 0] = jnp.zeros((SUB, LANE), f32)
    gain = jnp.sum(gain_sum[...], 0, keepdims=True)
    for a in range(SUB):
        sums[blk, 1, a : a + 1, :] = gain[:, a * LANE : (a + 1) * LANE]
    half = regions.per // 2
    wide_window[...] = jnp.zeros_like(wide_window)

    def own(value, row):
        spot = inside + (row * ROW - owner * span)
        return jnp.where((spot >= 0) & (spot < span), value, 0.0)

    def keep(total, value, row):
        wide_window[row - base + margin] = value
        part = own(value, row)
        return total + part * part

    zero = jnp.zeros((SUB, LANE), f32)

    @pl.when(base < regions.small_base)
    def _():
        def line(d, total):
            row = regions.in_base + (regions.in_first(owner) + d) * regions.per
            for q in range(half):
                total = keep(total, late_ref[d * half + q], row + q)
                total = keep(total, early_ref[d * half + q], row + half + q)
            return total

        sums[blk, 0] += lax.fori_loop(0, regions.lines, line, zero, unroll=2)

    @pl.when(base >= regions.small_base)
    def _():
        def line(i, total):
            return keep(total, early_ref[i], regions.out_base + regions.out_first(owner) + i)

        sums[blk, 0] += lax.fori_loop(0, regions.slot, line, zero, unroll=4)

    size = small_phases[0][2]

    @pl.when((base < regions.out_base) & (base + regions.need > regions.small_base))
    def _():
        def line(i, total):
            row = base + i
            tile = 0
            for first, spot, length in regions.small_parts:
                offset = row - regions.small_base - first
                tile = jnp.where(offset >= 0, spot + lax.min(offset, length - 1), tile)
            lot = tile // size
            value = small_ref[lot // 2**bits, lot % 2**bits, tile % size]
            here = (row >= regions.small_base) & (row < regions.out_base)
            wide_window[margin + i] = jnp.where(here, value, wide_window[margin + i])
            part = jnp.where(here, own(value, row), 0.0)
            return total + part * part

        sums[blk, 0] += lax.fori_loop(0, regions.need, line, zero, unroll=2)

    window_ref[...] = wide_window[margin : margin + regions.need]

    def everyone(slots, axis, index, count, first_sem):
        copies = [
            pltpu.make_async_remote_copy(
                src_ref=slots.at[index],
                dst_ref=slots.at[index],
                send_sem=ring_send.at[first_sem + by],
                recv_sem=ring_recv.at[first_sem + by],
                device_id={axis: lax.rem(index + by, count)},
                device_id_type=MESH,
            )
            for by in range(1, count)
        ]
        for copy in copies:
            copy.start()
        for copy in copies:
            copy.wait()
        total = slots[0]
        for k in range(1, count):
            total = total + slots[k]
        return total

    ring[z] = everyone(sums, "blk", blk, 2**bits, 0)
    total = everyone(ring, "batch", z, depth, 2**bits)
    totals_ref[...] = total

    @pl.when(base < regions.in_base)
    def _():
        window_ref[0] = total[1]


def late_call(flat, early, gain, sources, weights, regions):
    bits = regions.count.bit_length() - 1
    depth = regions.depth
    small_phases, stream_phases, targets = regions.late_phases()
    phases = small_phases + stream_phases
    few, size = len(small_phases), phases[0][2]
    margin = max(regions.slot_rows, regions.line_rows * regions.per) + SUB
    wide, used = weights[2].shape
    small_count = sum(x.size for x in weights) // ROW
    tile = (SUB, LANE)
    dma = pltpu.SemaphoreType.DMA
    hops = 2**bits + depth
    vmem = pl.BlockSpec(memory_space=pltpu.VMEM)
    far = pl.BlockSpec(memory_space=pl.ANY)
    rows, model = sources[3].shape
    blocks = 8
    return pl.pallas_call(
        functools.partial(late_kernel, regions, bits, small_phases, stream_phases, targets, blocks),
        name="reduce_late",
        in_specs=[far, vmem, vmem] + [far] * len(sources) + [vmem] * len(weights),
        out_specs=[vmem] * 5,
        out_shape=[
            jax.ShapeDtypeStruct((regions.need,) + tile, f32),
            jax.ShapeDtypeStruct((2,) + tile, f32),
            jax.ShapeDtypeStruct((rows, model), bf16),
            jax.ShapeDtypeStruct((rows, model), bf16),
            jax.ShapeDtypeStruct((regions.need,) + tile, f32),
        ],
        scratch_shapes=[
            pltpu.VMEM((2, rows // blocks, x.shape[1]) if n in (0, 1, 5) else x.shape, x.dtype)
            for n, x in enumerate(sources)
        ]
        + [
            pltpu.VMEM((regions.half,) + tile, f32),
            pltpu.VMEM((few, 2**bits, size) + tile, f32),
            pltpu.VMEM((regions.need + 2 * margin,) + tile, f32),
            pltpu.VMEM((model // LANE, rows // blocks, LANE), f32),
            pltpu.VMEM((SUB, model), f32),
            pltpu.VMEM((2**bits, 2) + tile, f32),
            pltpu.VMEM((depth, 2) + tile, f32),
            pltpu.VMEM((wide // blocks, LANE), f32),
            pltpu.VMEM((wide * used // LANE, LANE), f32),
            pltpu.VMEM((small_count,) + tile, f32),
            dma((3 * len(sources),)),
            dma((hops,)),
            dma((hops,)),
            dma((few, len(targets))),
            dma((few, 2**bits)),
        ]
        + Reducer.scratch(depth, bits, phases),
        compiler_params=pltpu.CompilerParams(
            vmem_limit_bytes=62 * 2**20, collective_id=1, has_side_effects=True
        ),
    )(flat, early, gain, *sources, *weights)


def exchange_kernel(bits, state, totals_ref, entry_ref, arriving_ref, here, far, pre, post, send_sem, recv_sem):
    blk = lax.axis_index("blk")
    mine = [(blk // 2**b) % 2 for b in range(bits)]
    partner = [blk + (1 - 2 * mine[b]) * 2**b for b in range(bits)]
    barrier = pltpu.get_barrier_semaphore()
    for other in partner:
        pl.semaphore_signal(barrier, inc=1, device_id={"blk": other}, device_id_type=MESH)
    pl.semaphore_wait(barrier, bits)
    first, second, third = (slice(k * state, (k + 1) * state) for k in range(3))
    here[0] = totals_ref[...]
    entry_ref[...] = jnp.zeros_like(entry_ref)
    arriving_ref[...] = jnp.zeros_like(arriving_ref)
    pre[...] = jnp.ones_like(pre)
    post[...] = jnp.ones_like(post)
    for b in range(bits):
        if b < bits - 1:
            src, dst = here.at[b], far.at[b]
        else:
            src = here.at[b, pl.ds(pl.multiple_of((1 + mine[b]) * state, state), state)]
            dst = far.at[b, first]
        copy = pltpu.make_async_remote_copy(
            src_ref=src,
            dst_ref=dst,
            send_sem=send_sem.at[b],
            recv_sem=recv_sem.at[b],
            device_id={"blk": partner[b]},
            device_id_type=MESH,
        )
        copy.start()
        copy.wait()
        if b == bits - 1:

            @pl.when(mine[b] == 1)
            def _():
                entry_ref[...] += pre[...] * far[b, first]

            @pl.when(mine[b] == 0)
            def _():
                arriving_ref[...] += post[...] * far[b, first]

            continue

        @pl.when(mine[b] == 1)
        def _():
            entry_ref[...] += pre[...] * far[b, second]
            pre[...] *= far[b, first]
            here[b + 1, second] = here[b, second] + here[b, first] * far[b, second]
            here[b + 1, third] = far[b, third] + far[b, first] * here[b, third]

        @pl.when(mine[b] == 0)
        def _():
            arriving_ref[...] += post[...] * far[b, third]
            post[...] *= far[b, first]
            here[b + 1, second] = far[b, second] + far[b, first] * here[b, second]
            here[b + 1, third] = here[b, third] + here[b, first] * far[b, third]

        here[b + 1, first] = here[b, first] * far[b, first]


def exchange(totals, state):
    bits = lax.axis_size("blk").bit_length() - 1
    rows, inner = totals.shape
    vmem = pl.BlockSpec(memory_space=pltpu.VMEM)
    return pl.pallas_call(
        functools.partial(exchange_kernel, bits, state),
        name="exchange",
        in_specs=[vmem],
        out_specs=[vmem] * 2,
        out_shape=[jax.ShapeDtypeStruct((state, inner), f32)] * 2,
        scratch_shapes=[pltpu.VMEM((bits, rows, inner), f32)] * 2
        + [pltpu.VMEM((state, inner), f32)] * 2
        + [pltpu.SemaphoreType.DMA((bits,))] * 2,
        compiler_params=pltpu.CompilerParams(
            vmem_limit_bytes=VMEM_BYTES, collective_id=3, has_side_effects=True
        ),
    )(totals)


def local(
    tokens,
    out_cot,
    norm_gain,
    in_weight,
    conv_weight,
    conv_bias,
    xproj_weight,
    dt_weight,
    dt_bias,
    a_log,
    d_skip,
    out_weight,
    moment_one,
    moment_two,
):
    contract = (((0,), (0,)), ((), ()))
    backward = (((1,), (1,)), ((), ()))
    token_rows = interleave(tokens[0])
    cot_low = interleave(out_cot[0])
    source = token_rows.astype(f32)
    length = source.shape[0]
    inner = dt_bias.shape[0]
    state = a_log.shape[0]
    rank = dt_weight.shape[0]
    width = conv_weight.shape[0]
    halo = (width - 1) * SUB
    scale = lax.rsqrt(jnp.mean(source * source, axis=-1, keepdims=True) + EPS)
    normed = (source * scale * norm_gain).astype(bf16)
    stream = jnp.dot(normed, in_weight[:, :inner], preferred_element_type=f32)
    ends = stream[length - halo :].reshape(width - 1, SUB, inner)
    tail = shifted(ends[:, SUB - 1], "blk", 1)
    gating = jnp.dot(normed, in_weight[:, inner:], preferred_element_type=f32)
    grad_gated = lax.dot_general(cot_low, out_weight, backward, preferred_element_type=f32)
    head = jnp.concatenate([tail[:, None], ends[:, : SUB - 1]], 1).reshape(halo, inner)
    rates = -jnp.exp(a_log)
    rates_wide = jnp.repeat(rates * LOG2E, SUB, axis=0)
    spots = spread_table(2 * state)
    (
        conv_sum,
        conv_low,
        step_size,
        drive,
        grad_scanned,
        sel_low,
        terms,
        pre_decay,
        pre_state,
        post_decay,
        post_state,
        totals,
    ) = summary_call(
        stream,
        gating,
        grad_gated,
        head,
        conv_weight,
        conv_bias[None],
        xproj_weight,
        dt_weight,
        dt_bias[None],
        spots,
        rates_wide,
    )
    entry, arriving = exchange(totals, state)
    prior, readout_grads, gated, grad_gating, skip_grads = forward_call(
        step_size,
        drive,
        grad_scanned,
        terms,
        spots,
        rates_wide,
        pre_decay,
        pre_state,
        entry,
        conv_low,
        gating,
        grad_gated,
        d_skip[None],
    )
    grad_d_skip = jnp.sum(skip_grads, 0)

    span = moment_one.shape[0]
    small_rows = sum(
        value.size for value in (conv_weight, conv_bias, xproj_weight, dt_weight, dt_bias, a_log, d_skip)
    ) // ROW
    lead = (conv_weight.size + conv_bias.size) // ROW
    packed = xproj_weight.size // ROW
    rest = small_rows - lead - packed
    small_parts = ((0, packed, lead), (lead, 0, packed), (lead + packed, packed + lead, rest))
    regions = Regions(
        lax.axis_size("batch"),
        lax.axis_size("blk"),
        span,
        norm_gain.size // ROW,
        in_weight.shape,
        small_rows,
        out_weight.shape,
        small_parts,
    )
    flat_early = product_call((normed, grad_gating), (gated, cot_low))
    grad_stream_low, grad_pre_low, grad_selectors, rate_grads, taps_grads, edges, early = backward_call(
        step_size,
        drive,
        grad_scanned,
        terms,
        spots,
        rates_wide,
        post_state + post_decay * jnp.repeat(arriving, SUB, axis=0),
        prior,
        conv_sum,
        stream,
        readout_grads,
        dt_weight,
        xproj_weight,
        conv_weight,
        d_skip[None],
        flat_early,
        regions,
        rank,
    )
    grad_a_log = LN2 * jnp.sum(rate_grads.reshape(state, SUB, inner), 1)
    begins = edges[:halo].reshape(width - 1, SUB, inner)
    ahead = shifted(begins[:, 0], "blk", -1)
    grad_dt_weight = lax.dot_general(sel_low, grad_pre_low, contract, preferred_element_type=f32)[:rank]
    grad_xproj = lax.dot_general(conv_low, grad_selectors, contract, preferred_element_type=f32)
    foot = jnp.concatenate([begins[:, 1:], ahead[:, None]], 1)
    lasts = edges[halo:].reshape(width - 1, SUB, inner)
    further = jnp.concatenate([lasts, foot], 0)
    last_stream = stream[length - halo :].reshape(width - 1, SUB, inner)
    grad_last = conv_weight[width - 1] * lasts
    taps_grads = jnp.sum(taps_grads.reshape(width + 2, SUB, inner), 1)
    tap_grads = []
    for offset in range(width - 1):
        lead = width - 1 - offset
        grad_last = grad_last + conv_weight[offset] * further[lead : lead + width - 1]
        over = jnp.sum(last_stream[width - 1 - lead :] * foot[:lead], (0, 1))
        tap_grads.append(taps_grads[offset] + over)
    tap_grads.append(taps_grads[width - 1])
    grad_conv_weight = jnp.stack(tap_grads, 0)
    grad_conv_bias = taps_grads[width]
    grad_dt_bias = taps_grads[width + 1]
    grad_stream_low = lax.dynamic_update_slice_in_dim(
        grad_stream_low, grad_last.reshape(halo, inner).astype(bf16), length - halo, 0
    )
    thin = (grad_conv_weight, grad_conv_bias[None], grad_dt_weight, grad_dt_bias[None], grad_a_log, grad_d_skip[None])
    window, totals, result, grad_tokens, owned = late_call(
        product_call((normed, grad_stream_low), small=(grad_xproj, thin, rank + 2 * state)),
        early,
        norm_gain[None],
        (grad_gating, grad_stream_low, in_weight, token_rows, cot_low, gated, out_weight),
        (conv_weight, conv_bias[None], xproj_weight, dt_weight, dt_bias[None], a_log, d_skip[None]),
        regions,
    )
    result, grad_tokens = result[None], grad_tokens[None]
    grad_norm = jnp.sqrt(jnp.sum(totals[0]) + jnp.sum(totals[1] * totals[1]))
    owner = lax.axis_index(("batch", "blk"))
    begin = owner * span
    shard = lax.dynamic_slice_in_dim(window.reshape(-1), begin % ROW, span)
    owned = lax.dynamic_slice_in_dim(owned.reshape(-1), begin % ROW, span)
    lower = norm_gain.size + in_weight.size + sum(
        value.size for value in (conv_weight, conv_bias, xproj_weight, dt_weight)
    )
    upper = lower + dt_bias.size + a_log.size + d_skip.size
    place = begin + lax.iota(jnp.int32, span)
    keep = jnp.where((place >= lower) & (place < upper), 0.0, 1.0).astype(f32)
    clipped = shard * jnp.minimum(1.0, CLIP / (grad_norm + 1e-06))
    new_one = BETA_ONE * moment_one + (1.0 - BETA_ONE) * clipped
    new_two = BETA_TWO * moment_two + (1.0 - BETA_TWO) * clipped * clipped
    first = new_one / (1.0 - BETA_ONE**ADAM_STEP)
    second = new_two / (1.0 - BETA_TWO**ADAM_STEP)
    param_step = -RATE * (first / (jnp.sqrt(second) + ADAM_EPS) + DECAY * keep * owned)
    return (result, grad_tokens, shard, grad_norm, param_step, new_one, new_two)


def solution(mesh):
    return jax.shard_map(
        local,
        mesh=mesh,
        in_specs=(P("batch", "blk", None),) * 2 + (P(),) * 10 + (P(("batch", "blk")),) * 2,
        out_specs=(P("batch", "blk", None),) * 2
        + (P(("batch", "blk")), P(), P(("batch", "blk")), P(("batch", "blk")), P(("batch", "blk"))),
        check_vma=False,
    )
```

```python
import functools
import math

import jax
import jax.numpy as jnp
from jax import lax
from jax.experimental import pallas as pl
from jax.experimental.pallas import tpu as pltpu
from jax.sharding import PartitionSpec as P

ADAM_STEP = 100
EPS = 1e-05
RATE = 0.002
BETA_ONE = 0.9
BETA_TWO = 0.95
ADAM_EPS = 1e-08
DECAY = 0.1
CLIP = 1.0

LOG2E = 1.0 / math.log(2.0)
LN2 = math.log(2.0)
SUB = 8
LANE = 128
ROW = 1024
VMEM_BYTES = 56 * 2**20

MESH = pl.DeviceIdType.MESH

f32 = jnp.float32
bf16 = jnp.bfloat16


def shifted(x, axis, by):
    count = lax.axis_size(axis)
    pairs = [(i, i + by) for i in range(count) if 0 <= i + by < count]
    return lax.ppermute(x, axis, pairs)


def silu_slope(value):
    sig = jax.nn.sigmoid(value)
    return sig * (1.0 + value * (1.0 - sig))


def interleave(x):
    rows, width = x.shape
    return x.reshape(SUB, rows // SUB, width).transpose(1, 0, 2).reshape(rows, width)


def restore(x):
    rows, width = x.shape
    return x.reshape(rows // SUB, SUB, width).transpose(1, 0, 2).reshape(rows, width)


def at(start, size):
    return pl.ds(pl.multiple_of(start, size), size)


def spread(sel_ref, spots_ref, out_ref):
    out_ref[...] = jnp.dot(sel_ref[...], spots_ref[...], preferred_element_type=f32)


def gather_table(out_ref):
    row = lax.broadcasted_iota(jnp.int32, (LANE, LANE), 1)
    for n in range(out_ref.shape[0] // LANE):
        out_ref[n * LANE : (n + 1) * LANE, :] = jnp.where(row == n, 1.0, 0.0).astype(bf16)


def gather_lanes(src_ref, table_ref, out_ref):
    out_ref[...] = jnp.dot(src_ref[...].astype(bf16), table_ref[...], preferred_element_type=f32)


def spread_table(count):
    row = lax.broadcasted_iota(jnp.int32, (LANE, count * LANE), 0)
    col = lax.broadcasted_iota(jnp.int32, (LANE, count * LANE), 1) // LANE
    return ((row % count == col) & (row < 3 * count)).astype(bf16)


def summary_kernel(
    shape,
    stream_ref,
    gating_ref,
    grad_gated_ref,
    head_ref,
    taps_ref,
    bias_ref,
    select_in_ref,
    step_in_ref,
    step_bias_ref,
    spots_ref,
    rates_ref,
    conv_sum_ref,
    conv_ref,
    step_ref,
    drive_ref,
    grad_ref,
    low_ref,
    sel_ref,
    pre_decay_ref,
    pre_state_ref,
    post_decay_ref,
    post_state_ref,
    totals_ref,
    end_ref,
    exit_ref,
    prod_ref,
    select_ref,
    longer_ref,
    wide_ref,
):
    tiles, state, inner, cols, group = shape
    turn = pl.program_id(0)
    block = tiles * SUB
    width = taps_ref.shape[0]
    halo = (width - 1) * SUB

    @pl.when(turn == 0)
    def _():
        end_ref[...] = jnp.zeros_like(end_ref)
        exit_ref[...] = jnp.zeros_like(exit_ref)
        prod_ref[...] = jnp.ones_like(prod_ref)
        longer_ref[:halo, :] = head_ref[...]

    @pl.when(turn > 0)
    def _():
        longer_ref[:halo, :] = longer_ref[block:, :]

    longer_ref[halo:, :] = stream_ref[...]

    def convs(c, carry):
        lanes = at(c * 2 * LANE, 2 * LANE)
        taps = [jnp.broadcast_to(taps_ref[k : k + 1, lanes], (2 * SUB, 2 * LANE)) for k in range(width)]
        bias = bias_ref[:, lanes]

        def pair(i, carry):
            here = at(i * 2 * SUB, 2 * SUB)
            total = bias + taps[width - 1] * stream_ref[here, lanes]
            for k in range(width - 1):
                total = total + taps[k] * longer_ref[pl.ds(pl.multiple_of((2 * i + k) * SUB, SUB), 2 * SUB), lanes]
            conv_sum_ref[here, lanes] = total
            conv_ref[here, lanes] = (total * jax.nn.sigmoid(total)).astype(bf16)
            gating = gating_ref[here, lanes]
            grad_ref[here, lanes] = grad_gated_ref[here, lanes] * (gating * jax.nn.sigmoid(gating))
            return carry

        lax.fori_loop(0, tiles // 2, pair, 0, unroll=tiles // 2)
        return carry

    lax.fori_loop(0, inner // (2 * LANE), convs, 0)
    lane = lax.broadcasted_iota(jnp.int32, (block, LANE), 1)
    rank = step_in_ref.shape[0]
    used = rank + 2 * state
    wide_ref[...] = jnp.zeros_like(wide_ref)
    wide_ref[:, :used] = jnp.dot(conv_ref[...], select_in_ref[...], preferred_element_type=f32)
    selectors = wide_ref[...]
    low_ref[...] = selectors.astype(bf16)
    low = low_ref[:, :rank]
    value = jnp.where(lane < 2 * state, pltpu.roll(selectors, LANE - rank, 1), 0.0)
    high = value.astype(bf16).astype(f32)
    middle = (value - high).astype(bf16).astype(f32)
    rest = value - high - middle
    sel_ref[...] = (high + pltpu.roll(middle, 2 * state, 1) + pltpu.roll(rest, 4 * state, 1)).astype(bf16)

    step_ref[...] = jnp.dot(low, step_in_ref[...], preferred_element_type=f32)

    def steps(c, carry):
        lanes = at(c * 2 * LANE, 2 * LANE)
        bias = step_bias_ref[:, lanes]

        def pair(i, carry):
            here = at(i * 2 * SUB, 2 * SUB)
            pre = step_ref[here, lanes] + bias
            step = jnp.maximum(pre, 0.0) + jnp.log1p(jnp.exp(-jnp.abs(pre)))
            step_ref[here, lanes] = step
            drive_ref[here, lanes] = step * conv_ref[here, lanes].astype(f32)
            return carry

        lax.fori_loop(0, tiles // 2, pair, 0, unroll=tiles // 2)
        return carry

    lax.fori_loop(0, inner // (2 * LANE), steps, 0)
    spread(sel_ref, spots_ref, select_ref)

    def columns(c, carry):
        lanes = [at((c * cols + k) * LANE, LANE) for k in range(cols)]
        for first in range(0, state, group):
            spots = [(n, k) for n in range(group) for k in range(cols)]
            where = [(slice((first + n) * SUB, (first + n + 1) * SUB), lanes[k]) for n, k in spots]
            rates = [rates_ref[w] for w in where]

            def advance(i, carry):
                ends, exits, prods = carry
                here = at(i * SUB, SUB)
                step = [step_ref[here, l] for l in lanes]
                drive = [drive_ref[here, l] for l in lanes]
                grad = [grad_ref[here, l] for l in lanes]
                inject = [select_ref[here, (first + n) * LANE : (first + n + 1) * LANE] for n in range(group)]
                readout = [
                    select_ref[here, (state + first + n) * LANE : (state + first + n + 1) * LANE] for n in range(group)
                ]
                new = ([], [], [])
                for s, (n, k) in enumerate(spots):
                    decay = jnp.exp2(step[k] * rates[s])
                    prod = prods[s] * decay
                    new[0].append(ends[s] * decay + drive[k] * inject[n])
                    new[1].append(exits[s] + prod * (grad[k] * readout[n]))
                    new[2].append(prod)
                return tuple(tuple(x) for x in new)

            start = tuple(tuple(ref[w] for w in where) for ref in (end_ref, exit_ref, prod_ref))
            ends, exits, prods = lax.fori_loop(0, tiles, advance, start, unroll=16)
            for s, w in enumerate(where):
                end_ref[w] = ends[s]
                exit_ref[w] = exits[s]
                prod_ref[w] = prods[s]
        return carry

    lax.fori_loop(0, inner // (LANE * cols), columns, 0)

    @pl.when(turn == pl.num_programs(0) - 1)
    def _():
        row = lax.broadcasted_iota(jnp.int32, (SUB, LANE), 0)

        def columns(c, carry):
            lanes = at(c * LANE, LANE)
            for n in range(state):
                here = (slice(n * SUB, (n + 1) * SUB), lanes)
                for way, src, decay_out, state_out, total_row in (
                    (1, end_ref, pre_decay_ref, pre_state_ref, 1),
                    (-1, exit_ref, post_decay_ref, post_state_ref, 2),
                ):
                    decay, value = prod_ref[here], src[here]

                    def seen(by):
                        return row >= by if way > 0 else row < SUB - by

                    for by in (1, 2, 4):
                        far_decay = pltpu.roll(decay, by if way > 0 else SUB - by, 0)
                        far_value = pltpu.roll(value, by if way > 0 else SUB - by, 0)
                        value = jnp.where(seen(by), value + decay * far_value, value)
                        decay = jnp.where(seen(by), decay * far_decay, decay)
                    last = SUB - 1 if way > 0 else 0
                    totals_ref[pl.ds(n, 1), lanes] = decay[last : last + 1]
                    totals_ref[pl.ds(total_row * state + n, 1), lanes] = value[last : last + 1]
                    turn_by = 1 if way > 0 else SUB - 1
                    decay_out[here] = jnp.where(seen(1), pltpu.roll(decay, turn_by, 0), 1.0)
                    state_out[here] = jnp.where(seen(1), pltpu.roll(value, turn_by, 0), 0.0)
            return carry

        lax.fori_loop(0, inner // LANE, columns, 0)


def forward_kernel(
    shape,
    step_ref,
    drive_ref,
    grad_ref,
    sel_ref,
    spots_ref,
    rates_ref,
    pre_decay_ref,
    pre_state_ref,
    entry_ref,
    conv_ref,
    gating_ref,
    grad_gated_ref,
    skip_ref,
    prior_ref,
    readout_grad_ref,
    gated_ref,
    grad_gating_ref,
    skip_grad_ref,
    state_ref,
    select_ref,
    sums_ref,
    scanned_ref,
    table_ref,
):
    tiles, state, inner, cols, group = shape

    @pl.when(pl.program_id(0) == 0)
    def _():
        skip_grad_ref[...] = jnp.zeros_like(skip_grad_ref)
        gather_table(table_ref)
        for n in range(state):
            here = slice(n * SUB, (n + 1) * SUB)
            state_ref[here, :] = pre_state_ref[here, :] + pre_decay_ref[here, :] * entry_ref[n : n + 1, :]

    spread(sel_ref, spots_ref, select_ref)
    sums_ref[...] = jnp.zeros_like(sums_ref)

    def columns(c, carry):
        lanes = [at((c * cols + k) * LANE, LANE) for k in range(cols)]
        for first in range(0, state, group):
            spots = [(n, k) for n in range(group) for k in range(cols)]
            where = [(slice((first + n) * SUB, (first + n + 1) * SUB), lanes[k]) for n, k in spots]
            rates = [rates_ref[w] for w in where]

            def advance(i, states):
                here = at(i * SUB, SUB)
                step = [step_ref[here, l] for l in lanes]
                drive = [drive_ref[here, l] for l in lanes]
                grad = [grad_ref[here, l] for l in lanes]
                outs = [None] * cols
                new = []
                for n in range(group):
                    spot = slice((first + n) * LANE, (first + n + 1) * LANE)
                    inject = select_ref[here, spot]
                    readout = select_ref[here, (state + first + n) * LANE : (state + first + n + 1) * LANE]
                    total = None
                    for k in range(cols):
                        s = n * cols + k
                        decay = jnp.exp2(step[k] * rates[s])
                        fresh = decay * states[s] + drive[k] * inject
                        new.append(fresh)
                        part = readout * fresh
                        outs[k] = part if outs[k] is None else outs[k] + part
                        part = grad[k] * fresh
                        total = part if total is None else total + part
                    sums_ref[here, spot] += total
                    if n % 2 == 1:
                        pair = pl.ds(pl.multiple_of((i * state + first + n - 1) * SUB, 2 * SUB), 2 * SUB)
                        for k in range(cols):
                            prior_ref[pair, lanes[k]] = jnp.concatenate(
                                [states[(n - 1) * cols + k], states[n * cols + k]], 0
                            ).astype(bf16)
                for k in range(cols):
                    if first == 0:
                        scanned_ref[here, lanes[k]] = outs[k]
                    else:
                        scanned_ref[here, lanes[k]] += outs[k]
                return tuple(new)

            states = lax.fori_loop(0, tiles, advance, tuple(state_ref[w] for w in where), unroll=16)
            for s, w in enumerate(where):
                state_ref[w] = states[s]
        return carry

    lax.fori_loop(0, inner // (LANE * cols), columns, 0)
    gather_lanes(sums_ref, table_ref, readout_grad_ref)

    def finish(c, carry):
        lanes = at(c * 2 * LANE, 2 * LANE)
        skip = skip_ref[:, lanes]

        def pair(i, total):
            here = at(i * 2 * SUB, 2 * SUB)
            conv = conv_ref[here, lanes].astype(f32)
            gating = gating_ref[here, lanes]
            sig = jax.nn.sigmoid(gating)
            gate = gating * sig
            scanned = scanned_ref[here, lanes] + skip * conv
            gated_ref[here, lanes] = (scanned * gate).astype(bf16)
            slope = sig + gate * (1.0 - sig)
            grad_gating_ref[here, lanes] = (grad_gated_ref[here, lanes] * scanned * slope).astype(bf16)
            product = grad_ref[here, lanes] * conv
            return total + product[:SUB] + product[SUB:]

        zero = jnp.zeros((SUB, 2 * LANE), f32)
        skip_grad_ref[:, lanes] += lax.fori_loop(0, tiles // 2, pair, zero, unroll=tiles // 2)
        return carry

    lax.fori_loop(0, inner // (2 * LANE), finish, 0)


def backward_kernel(
    shape,
    scan_turns,
    regions,
    bits,
    phases,
    step_ref,
    drive_ref,
    grad_ref,
    sel_ref,
    spots_ref,
    rates_ref,
    begin_ref,
    prior_ref,
    conv_sum_ref,
    stream_ref,
    readout_grad_ref,
    step_back_ref,
    select_back_ref,
    taps_ref,
    skip_ref,
    flat_ref,
    grad_stream_ref,
    grad_pre_ref,
    grad_select_ref,
    rate_grad_ref,
    taps_grad_ref,
    edge_ref,
    early_ref,
    carry_ref,
    select_ref,
    sums_ref,
    through_ref,
    feed_ref,
    grad_conv_ref,
    inject_grad_ref,
    low_grad_ref,
    table_ref,
    *refs,
):
    tiles, state, inner, cols, group, rank = shape
    block = tiles * SUB
    width = taps_ref.shape[0]
    halo = (width - 1) * SUB
    turn = pl.program_id(0)
    work = Reducer(
        regions.depth,
        bits,
        phases,
        1,
        lambda p, owner: regions.early_start(phases[p][0], owner) + phases[p][1],
        flat_ref,
        refs,
    )
    turns = scan_turns
    early = max(work.slots - turns, 0)
    for g in range(turns):

        @pl.when(turn == g)
        def _():
            if g == 0:
                work.greet()
            for t in range(0 if g == 0 else g + early, min(g + early + 1, work.slots)):
                work.run(t)

    @pl.when(pl.program_id(0) == 0)
    def _():
        gather_table(table_ref)
        rate_grad_ref[...] = jnp.zeros_like(rate_grad_ref)
        taps_grad_ref[...] = jnp.zeros_like(taps_grad_ref)
        grad_conv_ref[tiles * SUB :, :] = jnp.zeros((grad_conv_ref.shape[0] - tiles * SUB, inner), f32)
        carry_ref[...] = begin_ref[...]

    spread(sel_ref, spots_ref, select_ref)
    sums_ref[...] = jnp.zeros_like(sums_ref)

    def columns(c, carry):
        lanes = [at((c * cols + k) * LANE, LANE) for k in range(cols)]
        for first in range(0, state, group):
            spots = [(n, k) for n in range(group) for k in range(cols)]
            where = [(slice((first + n) * SUB, (first + n + 1) * SUB), lanes[k]) for n, k in spots]
            rates = [rates_ref[w] for w in where]

            def retreat(turn, carry):
                carries, rate_grads = carry
                i = tiles - 1 - turn
                here = at(i * SUB, SUB)
                step = [step_ref[here, l] for l in lanes]
                drive = [drive_ref[here, l] for l in lanes]
                grad = [grad_ref[here, l] for l in lanes]
                throughs = [None] * cols
                feeds = [None] * cols
                new = ([], [])
                for n in range(group):
                    spot = slice((first + n) * LANE, (first + n + 1) * LANE)
                    inject = select_ref[here, spot]
                    readout = select_ref[here, (state + first + n) * LANE : (state + first + n + 1) * LANE]
                    if n % 2 == 0:
                        pair = pl.ds(pl.multiple_of((i * state + first + n) * SUB, 2 * SUB), 2 * SUB)
                        pairs = [prior_ref[pair, lanes[k]].astype(f32) for k in range(cols)]
                    total = None
                    for k in range(cols):
                        s = n * cols + k
                        prior = pairs[k][(n % 2) * SUB : (n % 2 + 1) * SUB]
                        power = step[k] * rates[s]
                        adjoint = grad[k] * readout + carries[s]
                        back = jnp.exp2(power) * adjoint
                        through = back * prior * power
                        new[0].append(back)
                        new[1].append(rate_grads[s] + through)
                        throughs[k] = through if throughs[k] is None else throughs[k] + through
                        part = adjoint * inject
                        feeds[k] = part if feeds[k] is None else feeds[k] + part
                        part = adjoint * drive[k]
                        total = part if total is None else total + part
                    sums_ref[here, spot] += total
                for k in range(cols):
                    if first == 0:
                        through_ref[here, lanes[k]] = throughs[k]
                        feed_ref[here, lanes[k]] = feeds[k]
                    else:
                        through_ref[here, lanes[k]] += throughs[k]
                        feed_ref[here, lanes[k]] += feeds[k]
                return tuple(tuple(x) for x in new)

            start = tuple(tuple(ref[w] for w in where) for ref in (carry_ref, rate_grad_ref))
            carries, rate_grads = lax.fori_loop(0, tiles, retreat, start, unroll=8)
            for s, w in enumerate(where):
                carry_ref[w] = carries[s]
                rate_grad_ref[w] = rate_grads[s]
        return carry

    lax.fori_loop(0, inner // (LANE * cols), columns, 0)
    gather_lanes(sums_ref, table_ref, inject_grad_ref)

    def steps(c, carry):
        lanes = at(c * 2 * LANE, 2 * LANE)

        def pair(i, total):
            here = at(i * 2 * SUB, 2 * SUB)
            step = step_ref[here, lanes]
            series = 1.0 + step * (-1.0 / 2 + step * (1.0 / 6 + step * (-1.0 / 24 + step * (1.0 / 120))))
            near = step < 0.06
            exact = (1.0 - jnp.exp2(step * -LOG2E)) / jnp.where(near, 1.0, step)
            ratio = jnp.where(near, series, exact)
            pre = ratio * (LN2 * through_ref[here, lanes] + drive_ref[here, lanes] * feed_ref[here, lanes])
            grad_pre_ref[here, lanes] = pre.astype(bf16)
            return total + pre[:SUB] + pre[SUB:]

        zero = jnp.zeros((SUB, 2 * LANE), f32)
        taps_grad_ref[(width + 1) * SUB :, lanes] += lax.fori_loop(0, tiles // 2, pair, zero, unroll=tiles // 2)
        return carry

    lax.fori_loop(0, inner // (2 * LANE), steps, 0)
    lane = lax.broadcasted_iota(jnp.int32, (block, LANE), 1)
    across = (((1,), (1,)), ((), ()))
    low_grad_ref[:, :rank] = lax.dot_general(
        grad_pre_ref[...], step_back_ref[...], across, preferred_element_type=f32
    )
    grads = low_grad_ref[...]
    inject_grad = pltpu.roll(inject_grad_ref[...], rank, 1)
    readout_grad = pltpu.roll(readout_grad_ref[...], rank + state, 1)
    grads = jnp.where(lane < rank, grads, jnp.where(lane < rank + state, inject_grad, readout_grad))
    grads = jnp.where(lane < rank + 2 * state, grads, 0.0)
    grads = grads.astype(bf16)
    grad_select_ref[...] = grads

    through_ref[...] = lax.dot_general(
        grad_select_ref[:, : rank + 2 * state], select_back_ref[...], across, preferred_element_type=f32
    )

    def convs(c, carry):
        lanes = at(c * 2 * LANE, 2 * LANE)
        skip = skip_ref[:, lanes]

        def conv(i, carry):
            here = at(i * SUB, SUB)
            value = conv_sum_ref[here, lanes]
            sig = jax.nn.sigmoid(value)
            slope = sig * (1.0 + value * (1.0 - sig))
            out = grad_ref[here, lanes] * skip + step_ref[here, lanes] * feed_ref[here, lanes] + through_ref[here, lanes]
            grad_conv_ref[here, lanes] = out * slope
            return carry

        lax.fori_loop(0, tiles, conv, 0, unroll=8)
        taps = [jnp.broadcast_to(taps_ref[k : k + 1, lanes], (SUB, 2 * LANE)) for k in range(width)]

        def tap(i, totals):
            totals = list(totals)
            done = []
            for q in range(2):
                parts = [
                    grad_conv_ref[pl.ds(pl.multiple_of((2 * i + q + m) * SUB, SUB), SUB), lanes] for m in range(width)
                ]
                stream = stream_ref[pl.ds(pl.multiple_of((2 * i + q) * SUB, SUB), SUB), lanes]
                grad = taps[width - 1] * parts[0]
                totals[width - 1] = totals[width - 1] + parts[0] * stream
                totals[width] = totals[width] + parts[0]
                for m in range(1, width):
                    grad = grad + taps[width - 1 - m] * parts[m]
                    totals[width - 1 - m] = totals[width - 1 - m] + parts[m] * stream
                done.append(grad)
            grad_stream_ref[at(i * 2 * SUB, 2 * SUB), lanes] = jnp.concatenate(done, 0).astype(bf16)
            return tuple(totals)

        zero = jnp.zeros((SUB, 2 * LANE), f32)
        totals = lax.fori_loop(0, tiles // 2, tap, (zero,) * (width + 1), unroll=tiles // 2)
        for k in range(width + 1):
            taps_grad_ref[k * SUB : (k + 1) * SUB, lanes] += totals[k]
        return carry

    lax.fori_loop(0, inner // (2 * LANE), convs, 0)

    @pl.when(pl.program_id(0) == 0)
    def _():
        edge_ref[halo:, :] = grad_conv_ref[block - halo : block, :]

    edge_ref[:halo, :] = grad_conv_ref[:halo, :]
    grad_conv_ref[block:, :] = grad_conv_ref[:halo, :]

    @pl.when(turn == turns - 1)
    def _():
        work.collect(early_ref)


def scan_shapes(rows, state, inner, tiles=16):
    tiles = min(tiles, rows // SUB)
    count = rows // (SUB * tiles)
    return tiles, count


def summary_call(stream, gating, grad_gated, head, taps, bias, select_in, step_in, step_bias, spots, rates):
    rows, inner = stream.shape
    state = rates.shape[0] // SUB
    tiles, count = scan_shapes(rows, state, inner)
    halo = head.shape[0]
    wide = pl.BlockSpec((tiles * SUB, inner), lambda t: (t, 0))
    thin = pl.BlockSpec((tiles * SUB, LANE), lambda t: (t, 0))
    whole = pl.BlockSpec((state * SUB, inner), lambda t: (0, 0))
    total = pl.BlockSpec((3 * state, inner), lambda t: (0, 0))
    shape = (tiles, state, inner, 2, 4)
    big = jax.ShapeDtypeStruct((state * SUB, inner), f32)
    full = jax.ShapeDtypeStruct((rows, inner), f32)
    slim = jax.ShapeDtypeStruct((rows, LANE), bf16)

    def fixed(x):
        return pl.BlockSpec(x.shape, lambda t: (0, 0), pipeline_mode=pl.Buffered(1))

    constants = (head, taps, bias, select_in, step_in, step_bias, spots, rates)
    return pl.pallas_call(
        functools.partial(summary_kernel, shape),
        name="scan_summary",
        grid=(count,),
        in_specs=[wide, wide, wide] + [fixed(x) for x in constants],
        out_specs=[wide] * 5 + [thin] * 2 + [whole] * 4 + [total],
        out_shape=[full, jax.ShapeDtypeStruct((rows, inner), bf16), full, full, full, slim, slim]
        + [big] * 4
        + [jax.ShapeDtypeStruct((3 * state, inner), f32)],
        scratch_shapes=[pltpu.VMEM((state * SUB, inner), f32)] * 3
        + [
            pltpu.VMEM((tiles * SUB, 2 * state * LANE), f32),
            pltpu.VMEM((halo + tiles * SUB, inner), f32),
            pltpu.VMEM((tiles * SUB, LANE), f32),
        ],
        compiler_params=pltpu.CompilerParams(vmem_limit_bytes=VMEM_BYTES),
    )(stream, gating, grad_gated, *constants)


def forward_call(step, drive, grad, sel, spots, rates, pre_decay, pre_state, entry, conv, gating, grad_gated, skip):
    rows, inner = step.shape
    state = rates.shape[0] // SUB
    tiles, count = scan_shapes(rows, state, inner)
    wide = pl.BlockSpec((tiles * SUB, inner), lambda t: (t, 0))
    table = pl.BlockSpec(spots.shape, lambda t: (0, 0))
    thin = pl.BlockSpec((tiles * SUB, sel.shape[1]), lambda t: (t, 0))
    whole = pl.BlockSpec((state * SUB, inner), lambda t: (0, 0), pipeline_mode=pl.Buffered(1))
    line = pl.BlockSpec((1, inner), lambda t: (0, 0))
    short = pl.BlockSpec((state, inner), lambda t: (0, 0))
    shape = (tiles, state, inner, 2, 8)
    return pl.pallas_call(
        functools.partial(forward_kernel, shape),
        name="scan_forward",
        grid=(count,),
        in_specs=[wide, wide, wide, thin, table, whole, whole, whole, short, wide, wide, wide, line],
        out_specs=[
            pl.BlockSpec((tiles * state * SUB, inner), lambda t: (t, 0)),
            pl.BlockSpec((tiles * SUB, LANE), lambda t: (t, 0)),
            wide,
            wide,
            pl.BlockSpec((SUB, inner), lambda t: (0, 0)),
        ],
        out_shape=[
            jax.ShapeDtypeStruct((rows * state, inner), bf16),
            jax.ShapeDtypeStruct((rows, LANE), f32),
            jax.ShapeDtypeStruct((rows, inner), bf16),
            jax.ShapeDtypeStruct((rows, inner), bf16),
            jax.ShapeDtypeStruct((SUB, inner), f32),
        ],
        scratch_shapes=[pltpu.VMEM((state * SUB, inner), f32)]
        + [
            pltpu.VMEM((tiles * SUB, 2 * state * LANE), f32),
            pltpu.VMEM((tiles * SUB, state * LANE), f32),
            pltpu.VMEM((tiles * SUB, inner), f32),
            pltpu.VMEM((state * LANE, LANE), bf16),
        ],
        compiler_params=pltpu.CompilerParams(vmem_limit_bytes=VMEM_BYTES),
    )(step, drive, grad, sel, spots, rates, pre_decay, pre_state, entry, conv, gating, grad_gated, skip)


def backward_call(step, drive, grad, sel, spots, rates, begin, prior, conv_sum, stream, readout_grad, step_back, select_back, taps, skip, flat, regions, rank):
    rows, inner = step.shape
    state = rates.shape[0] // SUB
    tiles, count = scan_shapes(rows, state, inner, 8)
    bits = regions.count.bit_length() - 1
    phases = regions.early_phases()

    def back(t):
        return (count - 1 - t, 0)

    wide = pl.BlockSpec((tiles * SUB, inner), back)
    table = pl.BlockSpec(spots.shape, lambda t: (0, 0), pipeline_mode=pl.Buffered(1))
    thin = pl.BlockSpec((tiles * SUB, sel.shape[1]), back)
    whole = pl.BlockSpec((state * SUB, inner), lambda t: (0, 0), pipeline_mode=pl.Buffered(1))
    narrow = pl.BlockSpec((tiles * SUB, LANE), back)
    width = taps.shape[0]
    halo = (width - 1) * SUB

    def fixed(x):
        return pl.BlockSpec(x.shape, lambda t: (0, 0), pipeline_mode=pl.Buffered(1))

    shape = (tiles, state, inner, 2, 4, rank)
    return pl.pallas_call(
        functools.partial(backward_kernel, shape, count, regions, bits, phases),
        name="scan_backward",
        grid=(count,),
        in_specs=[wide, wide, wide, thin, table, whole, whole]
        + [pl.BlockSpec((tiles * state * SUB, inner), back), wide, wide, narrow]
        + [fixed(step_back), fixed(select_back), fixed(taps), fixed(skip)]
        + [pl.BlockSpec(memory_space=pl.ANY)],
        out_specs=[
            wide,
            wide,
            narrow,
            pl.BlockSpec((state * SUB, inner), lambda t: (0, 0)),
            pl.BlockSpec(((width + 2) * SUB, inner), lambda t: (0, 0)),
            pl.BlockSpec((2 * halo, inner), lambda t: (0, 0)),
            pl.BlockSpec((regions.slot, SUB, LANE), lambda t: (0, 0, 0)),
        ],
        out_shape=[
            jax.ShapeDtypeStruct((rows, inner), bf16),
            jax.ShapeDtypeStruct((rows, inner), bf16),
            jax.ShapeDtypeStruct((rows, LANE), bf16),
            jax.ShapeDtypeStruct((state * SUB, inner), f32),
            jax.ShapeDtypeStruct(((width + 2) * SUB, inner), f32),
            jax.ShapeDtypeStruct((2 * halo, inner), f32),
            jax.ShapeDtypeStruct((regions.slot, SUB, LANE), f32),
        ],
        scratch_shapes=[pltpu.VMEM((state * SUB, inner), f32)]
        + [
            pltpu.VMEM((tiles * SUB, 2 * state * LANE), f32),
            pltpu.VMEM((tiles * SUB, state * LANE), f32),
            pltpu.VMEM((tiles * SUB, inner), f32),
            pltpu.VMEM((tiles * SUB, inner), f32),
            pltpu.VMEM((tiles * SUB + halo, inner), f32),
            pltpu.VMEM((tiles * SUB, LANE), f32),
            pltpu.VMEM((tiles * SUB, LANE), f32),
            pltpu.VMEM((state * LANE, LANE), bf16),
        ]
        + Reducer.scratch(regions.depth, bits, phases),
        compiler_params=pltpu.CompilerParams(
            vmem_limit_bytes=62 * 2**20, collective_id=2, has_side_effects=True
        ),
    )(step, drive, grad, sel, spots, rates, begin, prior, conv_sum, stream, readout_grad, step_back, select_back, taps, skip, flat)


def turn_tiles(tiles):
    row = lax.broadcasted_iota(jnp.int32, (SUB, LANE), 0)
    for bit in (1, 2, 4):
        upper = (row // bit) % 2 == 1
        new = list(tiles)
        for a in range(SUB):
            if a & bit == 0:
                b = a + bit
                new[a] = jnp.where(upper, pltpu.roll(tiles[b], bit, 0), tiles[a])
                new[b] = jnp.where(upper, tiles[b], pltpu.roll(tiles[a], SUB - bit, 0))
        tiles = new
    return tiles


def pack_columns(src_ref, used, out_ref):
    part = LANE - used
    rows = src_ref.shape[0] // 4
    lane = lax.broadcasted_iota(jnp.int32, (SUB, LANE), 1)
    flat = out_ref

    def one(g, carry):
        quads = [src_ref[pl.ds(g * 4 * SUB + q, SUB, stride=4), :] for q in range(4)]
        for m in range(3):
            first = quads[m] if m == 0 else pltpu.roll(quads[m], LANE - m * part, 1)
            second = pltpu.roll(quads[m + 1], used - m * part, 1)
            flat[pl.ds(g * 3 * SUB + m, SUB, stride=3), :] = jnp.where(lane < used - m * part, first, second)
        return carry

    lax.fori_loop(0, rows // SUB, one, 0, unroll=4)


def row_tile(src_ref, r, q):
    return jnp.concatenate(
        [src_ref[r : r + 1, (q * SUB + a) * LANE : (q * SUB + a + 1) * LANE] for a in range(SUB)], 0
    )


def product_kernel(steps, shapes, used, *refs):
    if used:
        out_ref, held_ref, packed_ref = refs[-3:]
    else:
        out_ref, held_ref = refs[-2:]
    contract = (((0,), (0,)), ((), ()))
    step = pl.program_id(0)

    def lay(src_ref, first, rows, base, per, q):
        def one(r, carry):
            tiles = [
                src_ref[at(r * SUB, SUB), (first + a) * LANE : (first + a + 1) * LANE] for a in range(SUB)
            ]
            for b, tile in enumerate(turn_tiles(tiles)):
                out_ref[base + (r * SUB + b) * per + q] = tile
            return carry

        lax.fori_loop(0, rows // SUB, one, 0, unroll=rows // SUB)

    for turn, (rows, width) in enumerate(shapes):
        left_ref, right_ref = refs[2 * turn : 2 * turn + 2]
        per = width // ROW

        @pl.when(step // steps == turn)
        def _():
            for q in range(per):
                held_ref[q, :rows] = lax.dot_general(
                    left_ref[...], right_ref[:, q * ROW : (q + 1) * ROW], contract, preferred_element_type=f32
                )
                lay(held_ref.at[q], 0, rows, 0, per, q)

    if not used:
        return
    wide_ref, *thin_refs = refs[2 * len(shapes) : -3]
    tiles = packed_ref.shape[0] // SUB

    @pl.when(step == steps * len(shapes))
    def _():
        pack_columns(wide_ref, used, packed_ref)

        def one(i, carry):
            out_ref[i] = packed_ref[at(i * SUB, SUB), :]
            return carry

        out_ref[...] = jnp.zeros_like(out_ref)
        lax.fori_loop(0, tiles, one, 0, unroll=8)
        base = tiles
        for ref in thin_refs:
            rows, per = ref.shape[0], ref.shape[1] // ROW
            for q in range(per):
                if rows % SUB == 0:
                    lay(ref, q * SUB, rows, base, per, q)
                else:
                    for r in range(rows):
                        out_ref[base + r * per + q] = row_tile(ref, r, q)
            base += rows * per


def product_call(*pairs, small=None):
    steps = 4
    shapes = [(left.shape[1] // steps, right.shape[1]) for left, right in pairs]
    size = shapes[0][0] * shapes[0][1] // ROW

    def block(k):
        return lambda t: (0, jnp.clip(t - k * steps, 0, steps - 1))

    specs = []
    for k, (left, right) in enumerate(pairs):
        specs.append(pl.BlockSpec((left.shape[0], left.shape[1] // steps), block(k)))
        specs.append(pl.BlockSpec(right.shape, lambda t: (0, 0), pipeline_mode=pl.Buffered(1)))
    args = [x for pair in pairs for x in pair]
    scratch = [pltpu.VMEM((shapes[0][1] // ROW, max(rows for rows, _ in shapes), ROW), f32)]
    used, extra = 0, 0
    if small is not None:
        wide, thin, used = small
        extra = 1
        scratch.append(pltpu.VMEM((wide.shape[0] * used // LANE, LANE), f32))
        for x in (wide,) + thin:
            specs.append(pl.BlockSpec(x.shape, lambda t: (0, 0), pipeline_mode=pl.Buffered(1)))
            args.append(x)
    grid = steps * len(pairs) + extra
    return pl.pallas_call(
        functools.partial(product_kernel, steps, shapes, used),
        name="flat_product",
        grid=(grid,),
        in_specs=specs,
        out_specs=pl.BlockSpec((size, SUB, LANE), lambda t: (t, 0, 0)),
        out_shape=jax.ShapeDtypeStruct((size * grid, SUB, LANE), f32),
        scratch_shapes=scratch,
        compiler_params=pltpu.CompilerParams(vmem_limit_bytes=VMEM_BYTES),
    )(*args)


class Regions:
    def __init__(self, depth, count, span, gain, in_shape, small, out_shape, small_parts):
        self.depth, self.count, self.span = depth, count, span
        self.per = in_shape[1] // ROW
        self.in_rows = in_shape[0]
        self.in_base = gain
        self.small_base = gain + in_shape[0] * self.per
        self.out_base = self.small_base + small
        self.out_rows = out_shape[0] * out_shape[1] // ROW
        self.need = (span - 1) // ROW + 2
        self.lines = min((self.need + self.per - 2) // self.per + 1, self.in_rows)
        self.half = self.lines * self.per // 2
        self.pieces = -(-self.need // self.half)
        self.slot = self.pieces * self.half
        self.line_rows = min(-(-(self.lines + 15) // 16) * 16, self.in_rows)
        self.slot_rows = min(-(-(self.slot + 15) // 16) * 16, self.out_rows)
        self.small_parts = small_parts
        self.small_tiles = sum(length for _, _, length in small_parts)

    def base(self, owner):
        return owner * self.span // ROW

    def in_first(self, owner):
        line = lax.max(self.base(owner) - self.in_base, 0) // self.per
        return lax.min(line, self.in_rows - self.lines)

    def out_first(self, owner):
        return lax.max(lax.min(self.base(owner) - self.out_base, self.out_rows - self.slot), 0)

    def meets_in(self, z):
        return z * self.count * self.span // ROW < self.small_base

    def meets_out(self, z):
        return ((z + 1) * self.count * self.span - 1) // ROW >= self.out_base

    def early_start(self, z, owner):
        if not self.meets_out(z):
            return self.in_first(owner) * (self.per // 2)
        out = self.in_rows * self.per // 2 + self.out_first(owner)
        if not self.meets_in(z):
            return out
        inside = self.base(owner) < self.small_base
        return jnp.where(inside, self.in_first(owner) * (self.per // 2), out)

    def early_phases(self):
        phases = []
        cut = 2 if self.half % 4 == 0 else 1
        size = self.half // cut
        for z in range(self.depth):
            for piece in range((self.pieces if self.meets_out(z) else 1) * cut):
                phases.append((z, piece * size, size))
        return sorted(phases, key=lambda phase: -max(self.depth - 1 - phase[0], phase[0]))

    def late_phases(self):
        cut = 2 if self.half % 4 == 0 else 1
        size = self.half // cut
        owners = [k for k in range(self.depth * self.count) if self.meets_small(k)]
        goals = {k // self.count for k in owners}
        assert len(goals) == 1
        goal = goals.pop()
        small = [(goal, None, size)] * -(-self.small_tiles // (self.count * size))
        stream = [(z, piece * size, size) for z in range(self.depth) if self.meets_in(z) for piece in range(cut)]
        return small, stream, [k % self.count for k in owners]

    def meets_small(self, owner):
        base = self.base(owner)
        return base < self.out_base and base + self.need > self.small_base

    def late_start(self, phases, p, owner):
        goal, offset, size = phases[p]
        if offset is None:
            return self.in_rows * self.per // 2 + (p * self.count + owner % self.count) * size
        return self.in_first(owner) * (self.per // 2) + offset


class Reducer:
    def __init__(self, depth, bits, phases, gap, start, src_ref, refs):
        self.depth, self.bits, self.phases = depth, bits, phases
        self.start, self.src = start, src_ref
        self.n = bits - 1
        self.half = phases[0][2] // 2
        self.acc, self.first = refs[:2]
        self.bit_recvs = refs[2 : 2 + self.n]
        self.down, self.up = refs[2 + self.n : 4 + self.n]
        (
            self.local_sem,
            self.core_send,
            self.core_recv,
            self.bit_send,
            self.bit_recv,
            self.z_send,
            self.z_recv,
        ) = refs[4 + self.n : 11 + self.n]
        self.blk, self.z = lax.axis_index("blk"), lax.axis_index("batch")
        self.mine = [(self.blk // 2**b) % 2 for b in range(bits)]
        self.partner = [self.blk + (1 - 2 * self.mine[b]) * 2**b for b in range(bits)]
        self.last = self.n + depth - 1
        self.slot = [0] + [1 + 2 * s for s in range(self.n)]
        self.slot += [max(2 * self.n, 1) + gap * u for u in range(depth - 1)]
        self.done = self.slot[-1] + 1
        hops = [max(depth - 1 - goal, goal) for goal, _, _ in phases]
        self.slots = max(p + self.slot[self.n + h] + 1 for p, h in enumerate(hops))

    @staticmethod
    def scratch(depth, bits, phases):
        n, count, size = bits - 1, len(phases), phases[0][2]
        tile = (SUB, LANE)
        dma = pltpu.SemaphoreType.DMA
        return (
            [pltpu.VMEM((count,) + (2,) * n + (size,) + tile, f32)] * 2
            + [pltpu.VMEM((count, 2) + (2,) * (n - 1 - s) + (size // 2,) + tile, f32) for s in range(n)]
            + [pltpu.VMEM((count, size) + tile, f32)] * 2
            + [dma((count,))] * 3
            + [dma((max(count * n, 1),))] * 2
            + [dma((count,)), dma((2 * count,))]
        )

    def greet(self):
        barrier = pltpu.get_barrier_semaphore()
        peers = ("blk", self.blk, 2**self.bits), ("batch", self.z, self.depth)
        for axis, index, count in peers:
            for by in range(1, count):
                other = lax.rem(index + by, count)
                pl.semaphore_signal(barrier, inc=1, device_id={axis: other}, device_id_type=MESH)
        pl.semaphore_wait(barrier, 2**self.bits + self.depth - 2)

    def digits(self, r):
        return tuple((r // 2**i) % 2 for i in reversed(range(self.n)))

    def window(self, p, r, core):
        goal, offset, size = self.phases[p]
        owner = goal * 2**self.bits + 2 * r + core
        return pl.ds(self.start(p, owner), size)

    def core_copies(self, p, own=False):
        copies = []
        for r in range(2**self.n):
            where = (p,) + self.digits(r)
            if own:
                copies.append(
                    pltpu.make_async_copy(
                        self.src.at[self.window(p, r, self.mine[0])], self.acc.at[where], self.local_sem.at[p]
                    )
                )
            else:
                copies.append(
                    pltpu.make_async_remote_copy(
                        src_ref=self.src.at[self.window(p, r, 1 - self.mine[0])],
                        dst_ref=self.first.at[where],
                        send_sem=self.core_send.at[p],
                        recv_sem=self.core_recv.at[p],
                        device_id={"blk": self.partner[0]},
                        device_id_type=MESH,
                    )
                )
        return copies

    def order(self, part):
        return list(range(self.n)) if part == 0 else list(reversed(range(self.n)))

    def place(self, p, part, done, pick):
        spots = [slice(None)] * self.n
        for i in self.order(part)[:done]:
            spots[i] = self.mine[i + 1]
        spots[self.order(part)[done]] = pick
        return (p,) + tuple(reversed(spots)) + (slice(part * self.half, (part + 1) * self.half),)

    def bit_copies(self, p, s):
        copies = []
        for part in range(2):
            i = self.order(part)[s]
            spot = p * self.n + s
            copies.append(
                pltpu.make_async_remote_copy(
                    src_ref=self.acc.at[self.place(p, part, s, 1 - self.mine[i + 1])],
                    dst_ref=self.bit_recvs[s].at[p, part],
                    send_sem=self.bit_send.at[spot],
                    recv_sem=self.bit_recv.at[spot],
                    device_id={"blk": self.partner[i + 1]},
                    device_id_type=MESH,
                )
            )
        return copies

    def settled(self, p):
        return (p,) + tuple(reversed([self.mine[i + 1] for i in range(self.n)]))

    def z_copy(self, p, up):
        return pltpu.make_async_remote_copy(
            src_ref=self.acc.at[self.settled(p)],
            dst_ref=(self.up if up else self.down).at[p],
            send_sem=self.z_send.at[p],
            recv_sem=self.z_recv.at[2 * p + up],
            device_id={"batch": lax.rem(self.z + (1 if up else self.depth - 1), self.depth)},
            device_id_type=MESH,
        )

    def add(self, dst, dst_at, src, src_at):
        dst[dst_at] += src[src_at]

    def all_core(self, p):
        return pltpu.make_async_remote_copy(
            src_ref=self.first.at[p],
            dst_ref=self.first.at[p],
            send_sem=self.core_send.at[p],
            recv_sem=self.core_recv.at[p],
            device_id={"blk": self.partner[0]},
            device_id_type=MESH,
        )

    def all_bit(self, p, s):
        return pltpu.make_async_remote_copy(
            src_ref=self.bit_recvs[s].at[p],
            dst_ref=self.bit_recvs[s].at[p],
            send_sem=self.bit_send.at[p * self.n + s],
            recv_sem=self.bit_recv.at[p * self.n + s],
            device_id={"blk": self.partner[0]},
            device_id_type=MESH,
        )

    def finish_core(self, p):
        pltpu.make_async_copy(self.first.at[p], self.acc.at[p], self.local_sem.at[p]).wait()
        self.all_core(p).wait_recv()
        for r in range(2**self.n):
            where = (p,) + self.digits(r)
            self.add(self.acc, where, self.first, where)

    def finish_bit(self, p, s):
        self.all_bit(p, s).wait_recv()
        for part in range(2):
            kept = self.place(p, part, s, self.mine[self.order(part)[s] + 1])
            free = [i for i in range(1, 1 + self.n) if isinstance(kept[i], slice)]
            for r in range(2 ** len(free)):
                chosen = tuple((r // 2**j) % 2 for j in reversed(range(len(free))))
                to = list(kept)
                for i, v in zip(free, chosen):
                    to[i] = v
                self.add(self.acc, tuple(to), self.bit_recvs[s], (p, part) + chosen)

    def take(self, p, up):
        self.z_copy(p, up).wait_recv()
        self.add(self.acc, self.settled(p), self.up if up else self.down, p)

    def z_moves(self, p, u):
        goal = self.phases[p][0]
        moves = []
        if self.depth - 1 - u > goal:
            moves.append((self.depth - 1 - u, False))
        if u < goal:
            moves.append((u, True))
        return moves

    def act(self, p, stage):
        n = self.n
        if stage == 0:
            for copy in self.core_copies(p) + self.core_copies(p, True):
                copy.start()
            return
        if stage == 1:
            self.finish_core(p)
        elif stage <= n + 1:
            self.finish_bit(p, stage - 2)
        if stage <= n:
            for copy in self.bit_copies(p, stage - 1):
                copy.start()
            return
        u = stage - n - 1
        for mover, up in self.z_moves(p, u):

            @pl.when(self.z == mover)
            def _():
                if u > 0:
                    self.take(p, up)
                self.z_copy(p, up).start()

    def run(self, t):
        for stage in reversed(range(self.last + 1)):
            p = t - self.slot[stage]
            if 0 <= p < len(self.phases):
                self.act(p, stage)

    def finish(self, p):
        goal = self.phases[p][0]
        if goal < self.depth - 1:
            self.take(p, False)
        if goal > 0:
            self.take(p, True)

    def collect(self, out_ref, first=0):
        for p, (goal, offset, size) in list(enumerate(self.phases))[first:]:

            @pl.when(self.z == goal)
            def _():
                self.finish(p)
                out_ref[offset : offset + size] = self.acc[self.settled(p)]

        for p in range(len(self.phases)):
            self.all_core(p).wait_send()
            for s in range(self.n):
                self.all_bit(p, s).wait_send()
            for u in range(self.depth - 1):
                for mover, up in self.z_moves(p, u):

                    @pl.when(self.z == mover)
                    def _():
                        self.z_copy(p, up).wait_send()


def put_restored(value, turn_ref, out_ref, block):
    rows, width = value.shape
    tiles = rows // SUB
    step = out_ref.shape[0] // SUB
    for a in range(width // LANE):
        turn_ref[a] = value[:, a * LANE : (a + 1) * LANE]
    for j in range(SUB):
        here = pl.ds(pl.multiple_of(j * step + block * tiles, tiles), tiles)
        for a in range(width // LANE):
            part = turn_ref[a, pl.ds(j, tiles, stride=SUB), :]
            out_ref[here, a * LANE : (a + 1) * LANE] = part.astype(bf16)


def late_kernel(
    regions,
    bits,
    small_phases,
    stream_phases,
    targets,
    blocks,
    flat_ref,
    early_ref,
    gain_ref,
    *refs,
):
    depth, span = regions.depth, regions.span
    sources, weights, refs = refs[:7], refs[7:14], refs[14:]
    window_ref, totals_ref, result_ref, grad_ref, params_ref = refs[:5]
    held, refs = refs[5:12], refs[12:]
    gate_back, stream_back, in_w, token, cot, gated, out_w = held
    late_ref, small_ref, wide_window, turn_ref, gain_sum, sums, ring = refs[:7]
    columns_ref, packed_ref, small_params = refs[7:10]
    load_sem, ring_send, ring_recv, small_send, small_recv = refs[10:15]
    phases = small_phases + stream_phases
    few = len(small_phases)
    work = Reducer(
        depth, bits, phases, 2, lambda p, owner: regions.late_start(phases, p, owner), flat_ref, refs[15:]
    )
    blk, z = work.blk, work.z
    inner = gated.shape[2]
    size = token.shape[0] // blocks
    loads = [
        pltpu.make_async_copy(src, dst, load_sem.at[i])
        for i, (src, dst) in enumerate(zip(sources, held))
        if src.shape == dst.shape
    ]

    def pieces(t):
        here = pl.ds(pl.multiple_of(t * size, size), size)
        return [
            pltpu.make_async_copy(src.at[here], dst.at[t % 2], load_sem.at[len(held) + 2 * i + t % 2])
            for i, (src, dst) in enumerate(zip(sources, held))
            if src.shape != dst.shape
        ]

    for load in loads + pieces(0):
        load.start()
    work.greet()
    gain_sum[...] = jnp.zeros_like(gain_sum)
    across = (((1,), (1,)), ((), ()))

    goal = small_phases[0][0]
    owner = z * 2**bits + blk
    base = regions.base(owner)
    margin = (wide_window.shape[0] - regions.need) // 2

    def spread_rows(src_ref, first, rows, put):
        per = src_ref.shape[1] // ROW

        def one(r, carry):
            here = pl.ds(pl.multiple_of(first + r * 2 * SUB, 2 * SUB), 2 * SUB)
            for q in range(per):
                both = src_ref[here, q * ROW : (q + 1) * ROW].astype(f32)
                for side in range(2):
                    half = both[side * SUB : (side + 1) * SUB]
                    tiles = turn_tiles([half[:, a * LANE : (a + 1) * LANE] for a in range(SUB)])
                    for b, tile in enumerate(tiles):
                        put((first + r * 2 * SUB + side * SUB + b) * per + q, tile)
            return carry

        lax.fori_loop(0, rows // (2 * SUB), one, 0)

    inside = lax.broadcasted_iota(jnp.int32, (SUB, LANE), 0) * LANE + lax.broadcasted_iota(
        jnp.int32, (SUB, LANE), 1
    )
    def own(value, row):
        spot = inside + (row * ROW - owner * span)
        return jnp.where((spot >= 0) & (spot < span), value, 0.0)

    def keep(total, value, row):
        wide_window[row - base + margin] = value
        part = own(value, row)
        return total + part * part

    half = regions.per // 2
    zero = jnp.zeros((SUB, LANE), f32)

    def place_early():
        wide_window[...] = jnp.zeros_like(wide_window)

        @pl.when(base < regions.small_base)
        def _():
            def line(d, total):
                row = regions.in_base + (regions.in_first(owner) + d) * regions.per + half
                for q in range(half):
                    total = keep(total, early_ref[d * half + q], row + q)
                return total

            sums[blk, 0] = lax.fori_loop(0, regions.lines, line, zero, unroll=4)

        @pl.when(base >= regions.small_base)
        def _():
            def line(i, total):
                return keep(total, early_ref[i], regions.out_base + regions.out_first(owner) + i)

            sums[blk, 0] = lax.fori_loop(0, regions.slot, line, zero, unroll=8)

    def lay_params():
        conv_w, conv_b, select_w, step_w, step_b, rate, skip = weights
        used = select_w.shape[1]
        part = columns_ref.shape[0]
        for c in range(select_w.shape[0] // part):
            columns_ref[:, :used] = select_w[c * part : (c + 1) * part].astype(f32)
            pack_columns(columns_ref, used, packed_ref.at[c * part * used // LANE : (c + 1) * part * used // LANE])
        spot = 0
        for ref in (conv_w, conv_b, select_w, step_w, step_b, rate, skip):
            count = ref.shape[0] * ref.shape[1] // ROW
            if ref is select_w:

                def one(i, carry, spot=spot):
                    small_params[spot + i] = packed_ref[at(i * SUB, SUB), :]
                    return carry

                lax.fori_loop(0, count, one, 0, unroll=8)
            elif ref is step_w:

                def put(i, tile, spot=spot):
                    small_params[spot + i] = tile

                spread_rows(step_w, 0, step_w.shape[0], put)
            else:
                per = ref.shape[1] // ROW
                for i in range(count):
                    small_params[spot + i] = row_tile(ref, i // per, i % per)
            spot += count

    def place_params():
        params_ref[...] = jnp.zeros_like(params_ref)
        wide_window[...] = jnp.zeros_like(wide_window)

        @pl.when(base < regions.small_base)
        def _():
            first = regions.in_first(owner) // (2 * SUB) * (2 * SUB)
            first = lax.min(first, regions.in_rows - regions.line_rows)

            def put(i, tile):
                wide_window[regions.in_base + i - base + margin] = tile

            spread_rows(in_w, first, regions.line_rows, put)

        @pl.when(base >= regions.small_base)
        def _():
            first = regions.out_first(owner) // (2 * SUB) * (2 * SUB)
            first = lax.min(first, regions.out_rows - regions.slot_rows)

            def put(i, tile):
                wide_window[regions.out_base + i - base + margin] = tile

            spread_rows(out_w, first, regions.slot_rows, put)

        @pl.when((base < regions.out_base) & (base + regions.need > regions.small_base))
        def _():
            def line(i, carry):
                row = base + i
                tile = lax.max(lax.min(row - regions.small_base, small_params.shape[0] - 1), 0)
                here = (row >= regions.small_base) & (row < regions.out_base)
                wide_window[margin + i] = jnp.where(here, small_params[tile], wide_window[margin + i])
                return carry

            lax.fori_loop(0, regions.need, line, 0, unroll=2)

        params_ref[...] = wide_window[margin : margin + regions.need]

        @pl.when(base < regions.in_base)
        def _():
            params_ref[0] = row_tile(gain_ref, 0, 0)

    def hand_out(p, target):
        return pltpu.make_async_remote_copy(
            src_ref=small_ref.at[p, blk],
            dst_ref=small_ref.at[p, blk],
            send_sem=small_send.at[p, targets.index(target)],
            recv_sem=small_recv.at[p, blk],
            device_id={"blk": target},
            device_id_type=MESH,
        )

    def give_small(p):
        @pl.when(z == goal)
        def _():
            work.finish(p)
            small_ref[p, blk] = work.acc[work.settled(p)]
            for target in targets:

                @pl.when(blk != target)
                def _():
                    hand_out(p, target).start()

    def slot(t, carry):
        for k in range(work.slots):

            @pl.when(t == k)
            def _():
                if 0 <= k - work.done < few:
                    give_small(k - work.done)
                work.run(k)
                if k == 0:
                    for load in loads:
                        load.wait()

        @pl.when(t < blocks)
        def _():
            here = pl.ds(pl.multiple_of(t * size, size), size)
            part = t % 2
            for piece in pieces(t):
                piece.wait()

            @pl.when(t + 1 < blocks)
            def _():
                for piece in pieces(t + 1):
                    piece.start()

            source = token[here, :].astype(f32)
            output = jnp.dot(gated[part], out_w[...], preferred_element_type=f32)
            put_restored(source + output, turn_ref, result_ref, t)
            grad_normed = lax.dot_general(
                stream_back[part], in_w[:, :inner], across, preferred_element_type=f32
            ) + lax.dot_general(gate_back[part], in_w[:, inner:], across, preferred_element_type=f32)
            scale = lax.rsqrt(jnp.mean(source * source, axis=-1, keepdims=True) + EPS)
            scaled = source * scale
            product = grad_normed * scaled
            gain_sum[...] += jnp.sum(product.reshape(size // SUB, SUB, product.shape[1]), 0)
            weighted = grad_normed * gain_ref[...]
            mean = jnp.mean(weighted * source, axis=-1, keepdims=True)
            back = scale * weighted - source * (scale * scale * scale) * mean + cot[here, :].astype(f32)
            put_restored(back, turn_ref, grad_ref, t)

        @pl.when(t == blocks)
        def _():
            lay_params()

        @pl.when(t == blocks + 1)
        def _():
            place_params()

        @pl.when(t == blocks + 2)
        def _():
            place_early()

        return carry

    lax.fori_loop(0, max(work.slots, blocks + 3), slot, 0)
    for p in range(few):
        if p + work.done >= work.slots:
            give_small(p)
    late_ref[...] = jnp.zeros_like(late_ref)
    work.collect(late_ref, few)
    for target in targets:
        for p in range(few):

            @pl.when((z == goal) & (blk != target))
            def _():
                hand_out(p, target).wait_send()

            for source in range(2**bits):
                if source != target:

                    @pl.when((z == goal) & (blk == target))
                    def _():
                        pltpu.make_async_remote_copy(
                            src_ref=small_ref.at[p, source],
                            dst_ref=small_ref.at[p, source],
                            send_sem=small_send.at[p, 0],
                            recv_sem=small_recv.at[p, source],
                            device_id={"blk": source},
                            device_id_type=MESH,
                        ).wait_recv()

    gain = jnp.sum(gain_sum[...], 0, keepdims=True)
    for a in range(SUB):
        sums[blk, 1, a : a + 1, :] = gain[:, a * LANE : (a + 1) * LANE]

    @pl.when(base < regions.small_base)
    def _():
        def line(d, total):
            row = regions.in_base + (regions.in_first(owner) + d) * regions.per
            for q in range(half):
                total = keep(total, late_ref[d * half + q], row + q)
            return total

        sums[blk, 0] += lax.fori_loop(0, regions.lines, line, zero, unroll=4)

    size = small_phases[0][2]

    @pl.when((base < regions.out_base) & (base + regions.need > regions.small_base))
    def _():
        def line(i, total):
            row = base + i
            tile = 0
            for first, spot, length in regions.small_parts:
                offset = row - regions.small_base - first
                tile = jnp.where(offset >= 0, spot + lax.min(offset, length - 1), tile)
            lot = tile // size
            value = small_ref[lot // 2**bits, lot % 2**bits, tile % size]
            here = (row >= regions.small_base) & (row < regions.out_base)
            wide_window[margin + i] = jnp.where(here, value, wide_window[margin + i])
            part = jnp.where(here, own(value, row), 0.0)
            return total + part * part

        sums[blk, 0] += lax.fori_loop(0, regions.need, line, zero, unroll=5)

    window_ref[...] = wide_window[margin : margin + regions.need]

    def everyone(slots, axis, index, count, first_sem):
        copies = [
            pltpu.make_async_remote_copy(
                src_ref=slots.at[index],
                dst_ref=slots.at[index],
                send_sem=ring_send.at[first_sem + by],
                recv_sem=ring_recv.at[first_sem + by],
                device_id={axis: lax.rem(index + by, count)},
                device_id_type=MESH,
            )
            for by in range(1, count)
        ]
        for copy in copies:
            copy.start()
        for copy in copies:
            copy.wait()
        total = slots[0]
        for k in range(1, count):
            total = total + slots[k]
        return total

    ring[z] = everyone(sums, "blk", blk, 2**bits, 0)
    total = everyone(ring, "batch", z, depth, 2**bits)
    totals_ref[...] = total

    @pl.when(base < regions.in_base)
    def _():
        window_ref[0] = total[1]


def late_call(flat, early, gain, sources, weights, regions):
    bits = regions.count.bit_length() - 1
    depth = regions.depth
    small_phases, stream_phases, targets = regions.late_phases()
    phases = small_phases + stream_phases
    few, size = len(small_phases), phases[0][2]
    margin = max(regions.slot_rows, regions.line_rows * regions.per) + SUB
    wide, used = weights[2].shape
    small_count = sum(x.size for x in weights) // ROW
    tile = (SUB, LANE)
    dma = pltpu.SemaphoreType.DMA
    hops = 2**bits + depth
    vmem = pl.BlockSpec(memory_space=pltpu.VMEM)
    far = pl.BlockSpec(memory_space=pl.ANY)
    rows, model = sources[3].shape
    blocks = 8
    return pl.pallas_call(
        functools.partial(late_kernel, regions, bits, small_phases, stream_phases, targets, blocks),
        name="reduce_late",
        in_specs=[far, vmem, vmem] + [far] * len(sources) + [vmem] * len(weights),
        out_specs=[vmem] * 5,
        out_shape=[
            jax.ShapeDtypeStruct((regions.need,) + tile, f32),
            jax.ShapeDtypeStruct((2,) + tile, f32),
            jax.ShapeDtypeStruct((rows, model), bf16),
            jax.ShapeDtypeStruct((rows, model), bf16),
            jax.ShapeDtypeStruct((regions.need,) + tile, f32),
        ],
        scratch_shapes=[
            pltpu.VMEM((2, rows // blocks, x.shape[1]) if n in (0, 1, 5) else x.shape, x.dtype)
            for n, x in enumerate(sources)
        ]
        + [
            pltpu.VMEM((regions.half,) + tile, f32),
            pltpu.VMEM((few, 2**bits, size) + tile, f32),
            pltpu.VMEM((regions.need + 2 * margin,) + tile, f32),
            pltpu.VMEM((model // LANE, rows // blocks, LANE), f32),
            pltpu.VMEM((SUB, model), f32),
            pltpu.VMEM((2**bits, 2) + tile, f32),
            pltpu.VMEM((depth, 2) + tile, f32),
            pltpu.VMEM((wide // blocks, LANE), f32),
            pltpu.VMEM((wide * used // LANE, LANE), f32),
            pltpu.VMEM((small_count,) + tile, f32),
            dma((3 * len(sources),)),
            dma((hops,)),
            dma((hops,)),
            dma((few, len(targets))),
            dma((few, 2**bits)),
        ]
        + Reducer.scratch(depth, bits, phases),
        compiler_params=pltpu.CompilerParams(
            vmem_limit_bytes=62 * 2**20, collective_id=1, has_side_effects=True
        ),
    )(flat, early, gain, *sources, *weights)


def exchange_kernel(bits, state, totals_ref, entry_ref, arriving_ref, here, far, pre, post, send_sem, recv_sem):
    blk = lax.axis_index("blk")
    mine = [(blk // 2**b) % 2 for b in range(bits)]
    partner = [blk + (1 - 2 * mine[b]) * 2**b for b in range(bits)]
    barrier = pltpu.get_barrier_semaphore()
    for other in partner:
        pl.semaphore_signal(barrier, inc=1, device_id={"blk": other}, device_id_type=MESH)
    pl.semaphore_wait(barrier, bits)
    first, second, third = (slice(k * state, (k + 1) * state) for k in range(3))
    here[0] = totals_ref[...]
    entry_ref[...] = jnp.zeros_like(entry_ref)
    arriving_ref[...] = jnp.zeros_like(arriving_ref)
    pre[...] = jnp.ones_like(pre)
    post[...] = jnp.ones_like(post)
    for b in range(bits):
        if b < bits - 1:
            src, dst = here.at[b], far.at[b]
        else:
            src = here.at[b, pl.ds(pl.multiple_of((1 + mine[b]) * state, state), state)]
            dst = far.at[b, first]
        copy = pltpu.make_async_remote_copy(
            src_ref=src,
            dst_ref=dst,
            send_sem=send_sem.at[b],
            recv_sem=recv_sem.at[b],
            device_id={"blk": partner[b]},
            device_id_type=MESH,
        )
        copy.start()
        copy.wait()
        if b == bits - 1:

            @pl.when(mine[b] == 1)
            def _():
                entry_ref[...] += pre[...] * far[b, first]

            @pl.when(mine[b] == 0)
            def _():
                arriving_ref[...] += post[...] * far[b, first]

            continue

        @pl.when(mine[b] == 1)
        def _():
            entry_ref[...] += pre[...] * far[b, second]
            pre[...] *= far[b, first]
            here[b + 1, second] = here[b, second] + here[b, first] * far[b, second]
            here[b + 1, third] = far[b, third] + far[b, first] * here[b, third]

        @pl.when(mine[b] == 0)
        def _():
            arriving_ref[...] += post[...] * far[b, third]
            post[...] *= far[b, first]
            here[b + 1, second] = far[b, second] + far[b, first] * here[b, second]
            here[b + 1, third] = here[b, third] + here[b, first] * far[b, third]

        here[b + 1, first] = here[b, first] * far[b, first]


def exchange(totals, state):
    bits = lax.axis_size("blk").bit_length() - 1
    rows, inner = totals.shape
    vmem = pl.BlockSpec(memory_space=pltpu.VMEM)
    return pl.pallas_call(
        functools.partial(exchange_kernel, bits, state),
        name="exchange",
        in_specs=[vmem],
        out_specs=[vmem] * 2,
        out_shape=[jax.ShapeDtypeStruct((state, inner), f32)] * 2,
        scratch_shapes=[pltpu.VMEM((bits, rows, inner), f32)] * 2
        + [pltpu.VMEM((state, inner), f32)] * 2
        + [pltpu.SemaphoreType.DMA((bits,))] * 2,
        compiler_params=pltpu.CompilerParams(
            vmem_limit_bytes=VMEM_BYTES, collective_id=3, has_side_effects=True
        ),
    )(totals)


def local(
    tokens,
    out_cot,
    norm_gain,
    in_weight,
    conv_weight,
    conv_bias,
    xproj_weight,
    dt_weight,
    dt_bias,
    a_log,
    d_skip,
    out_weight,
    moment_one,
    moment_two,
):
    contract = (((0,), (0,)), ((), ()))
    backward = (((1,), (1,)), ((), ()))
    token_rows = interleave(tokens[0])
    cot_low = interleave(out_cot[0])
    source = token_rows.astype(f32)
    length = source.shape[0]
    inner = dt_bias.shape[0]
    state = a_log.shape[0]
    rank = dt_weight.shape[0]
    width = conv_weight.shape[0]
    halo = (width - 1) * SUB
    scale = lax.rsqrt(jnp.mean(source * source, axis=-1, keepdims=True) + EPS)
    normed = (source * scale * norm_gain).astype(bf16)
    stream = jnp.dot(normed, in_weight[:, :inner], preferred_element_type=f32)
    ends = stream[length - halo :].reshape(width - 1, SUB, inner)
    tail = shifted(ends[:, SUB - 1], "blk", 1)
    gating = jnp.dot(normed, in_weight[:, inner:], preferred_element_type=f32)
    grad_gated = lax.dot_general(cot_low, out_weight, backward, preferred_element_type=f32)
    head = jnp.concatenate([tail[:, None], ends[:, : SUB - 1]], 1).reshape(halo, inner)
    rates = -jnp.exp(a_log)
    rates_wide = jnp.repeat(rates * LOG2E, SUB, axis=0)
    spots = spread_table(2 * state)
    (
        conv_sum,
        conv_low,
        step_size,
        drive,
        grad_scanned,
        sel_low,
        terms,
        pre_decay,
        pre_state,
        post_decay,
        post_state,
        totals,
    ) = summary_call(
        stream,
        gating,
        grad_gated,
        head,
        conv_weight,
        conv_bias[None],
        xproj_weight,
        dt_weight,
        dt_bias[None],
        spots,
        rates_wide,
    )
    entry, arriving = exchange(totals, state)
    prior, readout_grads, gated, grad_gating, skip_grads = forward_call(
        step_size,
        drive,
        grad_scanned,
        terms,
        spots,
        rates_wide,
        pre_decay,
        pre_state,
        entry,
        conv_low,
        gating,
        grad_gated,
        d_skip[None],
    )
    grad_d_skip = jnp.sum(skip_grads, 0)

    span = moment_one.shape[0]
    small_rows = sum(
        value.size for value in (conv_weight, conv_bias, xproj_weight, dt_weight, dt_bias, a_log, d_skip)
    ) // ROW
    lead = (conv_weight.size + conv_bias.size) // ROW
    packed = xproj_weight.size // ROW
    rest = small_rows - lead - packed
    small_parts = ((0, packed, lead), (lead, 0, packed), (lead + packed, packed + lead, rest))
    regions = Regions(
        lax.axis_size("batch"),
        lax.axis_size("blk"),
        span,
        norm_gain.size // ROW,
        in_weight.shape,
        small_rows,
        out_weight.shape,
        small_parts,
    )
    flat_early = product_call((normed, grad_gating), (gated, cot_low))
    grad_stream_low, grad_pre_low, grad_selectors, rate_grads, taps_grads, edges, early = backward_call(
        step_size,
        drive,
        grad_scanned,
        terms,
        spots,
        rates_wide,
        post_state + post_decay * jnp.repeat(arriving, SUB, axis=0),
        prior,
        conv_sum,
        stream,
        readout_grads,
        dt_weight,
        xproj_weight,
        conv_weight,
        d_skip[None],
        flat_early,
        regions,
        rank,
    )
    grad_a_log = LN2 * jnp.sum(rate_grads.reshape(state, SUB, inner), 1)
    begins = edges[:halo].reshape(width - 1, SUB, inner)
    ahead = shifted(begins[:, 0], "blk", -1)
    grad_dt_weight = lax.dot_general(sel_low, grad_pre_low, contract, preferred_element_type=f32)[:rank]
    grad_xproj = lax.dot_general(conv_low, grad_selectors, contract, preferred_element_type=f32)
    foot = jnp.concatenate([begins[:, 1:], ahead[:, None]], 1)
    lasts = edges[halo:].reshape(width - 1, SUB, inner)
    further = jnp.concatenate([lasts, foot], 0)
    last_stream = stream[length - halo :].reshape(width - 1, SUB, inner)
    grad_last = conv_weight[width - 1] * lasts
    taps_grads = jnp.sum(taps_grads.reshape(width + 2, SUB, inner), 1)
    tap_grads = []
    for offset in range(width - 1):
        lead = width - 1 - offset
        grad_last = grad_last + conv_weight[offset] * further[lead : lead + width - 1]
        over = jnp.sum(last_stream[width - 1 - lead :] * foot[:lead], (0, 1))
        tap_grads.append(taps_grads[offset] + over)
    tap_grads.append(taps_grads[width - 1])
    grad_conv_weight = jnp.stack(tap_grads, 0)
    grad_conv_bias = taps_grads[width]
    grad_dt_bias = taps_grads[width + 1]
    grad_stream_low = lax.dynamic_update_slice_in_dim(
        grad_stream_low, grad_last.reshape(halo, inner).astype(bf16), length - halo, 0
    )
    thin = (grad_conv_weight, grad_conv_bias[None], grad_dt_weight, grad_dt_bias[None], grad_a_log, grad_d_skip[None])
    window, totals, result, grad_tokens, owned = late_call(
        product_call((normed, grad_stream_low), small=(grad_xproj, thin, rank + 2 * state)),
        early,
        norm_gain[None],
        (grad_gating, grad_stream_low, in_weight, token_rows, cot_low, gated, out_weight),
        (conv_weight, conv_bias[None], xproj_weight, dt_weight, dt_bias[None], a_log, d_skip[None]),
        regions,
    )
    result, grad_tokens = result[None], grad_tokens[None]
    grad_norm = jnp.sqrt(jnp.sum(totals[0]) + jnp.sum(totals[1] * totals[1]))
    owner = lax.axis_index(("batch", "blk"))
    begin = owner * span
    shard = lax.dynamic_slice_in_dim(window.reshape(-1), begin % ROW, span)
    owned = lax.dynamic_slice_in_dim(owned.reshape(-1), begin % ROW, span)
    lower = norm_gain.size + in_weight.size + sum(
        value.size for value in (conv_weight, conv_bias, xproj_weight, dt_weight)
    )
    upper = lower + dt_bias.size + a_log.size + d_skip.size
    place = begin + lax.iota(jnp.int32, span)
    keep = jnp.where((place >= lower) & (place < upper), 0.0, 1.0).astype(f32)
    clipped = shard * jnp.minimum(1.0, CLIP / (grad_norm + 1e-06))
    new_one = BETA_ONE * moment_one + (1.0 - BETA_ONE) * clipped
    new_two = BETA_TWO * moment_two + (1.0 - BETA_TWO) * clipped * clipped
    first = new_one / (1.0 - BETA_ONE**ADAM_STEP)
    second = new_two / (1.0 - BETA_TWO**ADAM_STEP)
    param_step = -RATE * (first / (jnp.sqrt(second) + ADAM_EPS) + DECAY * keep * owned)
    return (result, grad_tokens, shard, grad_norm, param_step, new_one, new_two)


def solution(mesh):
    return jax.shard_map(
        local,
        mesh=mesh,
        in_specs=(P("batch", "blk", None),) * 2 + (P(),) * 10 + (P(("batch", "blk")),) * 2,
        out_specs=(P("batch", "blk", None),) * 2
        + (P(("batch", "blk")), P(), P(("batch", "blk")), P(("batch", "blk")), P(("batch", "blk"))),
        check_vma=False,
    )
```
